128 devices in a mesh: group: 8 (over z, core), ingroup: 16 (over x, y).
Axes of the slice: x: 4, y: 4, z: 4, core: 2. Of those that a mesh axis runs over, the one named last changes fastest.
Arguments:
- hidden_in: bfloat16 [1024, 7168], P(('group', 'ingroup')), may hold values from -6 to 6
- queries: bfloat16 [1024, 64, 576], P(('group', 'ingroup')), may hold values from -20 to 20
- node_latent: bfloat16 [1024, 576], P(('group', 'ingroup')), may hold values from -8 to 8
- cache: bfloat16 [128, 1024, 576], P(('group', 'ingroup')), may hold values from -4 to 4
- cache_len: int32 [128], P(('group', 'ingroup')), may hold values from 512 to 1024
- parents: int32 [128, 8], P(('group', 'ingroup')), may hold values from 0 to 6, as said below
- value_up: bfloat16 [64, 512, 128], P('ingroup'), may hold values from -0.25 to 0.25
- out_proj: bfloat16 [8192, 7168], P('ingroup'), may hold values from -0.0625 to 0.0625
- ffn_gain: float32 [7168], replicated, may hold values from 0.1 to 1.9
- route_experts: int32 [1024, 8], P(('group', 'ingroup')), may hold values from 0 to 31, as said below
- route_weights: float32 [1024, 8], P(('group', 'ingroup')), may hold values from 0.1 to 0.6
- expert_gate: bfloat16 [128, 7168, 256], P(('group', 'ingroup')), may hold values from -0.0625 to 0.0625
- expert_up: bfloat16 [128, 7168, 256], P(('group', 'ingroup')), may hold values from -0.0625 to 0.0625
- expert_down: bfloat16 [128, 256, 7168], P(('group', 'ingroup')), may hold values from -0.1875 to 0.1875
- shared_gate: bfloat16 [7168, 1024], P(None, 'ingroup'), may hold values from -0.0625 to 0.0625
- shared_up: bfloat16 [7168, 1024], P(None, 'ingroup'), may hold values from -0.0625 to 0.0625
- shared_down: bfloat16 [1024, 7168], P('ingroup'), may hold values from -0.1875 to 0.1875
Outputs:
- mixed: bfloat16 [1024, 7168], P(('group', 'ingroup'))
The draws below stay inside these ranges and needn't reach their ends.
Inputs may be any that keep to these rules, and one draw needn't show every extreme that they name: `parents`: the parent of node n is a node below n; the root, node 0, has parent 0. `route_experts`: each row names 8 different experts, two in each of 4 node groups, expert e belonging to node group e // 4; over the rows of one device no expert is named more than 4 times.
All inputs are finite; a program needn't handle non-finite values.
Results may differ from the reference program's by a relative error of at most 0.023.
Values may be sent and summed in bfloat16 or wider, within the bound.
A program may use at most 128 MiB of HBM per device.

```python
import math
import jax
import jax.numpy as jnp
from jax import lax

D = 7168
HEADS = 64
LAT = 512
VH = 128
FF = 1024
SPLIT = 4
FF_DEV = 256
SFF = 1024
TOP = 8
TOPG = 4
NODES = 8
CACHE = 1024
DQ = 576
ROWS_DEV = 8
ROWS = 1024
REQS = 128
EPG = 4
EXPERTS = 32
CAP = 4
N_GROUP = 8
DEVICES = 128


def draw_cache(key, part):
    key = jax.random.fold_in(key, 3)
    entries = jnp.clip(jax.random.normal(key, (REQS, CACHE, DQ), jnp.float32), -4.0, 4.0)
    return entries.astype(jnp.bfloat16)


def draw_queries(key, part):
    key = jax.random.fold_in(key, 5)
    base_key = jax.random.fold_in(key, 0)
    entries = jnp.clip(jax.random.normal(base_key, (ROWS, HEADS, DQ), jnp.float32), -4.0, 4.0)
    return entries.astype(jnp.bfloat16)


def draw_cache_len(key, part):
    key = jax.random.fold_in(key, 7)
    lengths = jax.random.randint(key, (REQS,), CACHE // 2, CACHE + 1)
    return lengths.at[0].set(CACHE).astype(jnp.int32)


def draw_parents(key, part):
    key = jax.random.fold_in(key, 11)
    upper = jnp.maximum(jnp.arange(NODES, dtype=jnp.int32), 1)
    drawn = jax.random.randint(key, (REQS, NODES), 0, jnp.broadcast_to(upper, (REQS, NODES)))
    return drawn.at[0, NODES - 1].set(NODES - 2).astype(jnp.int32)


def draw_route_experts(key, part):
    key = jax.random.fold_in(key, 13)
    subkeys = jax.random.split(key, 5)
    group_order = jax.random.permutation(subkeys[0], N_GROUP)
    lower_pick = jnp.minimum(jax.random.randint(subkeys[1], (DEVICES,), 0, N_GROUP), jax.random.randint(subkeys[2], (DEVICES,), 0, N_GROUP))
    hot_group = group_order[lower_pick]
    group_ids = jnp.arange(N_GROUP, dtype=jnp.int32)
    group_score = jax.random.randint(subkeys[3], (DEVICES, ROWS_DEV, N_GROUP), 0, 2 ** 20) * 64 + group_ids
    group_score = jnp.where(group_ids[None, None, :] == hot_group[:, None, None], 2 ** 27, group_score)
    chosen_groups = jnp.argsort(-group_score, axis=-1)[:, :, :TOPG]
    expert_score = jax.random.randint(subkeys[4], (DEVICES, N_GROUP, EPG), 0, 2 ** 20) * 64 + jnp.arange(EPG, dtype=jnp.int32)
    expert_order = jnp.argsort(expert_score, axis=-1)
    device_ids = jnp.arange(DEVICES, dtype=jnp.int32)[:, None, None, None]
    position = jnp.arange(2, dtype=jnp.int32)[None, None, None, :] * (EPG // 2) + (jnp.arange(ROWS_DEV, dtype=jnp.int32) // CAP)[None, :, None, None]
    within = expert_order[device_ids, chosen_groups[:, :, :, None], position]
    experts = chosen_groups[:, :, :, None] * EPG + within
    return experts.reshape(ROWS, TOP).astype(jnp.int32)


def shard_levels(stream_key, dims, cuts, smallest, high):
    def one(dim, blocks):
        steps = jax.random.uniform(jax.random.fold_in(jax.random.fold_in(stream_key, 6), dim), (blocks,), jnp.float32, smallest / len(cuts), high / len(cuts))
        return jnp.repeat(jnp.exp(steps), dims[dim] // blocks).reshape((-1,) + (1,) * (len(dims) - dim - 1))

    level = one(*cuts[0])
    for cut in cuts[1:]:
        level = level * one(*cut)
    return level


def scatter_about(own_key, extent, width, limit, shards=(), held_as=jnp.bfloat16):
    values = width * jax.random.normal(own_key, extent, jnp.float32)
    if shards:
        values = values * shard_levels(own_key, extent, shards, -0.22, 0.18)
    return jnp.clip(values, -limit, limit).astype(held_as)


def setup_inputs(seed: int = 0) -> dict:
    key_list = jax.random.split(jax.random.key(seed), 18)
    return {
        "hidden_in": scatter_about(key_list[0], (ROWS, D), 1.0, 6.0, ((0, 128),)),
        "queries": draw_queries(jax.random.fold_in(key_list[17], 71), 0),
        "node_latent": scatter_about(key_list[2], (ROWS, DQ), 2.0, 8.0, ((0, 128),)),
        "cache": draw_cache(jax.random.fold_in(key_list[17], 71), 0),
        "cache_len": draw_cache_len(jax.random.fold_in(key_list[17], 71), 0),
        "parents": draw_parents(jax.random.fold_in(key_list[17], 71), 0),
        "value_up": scatter_about(key_list[6], (HEADS, LAT, VH), LAT ** -0.5, 0.25, ((0, 16),)),
        "out_proj": scatter_about(key_list[7], (HEADS * VH, D), (HEADS * VH) ** -0.5, 0.0625, ((0, 16),)),
        "ffn_gain": jnp.clip(1.0 + 0.18 * jax.random.normal(key_list[8], (D,), jnp.float32), 0.1, 1.9),
        "route_experts": draw_route_experts(jax.random.fold_in(key_list[17], 71), 0),
        "route_weights": jnp.clip(jnp.exp(math.log(0.6) - 1.7917595 * jax.random.uniform(key_list[10], (ROWS, TOP), jnp.float32) ** shard_levels(key_list[10], (ROWS, TOP), ((0, 128),), -0.2, 0.2)), 0.1, 0.6),
        "expert_gate": scatter_about(key_list[11], (EXPERTS * SPLIT, D, FF_DEV), D ** -0.5, 0.0625, ((0, 128),)),
        "expert_up": scatter_about(key_list[12], (EXPERTS * SPLIT, D, FF_DEV), D ** -0.5, 0.0625, ((0, 128),)),
        "expert_down": scatter_about(key_list[13], (EXPERTS * SPLIT, FF_DEV, D), FF ** -0.5, 0.1875, ((0, 128),)),
        "shared_gate": scatter_about(key_list[14], (D, SFF), D ** -0.5, 0.0625, ((1, 16),)),
        "shared_up": scatter_about(key_list[15], (D, SFF), D ** -0.5, 0.0625, ((1, 16),)),
        "shared_down": scatter_about(key_list[16], (SFF, D), SFF ** -0.5, 0.1875, ((0, 16),)),
    }


SCALE_QK = 192.0 ** (-0.5)
NORM_EPS = 1e-06

def widened_copy(tensor):
    return lax.optimization_barrier(tensor).astype(jnp.float32)

def ancestors(parents):
    node_count = parents.shape[-1]
    node_ids = jnp.arange(node_count, dtype=jnp.int32)
    pointer = jnp.broadcast_to(node_ids, parents.shape)
    visible = pointer[..., :, None] == node_ids
    for hop_index in range(node_count - 1):
        pointer = jnp.take_along_axis(parents, pointer, axis=-1)
        visible = visible | (pointer[..., :, None] == node_ids)
    return visible.astype(jnp.int32)

def attend(queries, node_keys, cache, cache_len, visible):
    query_wide = queries.astype(jnp.float32)
    cache_wide = cache.astype(jnp.float32)
    node_wide = node_keys.astype(jnp.float32)
    cache_scores = jnp.einsum('bnhc,blc->bnhl', query_wide, cache_wide) * SCALE_QK
    node_scores = jnp.einsum('bnhc,bmc->bnhm', query_wide, node_wide) * SCALE_QK
    positions = jnp.arange(cache.shape[1], dtype=jnp.int32)
    cache_live = positions[None, :] < cache_len[:, None]
    cache_scores = jnp.where(cache_live[:, None, None, :], cache_scores, -jnp.inf)
    node_scores = jnp.where((visible != 0)[:, :, None, :], node_scores, -jnp.inf)
    highest = jnp.maximum(lax.optimization_barrier(jnp.max(cache_scores, axis=-1)), lax.optimization_barrier(jnp.max(node_scores, axis=-1)))[..., None]
    cache_exp = jnp.exp(cache_scores - highest)
    node_exp = jnp.exp(node_scores - highest)
    exp_total = lax.optimization_barrier(jnp.sum(cache_exp, axis=-1, keepdims=True)) + lax.optimization_barrier(jnp.sum(node_exp, axis=-1, keepdims=True))
    cache_weights = widened_copy((cache_exp / exp_total).astype(jnp.bfloat16))
    node_weights = widened_copy((node_exp / exp_total).astype(jnp.bfloat16))
    latent = jnp.einsum('bnhl,blc->bnhc', cache_weights, cache_wide[:, :, :LAT])
    latent = latent + jnp.einsum('bnhm,bmc->bnhc', node_weights, node_wide[:, :, :LAT])
    return latent.astype(jnp.bfloat16)

def rms_normed(row_block, norm_gain):
    widened = row_block.astype(jnp.float32)
    mean_square = lax.optimization_barrier(jnp.mean(widened * widened, axis=-1, keepdims=True))
    return (widened * lax.rsqrt(mean_square + NORM_EPS) * norm_gain).astype(jnp.bfloat16)

def reference(hidden_in, queries, node_latent, cache, cache_len, parents, value_up, out_proj, ffn_gain, route_experts, route_weights, expert_gate, expert_up, expert_down, shared_gate, shared_up, shared_down):
    visible = ancestors(parents)

    def per_request(operands):
        req_queries, req_nodes, req_cache, req_length, req_visible = operands
        return attend(req_queries[None], req_nodes[None], req_cache[None], req_length[None], req_visible[None])[0]
    latent = lax.map(per_request, (queries.reshape(REQS, NODES, HEADS, DQ), node_latent.reshape(REQS, NODES, DQ), cache, cache_len, visible))
    latent = latent.reshape(ROWS, HEADS, LAT)
    head_out = jnp.einsum('rhc,hcv->rhv', widened_copy(latent), value_up.astype(jnp.float32)).astype(jnp.bfloat16)
    attention_out = jnp.dot(head_out.reshape(ROWS, HEADS * VH), out_proj, preferred_element_type=jnp.float32)
    attended = (hidden_in.astype(jnp.float32) + attention_out).astype(jnp.bfloat16)
    normed = rms_normed(attended, ffn_gain)
    shared_gate_part = jnp.dot(normed, shared_gate, preferred_element_type=jnp.float32)
    shared_up_part = jnp.dot(normed, shared_up, preferred_element_type=jnp.float32)
    shared_hidden = (jax.nn.silu(shared_gate_part) * shared_up_part).astype(jnp.bfloat16)
    shared_out = jnp.dot(shared_hidden, shared_down, preferred_element_type=jnp.float32)
    max_load = DEVICES * CAP
    gate_blocks = expert_gate.reshape(EXPERTS, SPLIT, D, FF_DEV)
    up_blocks = expert_up.reshape(EXPERTS, SPLIT, D, FF_DEV)
    down_blocks = expert_down.reshape(EXPERTS, SPLIT, FF_DEV, D)

    def expert_step(routed_sum, expert_id):
        is_named = route_experts == expert_id
        row_hit = jnp.any(is_named, axis=1)
        row_weight = lax.optimization_barrier(jnp.sum(jnp.where(is_named, route_weights, 0.0), axis=1))
        hit_count = jnp.sum(row_hit.astype(jnp.int32))
        picked = jnp.nonzero(row_hit, size=max_load, fill_value=0)[0].astype(jnp.int32)
        inputs = normed[picked]
        gate_set = gate_blocks[expert_id]
        up_set = up_blocks[expert_id]
        down_set = down_blocks[expert_id]
        output = jnp.zeros((max_load, D), jnp.float32)
        for block_index in range(SPLIT):
            gate_proj = jnp.dot(inputs, gate_set[block_index], preferred_element_type=jnp.float32)
            up_proj = jnp.dot(inputs, up_set[block_index], preferred_element_type=jnp.float32)
            hidden = (jax.nn.silu(gate_proj) * up_proj).astype(jnp.bfloat16)
            block_out = jnp.dot(hidden, down_set[block_index], preferred_element_type=jnp.float32).astype(jnp.bfloat16)
            output = output + widened_copy(block_out)
        is_valid = jnp.arange(max_load, dtype=jnp.int32) < hit_count
        scaled = jnp.where(is_valid[:, None], row_weight[picked][:, None] * output, 0.0)
        return (routed_sum.at[picked].add(scaled), hit_count)
    routed, unused_counts = lax.scan(expert_step, jnp.zeros((ROWS, D), jnp.float32), jnp.arange(EXPERTS, dtype=jnp.int32))
    return (attended.astype(jnp.float32) + shared_out + routed).astype(jnp.bfloat16)
```

```python
import functools

import jax
import jax.numpy as jnp
from jax import lax
from jax.experimental import pallas as pl
from jax.experimental.pallas import tpu as pltpu
from jax.sharding import PartitionSpec as P

MESH = pl.DeviceIdType.MESH
F32 = jnp.float32
BF16 = jnp.bfloat16
SCALE_QK = 192.0 ** (-0.5)
NORM_EPS = 1e-06
RING = 4
CORES = 2
LANES = 128
AXES = ("z", "x", "y")
GATHER_ORDERS = (("x", "y", "z"), ("y", "z", "x"), ("z", "x", "y"))
SCATTER_ORDERS = (("z", "x", "y"), ("x", "y", "z"), ("y", "z", "x"))
PLANE_ORDERS = (("x", "y"), ("y", "x"))


def column_parts(width, count):
    tiles = width // LANES
    sizes = [tiles // count + (1 if k < tiles % count else 0) for k in range(count)]
    parts, start = [], 0
    for size in sizes:
        parts.append((start * LANES, size * LANES))
        start += size
    return tuple(parts)


def my_position():
    group, inner = lax.axis_index("group"), lax.axis_index("ingroup")
    return {
        "z": lax.div(group, CORES),
        "core": lax.rem(group, CORES),
        "x": lax.div(inner, RING),
        "y": lax.rem(inner, RING),
    }


def device_at(pos):
    return (pos["z"] * CORES + pos["core"], pos["x"] * RING + pos["y"])


def moved(pos, axis, by):
    other = dict(pos)
    other[axis] = lax.rem(pos[axis] + (by % RING), RING)
    return other


def sibling_of(pos):
    other = dict(pos)
    other["core"] = 1 - pos["core"]
    return other


def greet(devices):
    barrier = pltpu.get_barrier_semaphore()
    for device in devices:
        pl.semaphore_signal(barrier, inc=1, device_id=device, device_id_type=MESH)
    pl.semaphore_wait(barrier, len(devices))


class Copies:
    def __init__(self, send_sems, recv_sems):
        self.send_sems, self.recv_sems, self.started = send_sems, recv_sems, []

    def start(self, src, dst, device):
        slot = len(self.started)
        copy = pltpu.make_async_remote_copy(
            src_ref=src,
            dst_ref=dst,
            send_sem=self.send_sems.at[slot],
            recv_sem=self.recv_sems.at[slot],
            device_id=device,
            device_id_type=MESH,
        )
        copy.start()
        self.started.append(copy)
        return copy

    def finish(self):
        for copy in self.started:
            copy.wait_send()


def view_index(axes, fixed, split_axis, half, columns):
    index = []
    for axis in axes:
        if axis in fixed:
            index.append(fixed[axis])
        elif axis == split_axis and half is not None:
            index.append(pl.ds(half * (RING // 2), RING // 2))
        else:
            index.append(slice(None))
    index.append(slice(None))
    if split_axis is None and half is not None:
        low = (columns // LANES + 1) // 2 * LANES
        index.append(pl.ds(0, low) if half == 0 else pl.ds(low, columns - low))
    else:
        index.append(slice(None))
    return tuple(index)


class Gather:
    def __init__(self, copies, pos, ref, order):
        self.copies, self.pos, self.ref, self.order = copies, pos, ref, order
        self.columns = ref.shape[-1]

    def view(self, place, half):
        fixed = {axis: self.pos[axis] for axis in self.order[self.phase + 1 :]}
        fixed[self.axis] = place
        split_axis = self.order[0] if self.phase else None
        return self.ref.at[view_index(AXES, fixed, split_axis, half, self.columns)]

    def begin(self, phase):
        self.phase, self.axis = phase, self.order[phase]
        pos, axis = self.pos, self.axis
        self.plus, self.minus = device_at(moved(pos, axis, 1)), device_at(moved(pos, axis, -1))
        own = [self.view(pos[axis], half) for half in (0, 1)]
        self.first = [
            self.copies.start(own[0], own[0], self.plus),
            self.copies.start(own[1], own[1], self.minus),
            self.copies.start(own[1], own[1], self.plus),
            self.copies.start(own[0], own[0], self.minus),
        ]

    def relay(self):
        below = moved(self.pos, self.axis, -1)[self.axis]
        above = moved(self.pos, self.axis, 1)[self.axis]
        self.first[0].wait_recv()
        low = self.view(below, 0)
        self.far = [self.copies.start(low, low, self.plus)]
        self.first[1].wait_recv()
        high = self.view(above, 1)
        self.far.append(self.copies.start(high, high, self.minus))

    def wait_near(self):
        self.first[2].wait_recv()
        self.first[3].wait_recv()

    def wait_far(self):
        self.far[0].wait_recv()
        self.far[1].wait_recv()


class Scatter:
    def __init__(self, copies, pos, axes, ref, order, landing):
        self.copies, self.pos, self.axes, self.ref = copies, pos, axes, ref
        self.order, self.landing = order, landing
        self.columns = ref.shape[-1]

    def begin(self, phase):
        self.phase, self.axis = phase, self.order[phase]
        self.later = tuple(axis for axis in self.axes if axis in self.order[phase + 1 :])
        self.split_axis = self.order[-1] if self.later else None
        self.relayed, self.from_minus, self.from_plus = self.landing[phase]
        pos, axis = self.pos, self.axis
        self.above, self.below = moved(pos, axis, 1)[axis], moved(pos, axis, -1)[axis]
        self.across = moved(pos, axis, 2)[axis]
        self.plus, self.minus = device_at(moved(pos, axis, 1)), device_at(moved(pos, axis, -1))

    def fixed(self, place):
        fixed = {axis: self.pos[axis] for axis in self.order[: self.phase]}
        fixed[self.axis] = place
        return fixed

    def block(self, place, half):
        return self.ref.at[
            view_index(self.axes, self.fixed(place), self.split_axis, half, self.columns)
        ]

    def landed(self, ref, half):
        return ref.at[view_index(self.later, {}, self.split_axis, half, self.columns)]

    def send_far(self):
        start = self.copies.start
        self.far = [
            start(self.block(self.across, 0), self.landed(self.relayed, 0), self.plus),
            start(self.block(self.across, 1), self.landed(self.relayed, 1), self.minus),
        ]

    def send_near(self):
        start = self.copies.start
        self.near = [
            start(self.block(self.above, 1), self.landed(self.from_minus, 1), self.plus),
            start(self.block(self.below, 0), self.landed(self.from_plus, 0), self.minus),
        ]

    def add_into(self, place, half, refs):
        if not self.later:
            block = view_index(self.axes, self.fixed(place), None, half, self.columns)
            land = view_index((), {}, None, half, self.columns)
            total = self.ref[block].astype(F32)
            for ref in refs:
                total += ref[land].astype(F32)
            self.ref[block] = total.astype(BF16)
            return
        spans = [
            RING // 2 if axis == self.split_axis and half is not None else RING
            for axis in self.later
        ]
        steps = 1
        for span in spans:
            steps *= span

        def slab(step, carry):
            places, rest = {}, step
            for axis, span in reversed(list(zip(self.later, spans))):
                place_in = lax.rem(rest, span)
                rest = lax.div(rest, span)
                if axis == self.split_axis and half is not None:
                    place_in = place_in + half * (RING // 2)
                places[axis] = place_in
            land = tuple(places[axis] for axis in self.later)
            both = dict(places)
            both.update(self.fixed(place))
            block = tuple(both[axis] for axis in self.axes)
            total = self.ref[block].astype(F32)
            for ref in refs:
                total += ref[land].astype(F32)
            self.ref[block] = total.astype(BF16)
            return carry

        lax.fori_loop(0, steps, slab, 0)

    def relay(self):
        start = self.copies.start
        self.far[0].wait_recv()
        self.add_into(self.above, 0, [self.relayed])
        self.near.append(
            start(self.block(self.above, 0), self.landed(self.from_minus, 0), self.plus)
        )
        self.far[1].wait_recv()
        self.add_into(self.below, 1, [self.relayed])
        self.near.append(
            start(self.block(self.below, 1), self.landed(self.from_plus, 1), self.minus)
        )

    def wait_near(self):
        for copy in self.near:
            copy.wait_recv()

    def finish(self):
        self.wait_near()
        self.add_into(self.pos[self.axis], None, [self.from_minus, self.from_plus])

    def finish_last(self):
        self.wait_near()
        block = tuple(self.pos[axis] for axis in self.axes)
        total = self.ref[block].astype(F32)
        return total + self.from_minus[...].astype(F32) + self.from_plus[...].astype(F32)


def landing_shapes(axis_count, rows, columns):
    shapes = []
    for phase in range(axis_count):
        lead = (RING,) * (axis_count - 1 - phase)
        shapes += [pltpu.VMEM(lead + (rows, columns), BF16)] * 3
    return shapes


def by_phase(refs):
    return [refs[3 * k : 3 * k + 3] for k in range(len(refs) // 3)]


def attention_kernel(
    latent_ref,
    value_up_ref,
    out_proj_hbm,
    hidden_ref,
    gain_ref,
    attended_ref,
    normed_ref,
    latents,
    proj,
    head_out,
    residual,
    hidden_away,
    squares,
    squares_in,
    part_refs,
    landing_refs,
    send_sems,
    recv_sems,
    local_sem,
):
    pos = my_position()
    core, group, inner = pos["core"], lax.axis_index("group"), lax.axis_index("ingroup")
    sibling = device_at(sibling_of(pos))
    rows = hidden_ref.shape[0]
    half = normed_ref.shape[1]
    model_width = hidden_ref.shape[1]
    inner_count = latent_ref.shape[0]
    head_count, latent_width, value_width = value_up_ref.shape
    mine = pl.ds(pl.multiple_of(core * half, LANES), half)
    other = pl.ds(pl.multiple_of((1 - core) * half, LANES), half)
    load_proj = pltpu.make_async_copy(out_proj_hbm.at[:, mine], proj, local_sem)
    load_proj.start()
    peers = [lax.rem(inner + step, inner_count) for step in range(1, inner_count)]
    greet([(group, peer) for peer in peers] + [sibling])
    copies = Copies(send_sems, recv_sems)

    arrivals = [
        copies.start(latent_ref.at[peer], latents.at[inner], (group, peer)) for peer in peers
    ]
    latents[inner] = latent_ref[inner]
    hidden_away[...] = hidden_ref[:, other].astype(F32)
    hidden_in_copy = copies.start(hidden_away, residual.at[core], sibling)
    residual[core] = hidden_ref[:, mine].astype(F32)
    for copy in arrivals:
        copy.wait_recv()

    stacked = latents[...].reshape(inner_count * head_count * rows, latent_width)
    for head in range(head_count):
        product = jnp.dot(stacked, value_up_ref[head], preferred_element_type=F32)
        product = product.reshape(inner_count, head_count, rows, value_width)[:, head]
        head_out[:, core, :, head * value_width : (head + 1) * value_width] = product.astype(
            BF16
        ).astype(F32)
    heads_copy = copies.start(head_out.at[:, core], head_out.at[:, core], sibling)
    load_proj.wait()
    heads_copy.wait_recv()
    heads = head_out[...].reshape(
        inner_count * CORES * rows, head_count * value_width
    ).astype(BF16)

    parts = column_parts(half, len(PLANE_ORDERS))
    scatters = []
    for (start, columns), ref, landing, order in zip(
        parts, part_refs, landing_refs, PLANE_ORDERS
    ):
        partial = jnp.dot(heads, proj[:, start : start + columns], preferred_element_type=F32)
        ref[...] = partial.astype(BF16).reshape(ref.shape)
        scatter = Scatter(copies, pos, ("x", "y"), ref, order, by_phase(landing))
        scatter.begin(0)
        scatter.send_far()
        scatter.send_near()
        scatters.append(scatter)
    for scatter in scatters:
        scatter.relay()
    for scatter in scatters:
        scatter.finish()
        scatter.begin(1)
        scatter.send_far()
        scatter.send_near()
    for scatter in scatters:
        scatter.relay()
    hidden_in_copy.wait_recv()
    square_sum = jnp.zeros((CORES * rows, 1), F32)
    for (start, columns), scatter in zip(parts, scatters):
        total = scatter.finish_last()
        total += residual[:, :, start : start + columns].reshape(CORES * rows, columns)
        attended = total.astype(BF16)
        attended_ref[:, start : start + columns] = attended
        wide = attended.astype(F32)
        square_sum += jnp.sum(wide * wide, axis=1, keepdims=True)
    squares[...] = jnp.broadcast_to(square_sum, squares.shape)
    squares_copy = copies.start(squares, squares_in, sibling)
    squares_copy.wait_recv()
    mean_square = (square_sum + squares_in[:, :1]) / model_width
    scale = lax.rsqrt(mean_square + NORM_EPS)
    normed_ref[...] = (attended_ref[...].astype(F32) * scale * gain_ref[:, mine]).astype(BF16)
    copies.finish()


def attention_call(latent, value_up, out_proj, hidden_in, gain):
    rows, model_width = hidden_in.shape
    half = model_width // CORES
    chip_rows = CORES * rows
    inner_count = latent.shape[0]
    proj_rows = out_proj.shape[0]
    parts = column_parts(half, len(PLANE_ORDERS))
    vmem = pl.BlockSpec(memory_space=pltpu.VMEM)
    hbm = pl.BlockSpec(memory_space=pl.ANY)
    copy_count = inner_count - 1 + 3 + 2 * 2 * 6
    block = jax.ShapeDtypeStruct((chip_rows, half), BF16)
    return pl.pallas_call(
        attention_kernel,
        out_shape=(block, block),
        in_specs=[vmem, vmem, hbm, vmem, vmem],
        out_specs=(vmem, vmem),
        scratch_shapes=[
            pltpu.VMEM(latent.shape, BF16),
            pltpu.VMEM((proj_rows, half), BF16),
            pltpu.VMEM((inner_count, CORES, rows, proj_rows), F32),
            pltpu.VMEM((CORES, rows, half), F32),
            pltpu.VMEM((rows, half), F32),
            pltpu.VMEM((chip_rows, LANES), F32),
            pltpu.VMEM((chip_rows, LANES), F32),
            [pltpu.VMEM((RING, RING, chip_rows, columns), BF16) for _, columns in parts],
            [landing_shapes(2, chip_rows, columns) for _, columns in parts],
            pltpu.SemaphoreType.DMA((copy_count,)),
            pltpu.SemaphoreType.DMA((copy_count,)),
            pltpu.SemaphoreType.DMA,
        ],
        compiler_params=pltpu.CompilerParams(
            collective_id=0, has_side_effects=True, vmem_limit_bytes=40 * 2**20
        ),
        name="attention_out",
    )(latent, value_up, out_proj, hidden_in, gain)


def silu(value):
    return value / (1.0 + jnp.exp(-value))


def expert_kernel(
    normed_ref,
    attended_ref,
    weight_ref,
    gate_hbm,
    up_hbm,
    down_hbm,
    shared_gate_hbm,
    shared_up_hbm,
    shared_down_hbm,
    out_ref,
    row_refs,
    inner_weights,
    shared_weights,
    down_weights,
    row_scale,
    sums,
    sums_out,
    sums_in,
    shared_sums,
    shared_in,
    hidden,
    part_refs,
    landing_refs,
    final,
    final_in,
    send_sems,
    recv_sems,
    local_sems,
):
    pos = my_position()
    core = pos["core"]
    sibling = device_at(sibling_of(pos))
    chip_rows, half = normed_ref.shape
    rows = chip_rows // CORES
    unit_count = gate_hbm.shape[2]
    shared_count = shared_gate_hbm.shape[1]
    plane_rows = RING * RING * chip_rows
    mine = pl.ds(pl.multiple_of(core * half, LANES), half)
    other = pl.ds(pl.multiple_of((1 - core) * half, LANES), half)
    parts = column_parts(half, len(GATHER_ORDERS))

    own_units = pl.ds(pl.multiple_of(core * unit_count, unit_count), unit_count)
    shared_units = pl.ds(CORES * unit_count, shared_count)
    local = [
        (gate_hbm.at[0, mine, :], inner_weights.at[2 * core]),
        (up_hbm.at[0, mine, :], inner_weights.at[2 * core + 1]),
        (shared_gate_hbm.at[mine, :], shared_weights.at[0]),
        (shared_up_hbm.at[mine, :], shared_weights.at[1]),
        (down_hbm.at[0, :, mine], down_weights.at[own_units, :]),
        (shared_down_hbm.at[:, mine], down_weights.at[shared_units, :]),
    ]
    loads = []
    for slot, (src, dst) in enumerate(local):
        load = pltpu.make_async_copy(src, dst, local_sems.at[slot])
        load.start()
        loads.append(load)
    for (start, columns), ref in zip(parts, row_refs):
        ref[pos["z"], pos["x"], pos["y"]] = normed_ref[:, start : start + columns]

    neighbours = [device_at(moved(pos, axis, by)) for axis in AXES for by in (1, -1)]
    greet(neighbours + [sibling])
    copies = Copies(send_sems, recv_sems)
    gathers = [
        Gather(copies, pos, ref, order) for ref, order in zip(row_refs, GATHER_ORDERS)
    ]
    for gather in gathers:
        gather.begin(0)
    weight_copies = [
        copies.start(gate_hbm.at[0, other, :], inner_weights.at[2 * core], sibling),
        copies.start(up_hbm.at[0, other, :], inner_weights.at[2 * core + 1], sibling),
        copies.start(down_hbm.at[0, :, other], down_weights.at[own_units, :], sibling),
    ]

    def prepare(step, carry):
        z, plane = lax.div(step, RING * RING), lax.rem(step, RING * RING)
        x, y = lax.div(plane, RING), lax.rem(plane, RING)
        for which in range(2 * CORES):
            sums[which, z, x, y] = jnp.zeros((chip_rows, unit_count), F32)
        hidden[z, x, y, :, CORES * unit_count :] = jnp.zeros((chip_rows, shared_count), BF16)
        weights = weight_ref[z, :, plane].reshape(chip_rows, weight_ref.shape[-1])
        lane = lax.broadcasted_iota(jnp.int32, weights.shape, 1)
        for which in range(CORES):
            expert = (pos["z"] * CORES + which) * RING + pos["x"]
            scale = jnp.sum(jnp.where(lane == expert, weights, 0.0), axis=1, keepdims=True)
            row_scale[which, z, x, y] = jnp.broadcast_to(scale, (chip_rows, LANES))
        return carry

    lax.fori_loop(0, RING**3, prepare, 0)

    def multiply(which_part, place):
        start, columns = parts[which_part]
        ref = row_refs[which_part]
        axis = GATHER_ORDERS[which_part][-1]
        index = view_index(AXES, {axis: place}, None, None, columns)

        def one(which, carry):
            block = ref[index].reshape(plane_rows, columns)
            product = jnp.dot(
                block,
                inner_weights[which, start : start + columns, :],
                preferred_element_type=F32,
            )
            at = (which,) + index
            sums[at] = sums[at] + product.reshape(RING, RING, chip_rows, unit_count)
            return carry

        lax.fori_loop(0, 2 * CORES, one, 0)

    for phase in range(3):
        if phase:
            for gather in gathers:
                gather.begin(phase)
        last = phase == 2
        if last:
            for load in loads:
                load.wait()
            for copy in weight_copies:
                copy.wait_recv()
            for k, gather in enumerate(gathers):
                multiply(k, pos[gather.axis])
        for gather in gathers:
            gather.relay()
        for k, gather in enumerate(gathers):
            gather.wait_near()
            if last:
                multiply(k, moved(pos, gather.axis, 1)[gather.axis])
                multiply(k, moved(pos, gather.axis, -1)[gather.axis])
        for k, gather in enumerate(gathers):
            gather.wait_far()
            if last:
                multiply(k, moved(pos, gather.axis, 2)[gather.axis])

    exchanges = []
    for z in range(RING):

        def narrow(step, carry):
            which, plane = lax.div(step, RING * RING), lax.rem(step, RING * RING)
            x, y = lax.div(plane, RING), lax.rem(plane, RING)
            sums_out[which, z, x, y] = sums[which, z, x, y].astype(BF16)
            return carry

        lax.fori_loop(0, 2 * CORES * RING * RING, narrow, 0)
        exchanges.append(copies.start(sums_out.at[:, z], sums_in.at[:, z], sibling))
    for which in range(2):
        total = jnp.zeros((plane_rows, shared_count), F32)
        for (start, columns), ref in zip(parts, row_refs):
            total += jnp.dot(
                ref[pos["z"]].reshape(plane_rows, columns),
                shared_weights[which, start : start + columns, :],
                preferred_element_type=F32,
            )
        shared_sums[which] = total
    shared_copy = copies.start(shared_sums, shared_in, sibling)
    for z in range(RING):
        exchanges[z].wait_recv()

        def activate(plane, carry):
            x, y = lax.div(plane, RING), lax.rem(plane, RING)
            for which in range(CORES):
                gate, up = (
                    sums[2 * which + k, z, x, y] + sums_in[2 * which + k, z, x, y].astype(F32)
                    for k in (0, 1)
                )
                scale = row_scale[which, z, x, y]
                scale = jnp.concatenate([scale] * (unit_count // LANES), axis=1)
                value = (silu(gate) * up * scale).astype(BF16)
                hidden[z, x, y, :, which * unit_count : (which + 1) * unit_count] = value
            return carry

        lax.fori_loop(0, RING * RING, activate, 0)
    shared_copy.wait_recv()
    shared_gate_part, shared_up_part = (shared_sums[k] + shared_in[k] for k in (0, 1))
    shared_hidden = (silu(shared_gate_part) * shared_up_part).astype(BF16)
    hidden[pos["z"], :, :, :, CORES * unit_count :] = shared_hidden.reshape(
        RING, RING, chip_rows, shared_count
    )

    scatters = [
        Scatter(copies, pos, AXES, ref, order, by_phase(landing))
        for ref, order, landing in zip(part_refs, SCATTER_ORDERS, landing_refs)
    ]

    def project(which_part, place):
        start, columns = parts[which_part]
        scatter = scatters[which_part]
        index = view_index(AXES, {scatter.axis: place}, None, None, columns)
        product = jnp.dot(
            hidden[index].reshape(plane_rows, hidden.shape[-1]),
            down_weights[:, start : start + columns],
            preferred_element_type=F32,
        )
        scatter.ref[index] = product.astype(BF16).reshape(RING, RING, chip_rows, columns)

    for k, scatter in enumerate(scatters):
        scatter.begin(0)
        project(k, scatter.across)
        scatter.send_far()
    for k, scatter in enumerate(scatters):
        project(k, scatter.above)
        project(k, scatter.below)
        scatter.send_near()
    for k, scatter in enumerate(scatters):
        project(k, pos[scatter.axis])
    for phase in range(2):
        for scatter in scatters:
            scatter.relay()
        for scatter in scatters:
            scatter.finish()
            scatter.begin(phase + 1)
            scatter.send_far()
            scatter.send_near()
    for scatter in scatters:
        scatter.relay()
    for (start, columns), scatter in zip(parts, scatters):
        total = scatter.finish_last() + attended_ref[:, start : start + columns].astype(F32)
        final[:, :, start : start + columns] = total.reshape(CORES, rows, columns)
    final_copy = copies.start(final.at[1 - core], final_in, sibling)
    out_ref[:, mine] = final[core].astype(BF16)
    final_copy.wait_recv()
    out_ref[:, other] = final_in[...].astype(BF16)
    copies.finish()


def expert_call(normed, attended, weights, gate, up, down, shared_gate, shared_up, shared_down):
    chip_rows, half = normed.shape
    rows = chip_rows // CORES
    model_width = half * CORES
    unit_count = gate.shape[2]
    shared_count = shared_gate.shape[1]
    plane_rows = RING * RING * chip_rows
    depth = CORES * unit_count + shared_count
    parts = column_parts(half, len(GATHER_ORDERS))
    vmem = pl.BlockSpec(memory_space=pltpu.VMEM)
    hbm = pl.BlockSpec(memory_space=pl.ANY)
    grid3 = (RING, RING, RING)
    copy_count = 3 * 3 * 6 * 2 + 3 + RING + 2
    return pl.pallas_call(
        expert_kernel,
        out_shape=jax.ShapeDtypeStruct((rows, model_width), BF16),
        in_specs=[vmem, vmem, vmem] + [hbm] * 6,
        out_specs=vmem,
        scratch_shapes=[
            [pltpu.VMEM(grid3 + (chip_rows, columns), BF16) for _, columns in parts],
            pltpu.VMEM((2 * CORES, half, unit_count), BF16),
            pltpu.VMEM((2, half, shared_count), BF16),
            pltpu.VMEM((depth, half), BF16),
            pltpu.VMEM((CORES,) + grid3 + (chip_rows, LANES), F32),
            pltpu.VMEM((2 * CORES,) + grid3 + (chip_rows, unit_count), F32),
            pltpu.VMEM((2 * CORES,) + grid3 + (chip_rows, unit_count), BF16),
            pltpu.VMEM((2 * CORES,) + grid3 + (chip_rows, unit_count), BF16),
            pltpu.VMEM((2, plane_rows, shared_count), F32),
            pltpu.VMEM((2, plane_rows, shared_count), F32),
            pltpu.VMEM(grid3 + (chip_rows, depth), BF16),
            [pltpu.VMEM(grid3 + (chip_rows, columns), BF16) for _, columns in parts],
            [landing_shapes(3, chip_rows, columns) for _, columns in parts],
            pltpu.VMEM((CORES, rows, half), F32),
            pltpu.VMEM((rows, half), F32),
            pltpu.SemaphoreType.DMA((copy_count,)),
            pltpu.SemaphoreType.DMA((copy_count,)),
            pltpu.SemaphoreType.DMA((6,)),
        ],
        compiler_params=pltpu.CompilerParams(
            collective_id=1, has_side_effects=True, vmem_limit_bytes=60 * 2**20
        ),
        name="experts",
    )(normed, attended, weights, gate, up, down, shared_gate, shared_up, shared_down)


def ancestors(parents):
    node_count = parents.shape[-1]
    node_ids = jnp.arange(node_count, dtype=jnp.int32)
    reach = (parents[:, :, None] == node_ids) | (node_ids[:, None] == node_ids)
    hops = 1
    while hops < node_count - 1:
        reach = jnp.any(reach[:, :, :, None] & reach[:, None, :, :], axis=2)
        hops *= 2
    return reach


def attend(queries, node_keys, cache, cache_len, visible, latent_width):
    cache_scores = (
        jnp.einsum("bnhc,blc->bnhl", queries, cache, preferred_element_type=F32) * SCALE_QK
    )
    node_scores = (
        jnp.einsum("bnhc,bmc->bnhm", queries, node_keys, preferred_element_type=F32) * SCALE_QK
    )
    positions = jnp.arange(cache.shape[1], dtype=jnp.int32)
    cache_live = positions[None, :] < cache_len[:, None]
    cache_scores = jnp.where(cache_live[:, None, None, :], cache_scores, -jnp.inf)
    node_scores = jnp.where(visible[:, :, None, :], node_scores, -jnp.inf)
    highest = jnp.maximum(jnp.max(cache_scores, axis=-1), jnp.max(node_scores, axis=-1))[..., None]
    cache_exp = jnp.exp(cache_scores - highest)
    node_exp = jnp.exp(node_scores - highest)
    exp_total = jnp.sum(cache_exp, axis=-1, keepdims=True) + jnp.sum(
        node_exp, axis=-1, keepdims=True
    )
    cache_weights = (cache_exp / exp_total).astype(BF16)
    node_weights = (node_exp / exp_total).astype(BF16)
    latent = jnp.einsum(
        "bnhl,blc->bnhc", cache_weights, cache[:, :, :latent_width], preferred_element_type=F32
    )
    latent = latent + jnp.einsum(
        "bnhm,bmc->bnhc", node_weights, node_keys[:, :, :latent_width], preferred_element_type=F32
    )
    return latent.astype(BF16)


def local(
    hidden_in,
    queries,
    node_latent,
    cache,
    cache_len,
    parents,
    value_up,
    out_proj,
    ffn_gain,
    route_experts,
    route_weights,
    expert_gate,
    expert_up,
    expert_down,
    shared_gate,
    shared_up,
    shared_down,
):
    req_count, _, query_width = cache.shape
    node_count = parents.shape[1]
    rows, head_count = queries.shape[:2]
    latent_width = value_up.shape[1]
    group_count = lax.axis_size("group")
    inner_count = lax.axis_size("ingroup")
    expert_count = group_count * RING
    named = route_experts[:, :, None] == jnp.arange(expert_count, dtype=jnp.int32)
    weights = jnp.sum(jnp.where(named, route_weights[:, :, None], 0.0), axis=1)
    weights = lax.all_gather(weights, ("group", "ingroup"), axis=0, tiled=True)
    weights = weights.reshape(group_count // CORES, CORES, inner_count, rows, expert_count)
    latent = attend(
        queries.reshape(req_count, node_count, head_count, query_width),
        node_latent.reshape(req_count, node_count, query_width),
        cache,
        cache_len,
        ancestors(parents),
        latent_width,
    )
    latent = jnp.transpose(latent.reshape(rows, head_count, latent_width), (1, 0, 2))
    latent = latent.reshape(inner_count, head_count // inner_count * rows, latent_width)
    attended, normed = attention_call(
        latent, value_up, out_proj, hidden_in, ffn_gain.reshape(1, -1)
    )
    return expert_call(
        normed,
        attended,
        weights,
        expert_gate,
        expert_up,
        expert_down,
        shared_gate,
        shared_up,
        shared_down,
    )


def solution(mesh):
    both = ("group", "ingroup")
    in_specs = (
        P(both, None),
        P(both, None, None),
        P(both, None),
        P(both, None, None),
        P(both),
        P(both, None),
        P("ingroup", None, None),
        P("ingroup", None),
        P(),
        P(both, None),
        P(both, None),
        P(both, None, None),
        P(both, None, None),
        P(both, None, None),
        P(None, "ingroup"),
        P(None, "ingroup"),
        P("ingroup", None),
    )
    return jax.shard_map(
        local, mesh=mesh, in_specs=in_specs, out_specs=P(both, None), check_vma=False
    )
```

```python
import functools

import jax
import jax.numpy as jnp
from jax import lax
from jax.experimental import pallas as pl
from jax.experimental.pallas import tpu as pltpu
from jax.sharding import PartitionSpec as P

MESH = pl.DeviceIdType.MESH
F32 = jnp.float32
BF16 = jnp.bfloat16
SCALE_QK = 192.0 ** (-0.5)
NORM_EPS = 1e-06
RING = 4
CORES = 2
LANES = 128
VMEM_LIMIT = 62 * 2**20
AXES = ("z", "x", "y")
GATHER_ORDERS = (("x", "y", "z"), ("y", "z", "x"), ("z", "x", "y"))
SCATTER_ORDERS = (("z", "x", "y"), ("x", "y", "z"), ("y", "z", "x"))
PLANE_ORDERS = (("x", "y"), ("y", "x"))


def column_parts(width, count):
    tiles = width // LANES
    sizes = [tiles // count + (1 if k < tiles % count else 0) for k in range(count)]
    parts, start = [], 0
    for size in sizes:
        parts.append((start * LANES, size * LANES))
        start += size
    return tuple(parts)


def my_position():
    group, inner = lax.axis_index("group"), lax.axis_index("ingroup")
    return {
        "z": lax.div(group, CORES),
        "core": lax.rem(group, CORES),
        "x": lax.div(inner, RING),
        "y": lax.rem(inner, RING),
    }


def device_at(pos):
    return (pos["z"] * CORES + pos["core"], pos["x"] * RING + pos["y"])


def moved(pos, axis, by):
    other = dict(pos)
    other[axis] = lax.rem(pos[axis] + (by % RING), RING)
    return other


def sibling_of(pos):
    other = dict(pos)
    other["core"] = 1 - pos["core"]
    return other


class Copies:
    def __init__(self, send_sems, recv_sems):
        self.send_sems, self.recv_sems, self.started = send_sems, recv_sems, []

    def start(self, src, dst, device):
        slot = len(self.started)
        copy = pltpu.make_async_remote_copy(
            src_ref=src,
            dst_ref=dst,
            send_sem=self.send_sems.at[slot],
            recv_sem=self.recv_sems.at[slot],
            device_id=device,
            device_id_type=MESH,
        )
        copy.start()
        self.started.append(copy)
        return copy

    def finish(self):
        for copy in self.started:
            copy.wait_send()


def view_index(axes, fixed, split_axis, half, columns):
    index = []
    for axis in axes:
        if axis in fixed:
            index.append(fixed[axis])
        elif axis == split_axis and half is not None:
            index.append(pl.ds(half * (RING // 2), RING // 2))
        else:
            index.append(slice(None))
    index.append(slice(None))
    if split_axis is None and half is not None:
        low = (columns // LANES + 1) // 2 * LANES
        index.append(pl.ds(0, low) if half == 0 else pl.ds(low, columns - low))
    else:
        index.append(slice(None))
    return tuple(index)


class Gather:
    def __init__(self, copies, pos, ref, order):
        self.copies, self.pos, self.ref, self.order = copies, pos, ref, order
        self.columns = ref.shape[-1]

    def view(self, place, half):
        fixed = {axis: self.pos[axis] for axis in self.order[self.phase + 1 :]}
        fixed[self.axis] = place
        split_axis = self.order[0] if self.phase else None
        return self.ref.at[view_index(AXES, fixed, split_axis, half, self.columns)]

    def begin(self, phase):
        self.phase, self.axis = phase, self.order[phase]
        pos, axis = self.pos, self.axis
        self.plus, self.minus = device_at(moved(pos, axis, 1)), device_at(moved(pos, axis, -1))
        own = [self.view(pos[axis], half) for half in (0, 1)]
        self.first = [
            self.copies.start(own[0], own[0], self.plus),
            self.copies.start(own[1], own[1], self.minus),
            self.copies.start(own[1], own[1], self.plus),
            self.copies.start(own[0], own[0], self.minus),
        ]

    def relay(self):
        below = moved(self.pos, self.axis, -1)[self.axis]
        above = moved(self.pos, self.axis, 1)[self.axis]
        self.first[0].wait_recv()
        low = self.view(below, 0)
        self.far = [self.copies.start(low, low, self.plus)]
        self.first[1].wait_recv()
        high = self.view(above, 1)
        self.far.append(self.copies.start(high, high, self.minus))

    def wait_near(self):
        self.first[2].wait_recv()
        self.first[3].wait_recv()

    def wait_far(self):
        self.far[0].wait_recv()
        self.far[1].wait_recv()


class Scatter:
    def __init__(self, copies, pos, axes, ref, order, landing):
        self.copies, self.pos, self.axes, self.ref = copies, pos, axes, ref
        self.order, self.landing = order, landing
        self.columns = ref.shape[-1]

    def begin(self, phase):
        self.phase, self.axis = phase, self.order[phase]
        self.later = tuple(axis for axis in self.axes if axis in self.order[phase + 1 :])
        self.split_axis = self.order[-1] if self.later else None
        self.relayed, self.from_minus, self.from_plus = self.landing[phase]
        pos, axis = self.pos, self.axis
        self.above, self.below = moved(pos, axis, 1)[axis], moved(pos, axis, -1)[axis]
        self.across = moved(pos, axis, 2)[axis]
        self.plus, self.minus = device_at(moved(pos, axis, 1)), device_at(moved(pos, axis, -1))

    def fixed(self, place):
        fixed = {axis: self.pos[axis] for axis in self.order[: self.phase]}
        fixed[self.axis] = place
        return fixed

    def block(self, place, half):
        return self.ref.at[
            view_index(self.axes, self.fixed(place), self.split_axis, half, self.columns)
        ]

    def landed(self, ref, half):
        return ref.at[view_index(self.later, {}, self.split_axis, half, self.columns)]

    def send_far(self):
        start = self.copies.start
        self.far = [
            start(self.block(self.across, 0), self.landed(self.relayed, 0), self.plus),
            start(self.block(self.across, 1), self.landed(self.relayed, 1), self.minus),
        ]

    def send_near(self):
        start = self.copies.start
        self.near = [
            start(self.block(self.above, 1), self.landed(self.from_minus, 1), self.plus),
            start(self.block(self.below, 0), self.landed(self.from_plus, 0), self.minus),
        ]

    def add_into(self, place, half, refs):
        if not self.later:
            block = view_index(self.axes, self.fixed(place), None, half, self.columns)
            land = view_index((), {}, None, half, self.columns)
            total = self.ref[block].astype(F32)
            for ref in refs:
                total += ref[land].astype(F32)
            self.ref[block] = total.astype(BF16)
            return
        spans = [
            RING // 2 if axis == self.split_axis and half is not None else RING
            for axis in self.later
        ]
        steps = 1
        for span in spans:
            steps *= span

        def slab(step, carry):
            places, rest = {}, step
            for axis, span in reversed(list(zip(self.later, spans))):
                place_in = lax.rem(rest, span)
                rest = lax.div(rest, span)
                if axis == self.split_axis and half is not None:
                    place_in = place_in + half * (RING // 2)
                places[axis] = place_in
            land = tuple(places[axis] for axis in self.later)
            both = dict(places)
            both.update(self.fixed(place))
            block = tuple(both[axis] for axis in self.axes)
            total = self.ref[block].astype(F32)
            for ref in refs:
                total += ref[land].astype(F32)
            self.ref[block] = total.astype(BF16)
            return carry

        lax.fori_loop(0, steps, slab, 0)

    def relay(self):
        start = self.copies.start
        self.far[0].wait_recv()
        self.add_into(self.above, 0, [self.relayed])
        self.near.append(
            start(self.block(self.above, 0), self.landed(self.from_minus, 0), self.plus)
        )
        self.far[1].wait_recv()
        self.add_into(self.below, 1, [self.relayed])
        self.near.append(
            start(self.block(self.below, 1), self.landed(self.from_plus, 1), self.minus)
        )

    def wait_near(self):
        for copy in self.near:
            copy.wait_recv()

    def finish(self):
        self.wait_near()
        self.add_into(self.pos[self.axis], None, [self.from_minus, self.from_plus])

    def finish_last(self):
        self.wait_near()
        block = tuple(self.pos[axis] for axis in self.axes)
        total = self.ref[block].astype(F32)
        return total + self.from_minus[...].astype(F32) + self.from_plus[...].astype(F32)


def landing_shapes(axis_count, rows, columns):
    shapes = []
    for phase in range(axis_count):
        lead = (RING,) * (axis_count - 1 - phase)
        shapes += [pltpu.VMEM(lead + (rows, columns), BF16)] * 3
    return shapes


def by_phase(refs):
    return [refs[3 * k : 3 * k + 3] for k in range(len(refs) // 3)]


def landing_shapes(axis_count, rows, columns):
    shapes = []
    for phase in range(axis_count):
        lead = (RING,) * (axis_count - 1 - phase)
        shapes += [pltpu.VMEM(lead + (rows, columns), BF16)] * 3
    return shapes


def by_phase(refs):
    return [refs[3 * k : 3 * k + 3] for k in range(len(refs) // 3)]


def attention_kernel(
    latent_ref,
    value_up_ref,
    out_proj_hbm,
    hidden_ref,
    gain_ref,
    attended_ref,
    normed_ref,
    latents,
    proj,
    head_out,
    residual,
    hidden_away,
    squares,
    squares_in,
    part_refs,
    landing_refs,
    send_sems,
    recv_sems,
    local_sem,
):
    pos = my_position()
    core, group, inner = pos["core"], lax.axis_index("group"), lax.axis_index("ingroup")
    sibling = device_at(sibling_of(pos))
    rows = hidden_ref.shape[0]
    half = normed_ref.shape[1]
    model_width = hidden_ref.shape[1]
    inner_count = latent_ref.shape[0]
    head_count, latent_width, value_width = value_up_ref.shape
    mine = pl.ds(pl.multiple_of(core * half, LANES), half)
    other = pl.ds(pl.multiple_of((1 - core) * half, LANES), half)
    load_proj = pltpu.make_async_copy(out_proj_hbm.at[:, mine], proj, local_sem)
    load_proj.start()
    peers = [lax.rem(inner + step, inner_count) for step in range(1, inner_count)]
    greet([(group, peer) for peer in peers] + [sibling])
    copies = Copies(send_sems, recv_sems)

    arrivals = [
        copies.start(latent_ref.at[peer], latents.at[inner], (group, peer)) for peer in peers
    ]
    latents[inner] = latent_ref[inner]
    hidden_away[...] = hidden_ref[:, other].astype(F32)
    hidden_in_copy = copies.start(hidden_away, residual.at[core], sibling)
    residual[core] = hidden_ref[:, mine].astype(F32)
    for copy in arrivals:
        copy.wait_recv()

    stacked = latents[...].reshape(inner_count * head_count * rows, latent_width)
    for head in range(head_count):
        product = jnp.dot(stacked, value_up_ref[head], preferred_element_type=F32)
        product = product.reshape(inner_count, head_count, rows, value_width)[:, head]
        head_out[:, core, :, head * value_width : (head + 1) * value_width] = product.astype(
            BF16
        ).astype(F32)
    heads_copy = copies.start(head_out.at[:, core], head_out.at[:, core], sibling)
    load_proj.wait()
    heads_copy.wait_recv()
    heads = head_out[...].reshape(
        inner_count * CORES * rows, head_count * value_width
    ).astype(BF16)

    parts = column_parts(half, len(PLANE_ORDERS))
    scatters = []
    for (start, columns), ref, landing, order in zip(
        parts, part_refs, landing_refs, PLANE_ORDERS
    ):
        partial = jnp.dot(heads, proj[:, start : start + columns], preferred_element_type=F32)
        ref[...] = partial.astype(BF16).reshape(ref.shape)
        scatter = Scatter(copies, pos, ("x", "y"), ref, order, by_phase(landing))
        scatter.begin(0)
        scatter.send_far()
        scatter.send_near()
        scatters.append(scatter)
    for scatter in scatters:
        scatter.relay()
    for scatter in scatters:
        scatter.finish()
        scatter.begin(1)
        scatter.send_far()
        scatter.send_near()
    for scatter in scatters:
        scatter.relay()
    hidden_in_copy.wait_recv()
    square_sum = jnp.zeros((CORES * rows, 1), F32)
    for (start, columns), scatter in zip(parts, scatters):
        total = scatter.finish_last()
        total += residual[:, :, start : start + columns].reshape(CORES * rows, columns)
        attended = total.astype(BF16)
        attended_ref[:, start : start + columns] = attended
        wide = attended.astype(F32)
        square_sum += jnp.sum(wide * wide, axis=1, keepdims=True)
    squares[...] = jnp.broadcast_to(square_sum, squares.shape)
    squares_copy = copies.start(squares, squares_in, sibling)
    squares_copy.wait_recv()
    mean_square = (square_sum + squares_in[:, :1]) / model_width
    scale = lax.rsqrt(mean_square + NORM_EPS)
    normed_ref[...] = (attended_ref[...].astype(F32) * scale * gain_ref[:, mine]).astype(BF16)
    copies.finish()


def nt_dot(left, right):
    return lax.dot_general(left, right, (((1,), (1,)), ((), ())), preferred_element_type=F32)


def nn_dot(left, right):
    return jnp.dot(left, right, preferred_element_type=F32)


def silu(value):
    return value / (1.0 + jnp.exp(-value))


def visible_from(parents):
    count = parents.shape[-1]
    above = lax.broadcasted_iota(jnp.int32, (count, count), 0)
    below = lax.broadcasted_iota(jnp.int32, (count, count), 1)
    reach = ((above == parents) | (above == below)).astype(F32)
    hops = 1
    while hops < count - 1:
        reach = (nn_dot(reach.astype(BF16), reach.astype(BF16)) > 0.5).astype(F32)
        hops *= 2
    return reach.astype(BF16)


def routing_lanes(experts, weights, expert_count):
    rows, top = experts.shape
    lane = lax.rem(lax.broadcasted_iota(jnp.int32, (rows, LANES), 1), expert_count)
    total = jnp.zeros((rows, LANES), F32)
    for k in range(top):
        total += jnp.where(lane == experts[:, k : k + 1], weights[:, k : k + 1], 0.0)
    return total


def in_three(values, expert_count):
    high = values.astype(BF16).astype(F32)
    middle = (values - high).astype(BF16).astype(F32)
    low = values - high - middle
    lane = lax.broadcasted_iota(jnp.int32, values.shape, 1)
    terms = jnp.where(
        lane < expert_count,
        high,
        jnp.where(lane < 2 * expert_count, middle, jnp.where(lane < 3 * expert_count, low, 0.0)),
    )
    return terms.astype(BF16)


def layer_kernel(
    cache_len_ref,
    parents_ref,
    experts_ref,
    weights_ref,
    hidden_ref,
    node_ref,
    gain_ref,
    queries_hbm,
    cache_hbm,
    value_up_hbm,
    out_proj_hbm,
    gate_hbm,
    up_hbm,
    down_hbm,
    shared_gate_hbm,
    shared_up_hbm,
    shared_down_hbm,
    out_ref,
    queries,
    cache,
    value_up,
    proj,
    latent_out,
    latents,
    head_out,
    residual,
    hidden_away,
    squares,
    squares_in,
    attended_rows,
    plane_refs,
    plane_landing,
    row_refs,
    inner_weights,
    shared_weights,
    down_weights,
    row_scale,
    sums,
    sums_out,
    sums_in,
    shared_sums,
    shared_in,
    hidden,
    part_refs,
    landing_refs,
    final,
    final_in,
    latent_send,
    latent_recv,
    send_sems,
    recv_sems,
    local_sems,
):
    pos = my_position()
    core, group, inner = pos["core"], lax.axis_index("group"), lax.axis_index("ingroup")
    sibling = device_at(sibling_of(pos))
    rows, model_width = hidden_ref.shape
    half = model_width // CORES
    chip_rows = CORES * rows
    plane_rows = RING * RING * chip_rows
    inner_count, _, latent_width = latents.shape
    head_count, _, value_width = value_up.shape
    all_heads, cached = queries.shape[1], cache.shape[1]
    unit_count = gate_hbm.shape[2]
    shared_count = shared_gate_hbm.shape[0]
    expert_count = RING * CORES * RING
    mine = pl.ds(pl.multiple_of(core * half, LANES), half)
    other = pl.ds(pl.multiple_of((1 - core) * half, LANES), half)
    own_units = pl.ds(pl.multiple_of(core * unit_count, unit_count), unit_count)
    shared_units = pl.ds(CORES * unit_count, shared_count)

    loads = []

    def load(src, dst):
        copy = pltpu.make_async_copy(src, dst, local_sems.at[len(loads)])
        copy.start()
        loads.append(copy)
        return copy

    first_loads = [load(queries_hbm, queries), load(cache_hbm.at[0], cache)]
    head_loads = [load(value_up_hbm, value_up), load(out_proj_hbm.at[:, mine], proj)]

    peers = [lax.rem(inner + step, inner_count) for step in range(1, inner_count)]
    z_neighbours = [device_at(moved(pos, "z", by)) for by in (1, -1)]
    partners = [(group, peer) for peer in peers] + z_neighbours + [sibling]
    barrier = pltpu.get_barrier_semaphore()
    for partner in partners:
        pl.semaphore_signal(barrier, inc=1, device_id=partner, device_id_type=MESH)

    routing = routing_lanes(experts_ref[...], weights_ref[...], expert_count)
    hidden_away[:, :half] = hidden_ref[:, other].astype(F32)
    hidden_away[:, half:] = routing
    residual[core, :, :half] = hidden_ref[:, mine].astype(F32)
    residual[core, :, half:] = routing

    reach = visible_from(parents_ref[...])
    node_keys = node_ref[...]
    chunk_heads = all_heads // 2
    chunk_rows = chunk_heads * rows
    chunk_peers = inner_count // 2
    row = lax.broadcasted_iota(jnp.int32, (chunk_rows, rows), 0)
    lane = lax.broadcasted_iota(jnp.int32, (chunk_rows, rows), 1)
    node_of = (lax.div(row, chunk_heads) == lane).astype(F32).astype(BF16)
    seen = nt_dot(node_of, reach) > 0.5
    to_row = lax.broadcasted_iota(jnp.int32, (chunk_rows, chunk_rows), 0)
    from_row = lax.broadcasted_iota(jnp.int32, (chunk_rows, chunk_rows), 1)
    head_major = (
        (from_row == lax.rem(to_row, rows) * chunk_heads + lax.div(to_row, rows))
        .astype(F32)
        .astype(BF16)
    )
    for copy in first_loads:
        copy.wait()

    def latent_copy(peer):
        return pltpu.make_async_remote_copy(
            src_ref=latent_out.at[peer],
            dst_ref=latents.at[inner],
            send_sem=latent_send.at[peer],
            recv_sem=latent_recv.at[inner],
            device_id=(group, peer),
            device_id_type=MESH,
        )

    for chunk in range(2):
        query = queries[:, chunk * chunk_heads : (chunk + 1) * chunk_heads, :]
        query = query.reshape(chunk_rows, query.shape[-1])
        scores = nn_dot(query, cache[...]) * SCALE_QK
        live = lax.broadcasted_iota(jnp.int32, scores.shape, 1) < cache_len_ref[0]
        scores = jnp.where(live, scores, -jnp.inf)
        node_scores = jnp.where(seen, nt_dot(query, node_keys) * SCALE_QK, -jnp.inf)
        highest = jnp.maximum(
            jnp.max(scores, axis=1, keepdims=True), jnp.max(node_scores, axis=1, keepdims=True)
        )
        scores = jnp.exp(scores - highest)
        node_scores = jnp.exp(node_scores - highest)
        total = jnp.sum(scores, axis=1, keepdims=True) + jnp.sum(
            node_scores, axis=1, keepdims=True
        )
        share = 1.0 / total
        latent = nt_dot((scores * share).astype(BF16), cache[:latent_width, :])
        latent += nn_dot((node_scores * share).astype(BF16), node_keys[:, :latent_width])
        latent = nn_dot(head_major, latent.astype(BF16)).astype(BF16)
        latent_out[chunk * chunk_peers : (chunk + 1) * chunk_peers] = latent.reshape(
            chunk_peers, head_count * rows, latent_width
        )
        if chunk == 0:
            pl.semaphore_wait(barrier, len(partners))
        for peer in range(chunk * chunk_peers, (chunk + 1) * chunk_peers):

            @pl.when(inner != peer)
            def _(peer=peer):
                latent_copy(peer).start()

    copies = Copies(send_sems, recv_sems)
    hidden_copy = copies.start(hidden_away, residual.at[core], sibling)
    late_loads = [
        load(gate_hbm.at[0, mine, :], inner_weights.at[2 * core]),
        load(up_hbm.at[0, mine, :], inner_weights.at[2 * core + 1]),
        load(shared_gate_hbm.at[:, mine], shared_weights.at[0]),
        load(shared_up_hbm.at[:, mine], shared_weights.at[1]),
        load(down_hbm.at[0, :, mine], down_weights.at[own_units, :]),
        load(shared_down_hbm.at[:, mine], down_weights.at[shared_units, :]),
    ]

    def prepare(step, carry):
        z, plane = lax.div(step, RING * RING), lax.rem(step, RING * RING)
        x, y = lax.div(plane, RING), lax.rem(plane, RING)
        for which in range(2 * CORES):
            sums[which, z, x, y] = jnp.zeros((chip_rows, unit_count), F32)
        hidden[z, x, y, :, CORES * unit_count :] = jnp.zeros((chip_rows, shared_count), BF16)
        return carry

    lax.fori_loop(0, RING**3, prepare, 0)

    latents[inner] = latent_out[inner]
    for peer in range(inner_count):

        @pl.when(inner != peer)
        def _(peer=peer):
            pltpu.make_async_remote_copy(
                src_ref=latent_out.at[peer],
                dst_ref=latents.at[peer],
                send_sem=latent_send.at[peer],
                recv_sem=latent_recv.at[peer],
                device_id=(group, peer),
                device_id_type=MESH,
            ).wait_recv()

    for copy in head_loads:
        copy.wait()
    stacked = latents[...].reshape(inner_count * head_count * rows, latent_width)
    for head in range(head_count):
        product = nn_dot(stacked, value_up[head])
        product = product.reshape(inner_count, head_count, rows, value_width)[:, head]
        head_out[:, core, :, head * value_width : (head + 1) * value_width] = product.astype(
            BF16
        ).astype(F32)
    heads_copy = copies.start(head_out.at[:, core], head_out.at[:, core], sibling)
    heads_copy.wait_recv()
    weight_copies = [
        copies.start(gate_hbm.at[0, other, :], inner_weights.at[2 * core], sibling),
        copies.start(up_hbm.at[0, other, :], inner_weights.at[2 * core + 1], sibling),
        copies.start(down_hbm.at[0, :, other], down_weights.at[own_units, :], sibling),
    ]
    heads = head_out[...].reshape(plane_rows, head_count * value_width).astype(BF16)

    plane_parts = column_parts(half, len(PLANE_ORDERS))
    scatters = []
    for (start, columns), ref, landing, order in zip(
        plane_parts, plane_refs, plane_landing, PLANE_ORDERS
    ):
        partial = nn_dot(heads, proj[:, start : start + columns])
        ref[...] = partial.astype(BF16).reshape(ref.shape)
        scatter = Scatter(copies, pos, ("x", "y"), ref, order, by_phase(landing))
        scatter.begin(0)
        scatter.send_far()
        scatter.send_near()
        scatters.append(scatter)
    for scatter in scatters:
        scatter.relay()
    for scatter in scatters:
        scatter.finish()
        scatter.begin(1)
        scatter.send_far()
        scatter.send_near()
    for scatter in scatters:
        scatter.relay()
    hidden_copy.wait_recv()
    square_sum = jnp.zeros((chip_rows, 1), F32)
    for (start, columns), scatter in zip(plane_parts, scatters):
        total = scatter.finish_last()
        total += residual[:, :, start : start + columns].reshape(chip_rows, columns)
        attended = total.astype(BF16)
        attended_rows[:, start : start + columns] = attended
        wide = attended.astype(F32)
        square_sum += jnp.sum(wide * wide, axis=1, keepdims=True)
    squares[...] = jnp.broadcast_to(square_sum, squares.shape)
    squares_copy = copies.start(squares, squares_in, sibling)
    squares_copy.wait_recv()
    mean_square = (square_sum + squares_in[:, :1]) / model_width
    scale = lax.rsqrt(mean_square + NORM_EPS)
    normed = (attended_rows[...].astype(F32) * scale * gain_ref[:, mine]).astype(BF16)

    parts = column_parts(half, len(GATHER_ORDERS))
    for (start, columns), ref in zip(parts, row_refs):
        ref[pos["z"], pos["x"], pos["y"], :, :columns] = normed[:, start : start + columns]
    weighed = parts[1][1]
    row_refs[1][pos["z"], pos["x"], pos["y"], :, weighed:] = in_three(
        residual[:, :, half:].reshape(chip_rows, LANES), expert_count
    )
    gathers = [
        Gather(copies, pos, ref, order) for ref, order in zip(row_refs, GATHER_ORDERS)
    ]

    def multiply(which_part, place):
        start, columns = parts[which_part]
        ref = row_refs[which_part]
        axis = GATHER_ORDERS[which_part][-1]
        index = view_index(AXES, {axis: place}, None, None, columns)

        def one(which, carry):
            block = ref[index[:-1] + (slice(0, columns),)].reshape(plane_rows, columns)
            product = nn_dot(block, inner_weights[which, start : start + columns, :])
            at = (which,) + index
            sums[at] = sums[at] + product.reshape(RING, RING, chip_rows, unit_count)
            return carry

        lax.fori_loop(0, 2 * CORES, one, 0)

    for phase in range(3):
        for gather in gathers:
            gather.begin(phase)
        last = phase == 2
        if last:
            for copy in late_loads:
                copy.wait()
            for copy in weight_copies:
                copy.wait_recv()
            for k, gather in enumerate(gathers):
                multiply(k, pos[gather.axis])
        for gather in gathers:
            gather.relay()
        for k, gather in enumerate(gathers):
            gather.wait_near()
            if last:
                multiply(k, moved(pos, gather.axis, 1)[gather.axis])
                multiply(k, moved(pos, gather.axis, -1)[gather.axis])
        for k, gather in enumerate(gathers):
            gather.wait_far()
            if last:
                multiply(k, moved(pos, gather.axis, 2)[gather.axis])

    exchanges = []
    for z in range(RING):

        def narrow(step, carry):
            which, plane = lax.div(step, RING * RING), lax.rem(step, RING * RING)
            x, y = lax.div(plane, RING), lax.rem(plane, RING)
            sums_out[which, z, x, y] = sums[which, z, x, y].astype(BF16)
            return carry

        lax.fori_loop(0, 2 * CORES * RING * RING, narrow, 0)
        exchanges.append(copies.start(sums_out.at[:, z], sums_in.at[:, z], sibling))
    for which in range(2):
        total = jnp.zeros((plane_rows, shared_count), F32)
        for (start, columns), ref in zip(parts, row_refs):
            total += nt_dot(
                ref[pos["z"], :, :, :, :columns].reshape(plane_rows, columns),
                shared_weights[which, :, start : start + columns],
            )
        shared_sums[which] = total
    shared_copy = copies.start(shared_sums, shared_in, sibling)
    picks_from = lax.broadcasted_iota(jnp.int32, (LANES, CORES * LANES), 0)
    picks_to = lax.div(lax.broadcasted_iota(jnp.int32, (LANES, CORES * LANES), 1), LANES)
    chosen = (pos["z"] * CORES + picks_to) * RING + pos["x"]
    picks = ((lax.rem(picks_from, expert_count) == chosen).astype(F32)).astype(BF16)
    for z in range(RING):
        terms = row_refs[1][z, :, :, :, weighed:].reshape(plane_rows, LANES)
        row_scale[z] = nn_dot(terms, picks).reshape(RING, RING, chip_rows, CORES * LANES)
    for z in range(RING):
        exchanges[z].wait_recv()

        def activate(plane, carry):
            x, y = lax.div(plane, RING), lax.rem(plane, RING)
            for which in range(CORES):
                gate, up = (
                    sums[2 * which + k, z, x, y] + sums_in[2 * which + k, z, x, y].astype(F32)
                    for k in (0, 1)
                )
                scale = row_scale[z, x, y, :, which * LANES : (which + 1) * LANES]
                scale = jnp.concatenate([scale] * (unit_count // LANES), axis=1)
                value = (silu(gate) * up * scale).astype(BF16)
                hidden[z, x, y, :, which * unit_count : (which + 1) * unit_count] = value
            return carry

        lax.fori_loop(0, RING * RING, activate, 0)
    shared_copy.wait_recv()
    shared_gate_part, shared_up_part = (shared_sums[k] + shared_in[k] for k in (0, 1))
    shared_hidden = (silu(shared_gate_part) * shared_up_part).astype(BF16)
    hidden[pos["z"], :, :, :, CORES * unit_count :] = shared_hidden.reshape(
        RING, RING, chip_rows, shared_count
    )

    scatters = [
        Scatter(copies, pos, AXES, ref, order, by_phase(landing))
        for ref, order, landing in zip(part_refs, SCATTER_ORDERS, landing_refs)
    ]

    def project(which_part, place):
        start, columns = parts[which_part]
        scatter = scatters[which_part]
        index = view_index(AXES, {scatter.axis: place}, None, None, columns)
        product = nn_dot(
            hidden[index].reshape(plane_rows, hidden.shape[-1]),
            down_weights[:, start : start + columns],
        )
        scatter.ref[index] = product.astype(BF16).reshape(RING, RING, chip_rows, columns)

    for k, scatter in enumerate(scatters):
        scatter.begin(0)
        project(k, scatter.across)
        scatter.send_far()
    for k, scatter in enumerate(scatters):
        project(k, scatter.above)
        project(k, scatter.below)
        scatter.send_near()
    for k, scatter in enumerate(scatters):
        project(k, pos[scatter.axis])
    for phase in range(2):
        for scatter in scatters:
            scatter.relay()
        for scatter in scatters:
            scatter.finish()
            scatter.begin(phase + 1)
            scatter.send_far()
            scatter.send_near()
    for scatter in scatters:
        scatter.relay()
    for (start, columns), scatter in zip(parts, scatters):
        total = scatter.finish_last() + attended_rows[:, start : start + columns].astype(F32)
        final[:, :, start : start + columns] = total.reshape(CORES, rows, columns)
    final_copy = copies.start(final.at[1 - core], final_in, sibling)
    out_ref[:, mine] = final[core].astype(BF16)
    final_copy.wait_recv()
    out_ref[:, other] = final_in[...].astype(BF16)
    copies.finish()
    for peer in range(inner_count):

        @pl.when(inner != peer)
        def _(peer=peer):
            latent_copy(peer).wait_send()


def local(
    hidden_in,
    queries,
    node_latent,
    cache,
    cache_len,
    parents,
    value_up,
    out_proj,
    ffn_gain,
    route_experts,
    route_weights,
    expert_gate,
    expert_up,
    expert_down,
    shared_gate,
    shared_up,
    shared_down,
):
    rows, model_width = hidden_in.shape
    half = model_width // CORES
    chip_rows = CORES * rows
    inner_count = lax.axis_size("ingroup")
    head_count, latent_width, value_width = value_up.shape
    proj_rows = out_proj.shape[0]
    unit_count = expert_gate.shape[2]
    shared_count = shared_gate.shape[1]
    plane_rows = RING * RING * chip_rows
    depth = CORES * unit_count + shared_count
    plane_parts = column_parts(half, len(PLANE_ORDERS))
    parts = column_parts(half, len(GATHER_ORDERS))
    gathered = [columns + (LANES if k == 1 else 0) for k, (_, columns) in enumerate(parts)]
    grid3 = (RING, RING, RING)
    vmem = pl.BlockSpec(memory_space=pltpu.VMEM)
    smem = pl.BlockSpec(memory_space=pltpu.SMEM)
    hbm = pl.BlockSpec(memory_space=pl.ANY)
    copy_count = 2 * 2 * 6 + 3 * 3 * 6 * 2 + 3 + RING + 5
    load_count = 10
    return pl.pallas_call(
        layer_kernel,
        out_shape=jax.ShapeDtypeStruct((rows, model_width), BF16),
        in_specs=[smem] + [vmem] * 6 + [hbm] * 10,
        out_specs=vmem,
        scratch_shapes=[
            pltpu.VMEM(queries.shape, BF16),
            pltpu.VMEM((cache.shape[2], cache.shape[1]), BF16),
            pltpu.VMEM(value_up.shape, BF16),
            pltpu.VMEM((proj_rows, half), BF16),
            pltpu.VMEM((inner_count, head_count * rows, latent_width), BF16),
            pltpu.VMEM((inner_count, head_count * rows, latent_width), BF16),
            pltpu.VMEM((inner_count, CORES, rows, proj_rows), F32),
            pltpu.VMEM((CORES, rows, half + LANES), F32),
            pltpu.VMEM((rows, half + LANES), F32),
            pltpu.VMEM((chip_rows, LANES), F32),
            pltpu.VMEM((chip_rows, LANES), F32),
            pltpu.VMEM((chip_rows, half), BF16),
            [pltpu.VMEM((RING, RING, chip_rows, columns), BF16) for _, columns in plane_parts],
            [landing_shapes(2, chip_rows, columns) for _, columns in plane_parts],
            [pltpu.VMEM(grid3 + (chip_rows, columns), BF16) for columns in gathered],
            pltpu.VMEM((2 * CORES, half, unit_count), BF16),
            pltpu.VMEM((2, shared_count, half), BF16),
            pltpu.VMEM((depth, half), BF16),
            pltpu.VMEM(grid3 + (chip_rows, CORES * LANES), F32),
            pltpu.VMEM((2 * CORES,) + grid3 + (chip_rows, unit_count), F32),
            pltpu.VMEM((2 * CORES,) + grid3 + (chip_rows, unit_count), BF16),
            pltpu.VMEM((2 * CORES,) + grid3 + (chip_rows, unit_count), BF16),
            pltpu.VMEM((2, plane_rows, shared_count), F32),
            pltpu.VMEM((2, plane_rows, shared_count), F32),
            pltpu.VMEM(grid3 + (chip_rows, depth), BF16),
            [pltpu.VMEM(grid3 + (chip_rows, columns), BF16) for _, columns in parts],
            [landing_shapes(3, chip_rows, columns) for _, columns in parts],
            pltpu.VMEM((CORES, rows, half), F32),
            pltpu.VMEM((rows, half), F32),
            pltpu.SemaphoreType.DMA((inner_count,)),
            pltpu.SemaphoreType.DMA((inner_count,)),
            pltpu.SemaphoreType.DMA((copy_count,)),
            pltpu.SemaphoreType.DMA((copy_count,)),
            pltpu.SemaphoreType.DMA((load_count,)),
        ],
        compiler_params=pltpu.CompilerParams(
            collective_id=0, has_side_effects=True, vmem_limit_bytes=VMEM_LIMIT
        ),
        name="layer",
    )(
        cache_len,
        parents,
        route_experts,
        route_weights,
        hidden_in,
        node_latent,
        ffn_gain.reshape(1, -1),
        queries,
        jnp.swapaxes(cache, 1, 2),
        value_up,
        out_proj,
        expert_gate,
        expert_up,
        expert_down,
        jnp.swapaxes(shared_gate, 0, 1),
        jnp.swapaxes(shared_up, 0, 1),
        shared_down,
    )


def solution(mesh):
    both = ("group", "ingroup")
    in_specs = (
        P(both, None),
        P(both, None, None),
        P(both, None),
        P(both, None, None),
        P(both),
        P(both, None),
        P("ingroup", None, None),
        P("ingroup", None),
        P(),
        P(both, None),
        P(both, None),
        P(both, None, None),
        P(both, None, None),
        P(both, None, None),
        P(None, "ingroup"),
        P(None, "ingroup"),
        P("ingroup", None),
    )
    return jax.shard_map(
        local, mesh=mesh, in_specs=in_specs, out_specs=P(both, None), check_vma=False
    )
```

```python
import functools

import jax
import jax.numpy as jnp
from jax import lax
from jax.experimental import pallas as pl
from jax.experimental.pallas import tpu as pltpu
from jax.sharding import PartitionSpec as P

MESH = pl.DeviceIdType.MESH
F32 = jnp.float32
BF16 = jnp.bfloat16
SCALE_QK = 192.0 ** (-0.5)
NORM_EPS = 1e-06
RING = 4
CORES = 2
LANES = 128
VMEM_LIMIT = 62 * 2**20
AXES = ("z", "x", "y")
GATHER_ORDERS = (("x", "y", "z"), ("y", "z", "x"), ("z", "x", "y"))
SCATTER_ORDERS = (("z", "x", "y"), ("x", "y", "z"), ("y", "z", "x"))
PLANE_ORDERS = (("x", "y"), ("y", "x"))


def column_parts(width, count):
    tiles = width // LANES
    sizes = [tiles // count + (1 if k < tiles % count else 0) for k in range(count)]
    parts, start = [], 0
    for size in sizes:
        parts.append((start * LANES, size * LANES))
        start += size
    return tuple(parts)


def my_position():
    group, inner = lax.axis_index("group"), lax.axis_index("ingroup")
    return {
        "z": lax.div(group, CORES),
        "core": lax.rem(group, CORES),
        "x": lax.div(inner, RING),
        "y": lax.rem(inner, RING),
    }


def device_at(pos):
    return (pos["z"] * CORES + pos["core"], pos["x"] * RING + pos["y"])


def moved(pos, axis, by):
    other = dict(pos)
    other[axis] = lax.rem(pos[axis] + (by % RING), RING)
    return other


def sibling_of(pos):
    other = dict(pos)
    other["core"] = 1 - pos["core"]
    return other


class Copies:
    def __init__(self, send_sems, recv_sems):
        self.send_sems, self.recv_sems, self.started = send_sems, recv_sems, []

    def start(self, src, dst, device):
        slot = len(self.started)
        copy = pltpu.make_async_remote_copy(
            src_ref=src,
            dst_ref=dst,
            send_sem=self.send_sems.at[slot],
            recv_sem=self.recv_sems.at[slot],
            device_id=device,
            device_id_type=MESH,
        )
        copy.start()
        self.started.append(copy)
        return copy

    def finish(self):
        for copy in self.started:
            copy.wait_send()


OFFSETS = (0, 1, -1, 2)
FACING = (0, 2, 1, 3)
NEXT, BEFORE, FAR = 1, 2, 3
WHOLE, OTHERS = (0, RING), (1, RING - 1)


def view_index(axes, chosen, split_axis, half, columns):
    index = []
    for axis in axes:
        at = chosen[axis]
        if isinstance(at, tuple):
            start, size = at
            if axis == split_axis and half is not None:
                start, size = start + half * (size // 2), size // 2
            index.append(pl.ds(start, size))
        else:
            index.append(at)
    index.append(slice(None))
    if split_axis is None and half is not None:
        low = (columns // LANES + 1) // 2 * LANES
        index.append(pl.ds(0, low) if half == 0 else pl.ds(low, columns - low))
    else:
        index.append(slice(None))
    return tuple(index)


def over_blocks(axes, chosen, split_axis, half, body):
    spans = []
    for axis in axes:
        at = chosen[axis]
        start, size = at if isinstance(at, tuple) else (at, 1)
        if axis == split_axis and half is not None:
            start, size = start + half * (size // 2), size // 2
        spans.append((axis, start, size))
    steps = 1
    for _, _, size in spans:
        steps *= size

    def one(step, carry):
        places, rest = {}, step
        for axis, start, size in reversed(spans):
            if size == 1:
                places[axis] = start
            else:
                places[axis] = start + lax.rem(rest, size)
                rest = lax.div(rest, size)
        body(places)
        return carry

    if steps == 1:
        one(0, 0)
    else:
        lax.fori_loop(0, steps, one, 0)


class Ring:
    def __init__(self, copies, pos, ref, axes, axis, chosen, split_axis):
        self.copies, self.ref, self.axes, self.axis = copies, ref, axes, axis
        self.chosen, self.split_axis = chosen, split_axis
        self.columns = ref.shape[-1]
        self.plus, self.minus = device_at(moved(pos, axis, 1)), device_at(moved(pos, axis, -1))

    def block(self, place, half):
        chosen = dict(self.chosen)
        chosen[self.axis] = place
        return self.ref.at[view_index(self.axes, chosen, self.split_axis, half, self.columns)]


class Gather(Ring):
    def begin(self):
        start, block = self.copies.start, self.block
        self.first = [
            start(block(0, 0), block(BEFORE, 0), self.plus),
            start(block(0, 1), block(NEXT, 1), self.minus),
            start(block(0, 1), block(BEFORE, 1), self.plus),
            start(block(0, 0), block(NEXT, 0), self.minus),
        ]

    def relay(self):
        start, block = self.copies.start, self.block
        self.first[0].wait_recv()
        self.far = [start(block(BEFORE, 0), block(FAR, 0), self.plus)]
        self.first[1].wait_recv()
        self.far.append(start(block(NEXT, 1), block(FAR, 1), self.minus))

    def wait_near(self):
        self.first[2].wait_recv()
        self.first[3].wait_recv()

    def wait_far(self):
        self.far[0].wait_recv()
        self.far[1].wait_recv()


class Scatter(Ring):
    def land(self, landing):
        self.later = tuple(a for a in self.axes if isinstance(self.chosen.get(a), tuple))
        self.landing_axes, self.landing = landing
        self.relayed, self.from_before, self.from_next = self.landing
        return self

    def landed(self, ref, half):
        return ref.at[
            view_index(self.landing_axes, self.chosen, self.split_axis, half, self.columns)
        ]

    def send_far(self):
        start = self.copies.start
        self.far = [
            start(self.block(FAR, 0), self.landed(self.relayed, 0), self.plus),
            start(self.block(FAR, 1), self.landed(self.relayed, 1), self.minus),
        ]

    def send_near(self):
        start = self.copies.start
        self.near = [
            start(self.block(NEXT, 1), self.landed(self.from_before, 1), self.plus),
            start(self.block(BEFORE, 0), self.landed(self.from_next, 0), self.minus),
        ]

    def add_into(self, place, half, refs):
        tail = view_index((), {}, self.split_axis, half, self.columns)

        def slab(places):
            both = dict(self.chosen)
            both.update(places)
            both[self.axis] = place
            block = tuple(both[axis] for axis in self.axes) + tail
            land = tuple(both[axis] for axis in self.landing_axes) + tail
            total = self.ref[block].astype(F32)
            for ref in refs:
                total += ref[land].astype(F32)
            self.ref[block] = total.astype(BF16)

        over_blocks(self.later, self.chosen, self.split_axis, half, slab)

    def relay(self):
        start = self.copies.start
        self.far[0].wait_recv()
        self.add_into(NEXT, 0, [self.relayed])
        self.near.append(start(self.block(NEXT, 0), self.landed(self.from_before, 0), self.plus))
        self.far[1].wait_recv()
        self.add_into(BEFORE, 1, [self.relayed])
        self.near.append(start(self.block(BEFORE, 1), self.landed(self.from_next, 1), self.minus))

    def wait_near(self):
        for copy in self.near:
            copy.wait_recv()

    def finish(self):
        self.wait_near()
        self.add_into(0, None, [self.from_before, self.from_next])

    def finish_last(self):
        self.wait_near()
        total = self.ref[(0,) * len(self.axes)].astype(F32)
        return total + self.from_before[...].astype(F32) + self.from_next[...].astype(F32)


class Scatters:
    def __init__(self, copies, pos, axes, ref, order, landing):
        first, rest = order[0], order[1:]

        def ring(phase, chosen):
            later = [axis for axis in order[phase + 1 :] if isinstance(chosen[axis], tuple)]
            even = [axis for axis in later if chosen[axis][1] % 2 == 0]
            landing_axes = tuple(axis for axis in axes if axis in order[phase + 1 :])
            one = Scatter(
                copies, pos, ref, axes, order[phase], chosen, even[-1] if even else None
            )
            return one.land((landing_axes, landing[phase]))

        whole = {axis: WHOLE for axis in rest}
        self.portion = ring(0, {**whole, rest[0]: OTHERS})
        self.remainder = ring(0, {**whole, rest[0]: 0})
        self.second = ring(1, {first: 0, **{axis: WHOLE for axis in rest[1:]}})
        self.third = ring(2, {first: 0, rest[0]: 0}) if len(rest) > 1 else None
        self.last = self.third or self.second


def landing_shapes(axis_count, rows, columns):
    shapes = []
    for phase in range(axis_count):
        lead = (RING,) * (axis_count - 1 - phase)
        shapes += [pltpu.VMEM(lead + (rows, columns), BF16)] * 3
    return shapes


def by_phase(refs):
    return [refs[3 * k : 3 * k + 3] for k in range(len(refs) // 3)]


def landing_shapes(axis_count, rows, columns):
    shapes = []
    for phase in range(axis_count):
        lead = (RING,) * (axis_count - 1 - phase)
        shapes += [pltpu.VMEM(lead + (rows, columns), BF16)] * 3
    return shapes


def by_phase(refs):
    return [refs[3 * k : 3 * k + 3] for k in range(len(refs) // 3)]


def attention_kernel(
    latent_ref,
    value_up_ref,
    out_proj_hbm,
    hidden_ref,
    gain_ref,
    attended_ref,
    normed_ref,
    latents,
    proj,
    head_out,
    residual,
    hidden_away,
    squares,
    squares_in,
    part_refs,
    landing_refs,
    send_sems,
    recv_sems,
    local_sem,
):
    pos = my_position()
    core, group, inner = pos["core"], lax.axis_index("group"), lax.axis_index("ingroup")
    sibling = device_at(sibling_of(pos))
    rows = hidden_ref.shape[0]
    half = normed_ref.shape[1]
    model_width = hidden_ref.shape[1]
    inner_count = latent_ref.shape[0]
    head_count, latent_width, value_width = value_up_ref.shape
    mine = pl.ds(pl.multiple_of(core * half, LANES), half)
    other = pl.ds(pl.multiple_of((1 - core) * half, LANES), half)
    load_proj = pltpu.make_async_copy(out_proj_hbm.at[:, mine], proj, local_sem)
    load_proj.start()
    peers = [lax.rem(inner + step, inner_count) for step in range(1, inner_count)]
    greet([(group, peer) for peer in peers] + [sibling])
    copies = Copies(send_sems, recv_sems)

    arrivals = [
        copies.start(latent_ref.at[peer], latents.at[inner], (group, peer)) for peer in peers
    ]
    latents[inner] = latent_ref[inner]
    hidden_away[...] = hidden_ref[:, other].astype(F32)
    hidden_in_copy = copies.start(hidden_away, residual.at[core], sibling)
    residual[core] = hidden_ref[:, mine].astype(F32)
    for copy in arrivals:
        copy.wait_recv()

    stacked = latents[...].reshape(inner_count * head_count * rows, latent_width)
    for head in range(head_count):
        product = jnp.dot(stacked, value_up_ref[head], preferred_element_type=F32)
        product = product.reshape(inner_count, head_count, rows, value_width)[:, head]
        head_out[:, core, :, head * value_width : (head + 1) * value_width] = product.astype(
            BF16
        ).astype(F32)
    heads_copy = copies.start(head_out.at[:, core], head_out.at[:, core], sibling)
    load_proj.wait()
    heads_copy.wait_recv()
    heads = head_out[...].reshape(
        inner_count * CORES * rows, head_count * value_width
    ).astype(BF16)

    parts = column_parts(half, len(PLANE_ORDERS))
    scatters = []
    for (start, columns), ref, landing, order in zip(
        parts, part_refs, landing_refs, PLANE_ORDERS
    ):
        partial = jnp.dot(heads, proj[:, start : start + columns], preferred_element_type=F32)
        ref[...] = partial.astype(BF16).reshape(ref.shape)
        scatter = Scatter(copies, pos, ("x", "y"), ref, order, by_phase(landing))
        scatter.begin(0)
        scatter.send_far()
        scatter.send_near()
        scatters.append(scatter)
    for scatter in scatters:
        scatter.relay()
    for scatter in scatters:
        scatter.finish()
        scatter.begin(1)
        scatter.send_far()
        scatter.send_near()
    for scatter in scatters:
        scatter.relay()
    hidden_in_copy.wait_recv()
    square_sum = jnp.zeros((CORES * rows, 1), F32)
    for (start, columns), scatter in zip(parts, scatters):
        total = scatter.last.finish_last()
        total += residual[:, :, start : start + columns].reshape(CORES * rows, columns)
        attended = total.astype(BF16)
        attended_ref[:, start : start + columns] = attended
        wide = attended.astype(F32)
        square_sum += jnp.sum(wide * wide, axis=1, keepdims=True)
    squares[...] = jnp.broadcast_to(square_sum, squares.shape)
    squares_copy = copies.start(squares, squares_in, sibling)
    squares_copy.wait_recv()
    mean_square = (square_sum + squares_in[:, :1]) / model_width
    scale = lax.rsqrt(mean_square + NORM_EPS)
    normed_ref[...] = (attended_ref[...].astype(F32) * scale * gain_ref[:, mine]).astype(BF16)
    copies.finish()


def nt_dot(left, right):
    return lax.dot_general(left, right, (((1,), (1,)), ((), ())), preferred_element_type=F32)


def nn_dot(left, right):
    return jnp.dot(left, right, preferred_element_type=F32)


def silu(value):
    return value / (1.0 + jnp.exp(-value))


def visible_from(parents):
    count = parents.shape[-1]
    above = lax.broadcasted_iota(jnp.int32, (count, count), 0)
    below = lax.broadcasted_iota(jnp.int32, (count, count), 1)
    reach = ((above == parents) | (above == below)).astype(F32)
    hops = 1
    while hops < count - 1:
        reach = (nn_dot(reach.astype(BF16), reach.astype(BF16)) > 0.5).astype(F32)
        hops *= 2
    return reach.astype(BF16)


def routing_lanes(experts, weights, expert_count):
    rows, top = experts.shape
    lane = lax.rem(lax.broadcasted_iota(jnp.int32, (rows, LANES), 1), expert_count)
    total = jnp.zeros((rows, LANES), F32)
    for k in range(top):
        total += jnp.where(lane == experts[:, k : k + 1], weights[:, k : k + 1], 0.0)
    return total


def in_three(values, expert_count):
    high = values.astype(BF16).astype(F32)
    middle = (values - high).astype(BF16).astype(F32)
    low = values - high - middle
    lane = lax.broadcasted_iota(jnp.int32, values.shape, 1)
    terms = jnp.where(
        lane < expert_count,
        high,
        jnp.where(lane < 2 * expert_count, middle, jnp.where(lane < 3 * expert_count, low, 0.0)),
    )
    return terms.astype(BF16)


def layer_kernel(
    cache_len_ref,
    parents_ref,
    experts_ref,
    weights_ref,
    hidden_ref,
    node_ref,
    gain_ref,
    queries_hbm,
    cache_hbm,
    value_up_hbm,
    out_proj_hbm,
    gate_hbm,
    up_hbm,
    down_hbm,
    shared_gate_hbm,
    shared_up_hbm,
    shared_down_hbm,
    out_ref,
    queries,
    cache,
    value_up,
    proj,
    latent_out,
    latents,
    head_out,
    residual,
    hidden_away,
    squares,
    squares_in,
    attended_rows,
    plane_refs,
    plane_landing,
    row_refs,
    inner_weights,
    shared_weights,
    down_weights,
    row_scale,
    sums,
    sums_out,
    sums_in,
    shared_sums,
    shared_in,
    hidden,
    part_refs,
    landing_refs,
    final,
    final_in,
    send_sems,
    recv_sems,
    local_sems,
):
    pos = my_position()
    core, group, inner = pos["core"], lax.axis_index("group"), lax.axis_index("ingroup")
    sibling = device_at(sibling_of(pos))
    rows, model_width = hidden_ref.shape
    half = model_width // CORES
    chip_rows = CORES * rows
    plane_rows = RING * RING * chip_rows
    inner_count, _, latent_width = latents.shape
    head_count, _, value_width = value_up.shape
    all_heads, cached = queries.shape[1], cache.shape[1]
    unit_count = gate_hbm.shape[2]
    shared_count = shared_gate_hbm.shape[0]
    expert_count = RING * CORES * RING
    depth = CORES * unit_count + shared_count
    mine = pl.ds(pl.multiple_of(core * half, LANES), half)
    other = pl.ds(pl.multiple_of((1 - core) * half, LANES), half)
    own_units = pl.ds(pl.multiple_of(core * unit_count, unit_count), unit_count)
    shared_units = pl.ds(CORES * unit_count, shared_count)

    loads = []

    def load(src, dst):
        copy = pltpu.make_async_copy(src, dst, local_sems.at[len(loads)])
        copy.start()
        loads.append(copy)
        return copy

    first_loads = [load(queries_hbm, queries), load(cache_hbm.at[0], cache)]
    head_loads = [load(value_up_hbm, value_up), load(out_proj_hbm.at[:, mine], proj)]

    peers = [lax.rem(inner + step, inner_count) for step in range(1, inner_count)]
    z_neighbours = [device_at(moved(pos, "z", by)) for by in (1, -1)]
    partners = [(group, peer) for peer in peers] + z_neighbours + [sibling]
    barrier = pltpu.get_barrier_semaphore()
    for partner in partners:
        pl.semaphore_signal(barrier, inc=1, device_id=partner, device_id_type=MESH)

    routing = routing_lanes(experts_ref[...], weights_ref[...], expert_count)
    hidden_away[:, :half] = hidden_ref[:, other].astype(F32)
    hidden_away[:, half:] = routing
    residual[core, :, :half] = hidden_ref[:, mine].astype(F32)
    residual[core, :, half:] = routing

    reach = visible_from(parents_ref[...])
    node_keys = node_ref[...]
    chunk_heads = all_heads // 2
    chunk_rows = chunk_heads * rows
    chunk_peers = inner_count // 2
    row = lax.broadcasted_iota(jnp.int32, (chunk_rows, rows), 0)
    lane = lax.broadcasted_iota(jnp.int32, (chunk_rows, rows), 1)
    node_of = (lax.div(row, chunk_heads) == lane).astype(F32).astype(BF16)
    seen = nt_dot(node_of, reach) > 0.5
    to_row = lax.broadcasted_iota(jnp.int32, (chunk_rows, chunk_rows), 0)
    from_row = lax.broadcasted_iota(jnp.int32, (chunk_rows, chunk_rows), 1)
    head_major = (
        (from_row == lax.rem(to_row, rows) * chunk_heads + lax.div(to_row, rows))
        .astype(F32)
        .astype(BF16)
    )
    for copy in first_loads:
        copy.wait()

    for chunk in range(2):
        query = queries[:, chunk * chunk_heads : (chunk + 1) * chunk_heads, :]
        query = query.reshape(chunk_rows, query.shape[-1])
        scores = nn_dot(query, cache[...]) * SCALE_QK
        live = lax.broadcasted_iota(jnp.int32, scores.shape, 1) < cache_len_ref[0]
        scores = jnp.where(live, scores, -jnp.inf)
        node_scores = jnp.where(seen, nt_dot(query, node_keys) * SCALE_QK, -jnp.inf)
        highest = jnp.maximum(
            jnp.max(scores, axis=1, keepdims=True), jnp.max(node_scores, axis=1, keepdims=True)
        )
        scores = jnp.exp(scores - highest)
        node_scores = jnp.exp(node_scores - highest)
        total = jnp.sum(scores, axis=1, keepdims=True) + jnp.sum(
            node_scores, axis=1, keepdims=True
        )
        share = 1.0 / total
        latent = nt_dot((scores * share).astype(BF16), cache[:latent_width, :])
        latent += nn_dot((node_scores * share).astype(BF16), node_keys[:, :latent_width])
        latent = nn_dot(head_major, latent.astype(BF16)).astype(BF16)
        latent_out[chunk * chunk_peers : (chunk + 1) * chunk_peers] = latent.reshape(
            chunk_peers, head_count * rows, latent_width
        )
    pl.semaphore_wait(barrier, len(partners))
    copies = Copies(send_sems, recv_sems)
    arrivals = []
    for place_x, place_y in sorted(
        ((i, j) for i in range(RING) for j in range(RING) if i or j), reverse=True
    ):
        peer = moved(moved(pos, "x", OFFSETS[place_x]), "y", OFFSETS[place_y])
        src = latent_out.at[peer["x"] * RING + peer["y"]]
        dst = latents.at[FACING[place_x] * RING + FACING[place_y]]
        arrivals.append(copies.start(src, dst, device_at(peer)))
    hidden_copy = copies.start(hidden_away, residual.at[core], sibling)
    late_loads = [
        load(gate_hbm.at[0, mine, :], inner_weights.at[2 * core]),
        load(up_hbm.at[0, mine, :], inner_weights.at[2 * core + 1]),
        load(shared_gate_hbm.at[:, mine], shared_weights.at[0]),
        load(shared_up_hbm.at[:, mine], shared_weights.at[1]),
        load(down_hbm.at[0, :, mine], down_weights.at[own_units, :]),
        load(shared_down_hbm.at[:, mine], down_weights.at[shared_units, :]),
    ]

    latents[0] = latent_out[inner]
    for copy in arrivals:
        copy.wait_recv()

    for copy in head_loads:
        copy.wait()
    stacked = latents[...].reshape(inner_count * head_count * rows, latent_width)
    for head in range(head_count):
        product = nn_dot(stacked, value_up[head])
        product = product.reshape(inner_count, head_count, rows, value_width)[:, head]
        head_out[:, core, :, head * value_width : (head + 1) * value_width] = product.astype(
            BF16
        ).astype(F32)
    heads_copy = copies.start(head_out.at[:, core], head_out.at[:, core], sibling)
    heads_copy.wait_recv()
    weight_copies = [
        copies.start(gate_hbm.at[0, other, :], inner_weights.at[2 * core], sibling),
        copies.start(up_hbm.at[0, other, :], inner_weights.at[2 * core + 1], sibling),
        copies.start(down_hbm.at[0, :, other], down_weights.at[own_units, :], sibling),
    ]
    heads = head_out[...].reshape(plane_rows, head_count * value_width).astype(BF16)

    plane_parts = column_parts(half, len(PLANE_ORDERS))
    scatters = []
    for (start, columns), ref, landing, order in zip(
        plane_parts, plane_refs, plane_landing, PLANE_ORDERS
    ):
        partial = nn_dot(heads, proj[:, start : start + columns])
        ref[...] = partial.astype(BF16).reshape(ref.shape)
        scatter = Scatters(copies, pos, ("x", "y"), ref, order, by_phase(landing))
        scatter.portion.send_far()
        scatter.portion.send_near()
        scatters.append(scatter)
    for scatter in scatters:
        scatter.portion.relay()
        scatter.remainder.send_far()
        scatter.remainder.send_near()
    for scatter in scatters:
        scatter.portion.finish()
        scatter.second.send_far()
        scatter.second.send_near()
    for scatter in scatters:
        scatter.remainder.relay()
    for scatter in scatters:
        scatter.second.relay()
    for scatter in scatters:
        scatter.remainder.finish()
    hidden_copy.wait_recv()
    square_sum = jnp.zeros((chip_rows, 1), F32)
    for (start, columns), scatter in zip(plane_parts, scatters):
        total = scatter.last.finish_last()
        total += residual[:, :, start : start + columns].reshape(chip_rows, columns)
        attended = total.astype(BF16)
        attended_rows[:, start : start + columns] = attended
        wide = attended.astype(F32)
        square_sum += jnp.sum(wide * wide, axis=1, keepdims=True)
    squares[...] = jnp.broadcast_to(square_sum, squares.shape)
    squares_copy = copies.start(squares, squares_in, sibling)
    squares_copy.wait_recv()
    mean_square = (square_sum + squares_in[:, :1]) / model_width
    scale = lax.rsqrt(mean_square + NORM_EPS)
    normed = (attended_rows[...].astype(F32) * scale * gain_ref[:, mine]).astype(BF16)

    parts = column_parts(half, len(GATHER_ORDERS))
    for (start, columns), ref in zip(parts, row_refs):
        ref[0, 0, 0, :, :columns] = normed[:, start : start + columns]
    weighed = parts[1][1]
    row_refs[1][0, 0, 0, :, weighed:] = in_three(
        residual[:, :, half:].reshape(chip_rows, LANES), expert_count
    )

    def gather_ring(ref, order, phase, ranges):
        chosen = {axis: 0 for axis in AXES}
        chosen.update(zip(order, ranges))
        return Gather(copies, pos, ref, AXES, order[phase], chosen, order[0] if phase else None)

    rings = [
        (
            gather_ring(ref, order, 0, ()),
            gather_ring(ref, order, 1, (WHOLE,)),
            gather_ring(ref, order, 2, (WHOLE, 0)),
            gather_ring(ref, order, 2, (WHOLE, OTHERS)),
        )
        for ref, order in zip(row_refs, GATHER_ORDERS)
    ]

    def multiply(which_part, places):
        start, columns = parts[which_part]
        ref = row_refs[which_part]
        chosen = {axis: WHOLE for axis in AXES}
        chosen[GATHER_ORDERS[which_part][-1]] = places
        index = view_index(AXES, chosen, None, None, columns)
        spans = tuple(chosen[axis][1] for axis in AXES)
        count = places[1] * plane_rows

        def one(which, carry):
            block = ref[index[:-1] + (slice(0, columns),)].reshape(count, columns)
            product = nn_dot(block, inner_weights[which, start : start + columns, :])
            at = (which,) + index
            sums[at] = sums[at] + product.reshape(spans + (chip_rows, unit_count))
            return carry

        lax.fori_loop(0, 2 * CORES, one, 0)

    for ring in rings:
        ring[0].begin()

    def prepare(places):
        at = tuple(places[axis] for axis in AXES)
        for which in range(2 * CORES):
            sums[(which,) + at] = jnp.zeros((chip_rows, unit_count), F32)
        hidden[at + (slice(None), slice(CORES * unit_count, depth))] = jnp.zeros(
            (chip_rows, shared_count), BF16
        )

    over_blocks(AXES, {axis: WHOLE for axis in AXES}, None, None, prepare)
    for ring in rings:
        ring[0].relay()
    for ring in rings:
        ring[0].wait_near()
        ring[0].wait_far()
        ring[1].begin()
    for ring in rings:
        ring[2].begin()
    for ring in rings:
        ring[1].relay()
    for copy in late_loads:
        copy.wait()
    for ring in rings:
        ring[1].wait_near()
        ring[1].wait_far()
        ring[3].begin()
    for ring in rings:
        ring[2].relay()
    for copy in weight_copies:
        copy.wait_recv()
    for k in range(len(rings)):
        multiply(k, (0, 1))
    for ring in rings:
        ring[3].relay()
    for k, ring in enumerate(rings):
        ring[2].wait_near()
        ring[3].wait_near()
        multiply(k, (NEXT, 2))

    def narrow(ranges):
        chosen = dict(zip(AXES, ranges))

        def one(places):
            at = tuple(places[axis] for axis in AXES)
            for which in range(2 * CORES):
                sums_out[(which,) + at] = sums[(which,) + at].astype(BF16)

        over_blocks(AXES, chosen, None, None, one)
        index = (slice(None),) + view_index(AXES, chosen, None, None, unit_count)
        return copies.start(sums_out.at[index], sums_in.at[index], sibling)

    near, far = (0, FAR), (FAR, 1)
    regions = [((z, 1), near, near) for z in range(FAR)]
    regions += [(far, WHOLE, WHOLE), (near, far, WHOLE), (near, near, far)]
    exchanges = [narrow(region) for region in regions[:FAR]]
    for k, ring in enumerate(rings):
        ring[2].wait_far()
        ring[3].wait_far()
        multiply(k, far)
    exchanges += [narrow(region) for region in regions[FAR:]]
    for which in range(2):
        total = jnp.zeros((plane_rows, shared_count), F32)
        for (start, columns), ref in zip(parts, row_refs):
            total += nt_dot(
                ref[0, :, :, :, :columns].reshape(plane_rows, columns),
                shared_weights[which, :, start : start + columns],
            )
        shared_sums[which] = total
    shared_copy = copies.start(shared_sums, shared_in, sibling)
    picks_from = lax.broadcasted_iota(jnp.int32, (LANES, CORES * LANES), 0)
    picks_to = lax.div(lax.broadcasted_iota(jnp.int32, (LANES, CORES * LANES), 1), LANES)
    chosen = (pos["z"] * CORES + picks_to) * RING + pos["x"]
    picks = ((lax.rem(picks_from, expert_count) == chosen).astype(F32)).astype(BF16)
    for z in range(RING):
        terms = row_refs[1][z, :, :, :, weighed:].reshape(plane_rows, LANES)
        row_scale[z] = nn_dot(terms, picks).reshape(RING, RING, chip_rows, CORES * LANES)
    for region, exchange in zip(regions, exchanges):
        exchange.wait_recv()

        def activate(places):
            at = tuple(places[axis] for axis in AXES)
            for which in range(CORES):
                gate, up = (
                    sums[(2 * which + k,) + at] + sums_in[(2 * which + k,) + at].astype(F32)
                    for k in (0, 1)
                )
                lanes = slice(which * LANES, (which + 1) * LANES)
                scale = row_scale[at + (slice(None), lanes)]
                scale = jnp.concatenate([scale] * (unit_count // LANES), axis=1)
                value = (silu(gate) * up * scale).astype(BF16)
                units = slice(which * unit_count, (which + 1) * unit_count)
                hidden[at + (slice(None), units)] = value

        over_blocks(AXES, dict(zip(AXES, region)), None, None, activate)
    shared_copy.wait_recv()
    shared_gate_part, shared_up_part = (shared_sums[k] + shared_in[k] for k in (0, 1))
    shared_hidden = (silu(shared_gate_part) * shared_up_part).astype(BF16)
    hidden[0, :, :, :, CORES * unit_count :] = shared_hidden.reshape(
        RING, RING, chip_rows, shared_count
    )

    scatters = [
        Scatters(copies, pos, AXES, ref, order, by_phase(landing))
        for ref, order, landing in zip(part_refs, SCATTER_ORDERS, landing_refs)
    ]

    def project(which_part, places):
        start, columns = parts[which_part]
        chosen = {axis: WHOLE for axis in AXES}
        chosen[SCATTER_ORDERS[which_part][0]] = places
        index = view_index(AXES, chosen, None, None, columns)
        spans = tuple(chosen[axis][1] for axis in AXES)
        product = nn_dot(
            hidden[index].reshape(places[1] * plane_rows, depth),
            down_weights[:, start : start + columns],
        )
        part_refs[which_part][index] = product.astype(BF16).reshape(
            spans + (chip_rows, columns)
        )

    for k, scatter in enumerate(scatters):
        project(k, far)
        scatter.portion.send_far()
    for k, scatter in enumerate(scatters):
        project(k, (NEXT, 1))
        project(k, (BEFORE, 1))
        scatter.portion.send_near()
    for k in range(len(scatters)):
        project(k, (0, 1))
    for scatter in scatters:
        scatter.portion.relay()
    for scatter in scatters:
        scatter.remainder.send_far()
        scatter.remainder.send_near()
    for scatter in scatters:
        scatter.portion.finish()
        scatter.second.send_far()
        scatter.second.send_near()
    for scatter in scatters:
        scatter.remainder.relay()
    for scatter in scatters:
        scatter.second.relay()
    for scatter in scatters:
        scatter.remainder.finish()
        scatter.second.finish()
        scatter.third.send_far()
        scatter.third.send_near()
    for scatter in scatters:
        scatter.third.relay()
    for (start, columns), scatter in zip(parts, scatters):
        total = scatter.last.finish_last() + attended_rows[:, start : start + columns].astype(F32)
        final[:, :, start : start + columns] = total.reshape(CORES, rows, columns)
    final_copy = copies.start(final.at[1 - core], final_in, sibling)
    out_ref[:, mine] = final[core].astype(BF16)
    final_copy.wait_recv()
    out_ref[:, other] = final_in[...].astype(BF16)
    copies.finish()


def local(
    hidden_in,
    queries,
    node_latent,
    cache,
    cache_len,
    parents,
    value_up,
    out_proj,
    ffn_gain,
    route_experts,
    route_weights,
    expert_gate,
    expert_up,
    expert_down,
    shared_gate,
    shared_up,
    shared_down,
):
    rows, model_width = hidden_in.shape
    half = model_width // CORES
    chip_rows = CORES * rows
    inner_count = lax.axis_size("ingroup")
    head_count, latent_width, value_width = value_up.shape
    proj_rows = out_proj.shape[0]
    unit_count = expert_gate.shape[2]
    shared_count = shared_gate.shape[1]
    plane_rows = RING * RING * chip_rows
    depth = CORES * unit_count + shared_count
    plane_parts = column_parts(half, len(PLANE_ORDERS))
    parts = column_parts(half, len(GATHER_ORDERS))
    gathered = [columns + (LANES if k == 1 else 0) for k, (_, columns) in enumerate(parts)]
    grid3 = (RING, RING, RING)
    vmem = pl.BlockSpec(memory_space=pltpu.VMEM)
    smem = pl.BlockSpec(memory_space=pltpu.SMEM)
    hbm = pl.BlockSpec(memory_space=pl.ANY)
    copy_count = inner_count - 1 + 6 * (2 * 3 + 3 * 4 * 2) + 6 + 3 + 5
    load_count = 10
    return pl.pallas_call(
        layer_kernel,
        out_shape=jax.ShapeDtypeStruct((rows, model_width), BF16),
        in_specs=[smem] + [vmem] * 6 + [hbm] * 10,
        out_specs=vmem,
        scratch_shapes=[
            pltpu.VMEM(queries.shape, BF16),
            pltpu.VMEM((cache.shape[2], cache.shape[1]), BF16),
            pltpu.VMEM(value_up.shape, BF16),
            pltpu.VMEM((proj_rows, half), BF16),
            pltpu.VMEM((inner_count, head_count * rows, latent_width), BF16),
            pltpu.VMEM((inner_count, head_count * rows, latent_width), BF16),
            pltpu.VMEM((inner_count, CORES, rows, proj_rows), F32),
            pltpu.VMEM((CORES, rows, half + LANES), F32),
            pltpu.VMEM((rows, half + LANES), F32),
            pltpu.VMEM((chip_rows, LANES), F32),
            pltpu.VMEM((chip_rows, LANES), F32),
            pltpu.VMEM((chip_rows, half), BF16),
            [pltpu.VMEM((RING, RING, chip_rows, columns), BF16) for _, columns in plane_parts],
            [landing_shapes(2, chip_rows, columns) for _, columns in plane_parts],
            [pltpu.VMEM(grid3 + (chip_rows, columns), BF16) for columns in gathered],
            pltpu.VMEM((2 * CORES, half, unit_count), BF16),
            pltpu.VMEM((2, shared_count, half), BF16),
            pltpu.VMEM((depth, half), BF16),
            pltpu.VMEM(grid3 + (chip_rows, CORES * LANES), F32),
            pltpu.VMEM((2 * CORES,) + grid3 + (chip_rows, unit_count), F32),
            pltpu.VMEM((2 * CORES,) + grid3 + (chip_rows, unit_count), BF16),
            pltpu.VMEM((2 * CORES,) + grid3 + (chip_rows, unit_count), BF16),
            pltpu.VMEM((2, plane_rows, shared_count), F32),
            pltpu.VMEM((2, plane_rows, shared_count), F32),
            pltpu.VMEM(grid3 + (chip_rows, depth), BF16),
            [pltpu.VMEM(grid3 + (chip_rows, columns), BF16) for _, columns in parts],
            [landing_shapes(3, chip_rows, columns) for _, columns in parts],
            pltpu.VMEM((CORES, rows, half), F32),
            pltpu.VMEM((rows, half), F32),
            pltpu.SemaphoreType.DMA((copy_count,)),
            pltpu.SemaphoreType.DMA((copy_count,)),
            pltpu.SemaphoreType.DMA((load_count,)),
        ],
        compiler_params=pltpu.CompilerParams(
            collective_id=0, has_side_effects=True, vmem_limit_bytes=VMEM_LIMIT
        ),
        name="layer",
    )(
        cache_len,
        parents,
        route_experts,
        route_weights,
        hidden_in,
        node_latent,
        ffn_gain.reshape(1, -1),
        queries,
        jnp.swapaxes(cache, 1, 2),
        value_up,
        out_proj,
        expert_gate,
        expert_up,
        expert_down,
        jnp.swapaxes(shared_gate, 0, 1),
        jnp.swapaxes(shared_up, 0, 1),
        shared_down,
    )


def solution(mesh):
    both = ("group", "ingroup")
    in_specs = (
        P(both, None),
        P(both, None, None),
        P(both, None),
        P(both, None, None),
        P(both),
        P(both, None),
        P("ingroup", None, None),
        P("ingroup", None),
        P(),
        P(both, None),
        P(both, None),
        P(both, None, None),
        P(both, None, None),
        P(both, None, None),
        P(None, "ingroup"),
        P(None, "ingroup"),
        P("ingroup", None),
    )
    return jax.shard_map(
        local, mesh=mesh, in_specs=in_specs, out_specs=P(both, None), check_vma=False
    )
```

```python
import functools

import jax
import jax.numpy as jnp
from jax import lax
from jax.experimental import pallas as pl
from jax.experimental.pallas import tpu as pltpu
from jax.sharding import PartitionSpec as P

MESH = pl.DeviceIdType.MESH
F32 = jnp.float32
BF16 = jnp.bfloat16
SCALE_QK = 192.0 ** (-0.5)
NORM_EPS = 1e-06
RING = 4
CORES = 2
LANES = 128
VMEM_LIMIT = 62 * 2**20
AXES = ("z", "x", "y")
GATHER_ORDERS = (("x", "y", "z"), ("y", "z", "x"), ("z", "x", "y"))
SCATTER_ORDERS = (("z", "x", "y"), ("x", "y", "z"), ("y", "z", "x"))
PLANE_ORDERS = (("x", "y"), ("y", "x"))


def column_parts(width, count):
    tiles = width // LANES
    sizes = [tiles // count + (1 if k < tiles % count else 0) for k in range(count)]
    parts, start = [], 0
    for size in sizes:
        parts.append((start * LANES, size * LANES))
        start += size
    return tuple(parts)


def my_position():
    group, inner = lax.axis_index("group"), lax.axis_index("ingroup")
    return {
        "z": lax.div(group, CORES),
        "core": lax.rem(group, CORES),
        "x": lax.div(inner, RING),
        "y": lax.rem(inner, RING),
    }


def device_at(pos):
    return (pos["z"] * CORES + pos["core"], pos["x"] * RING + pos["y"])


def moved(pos, axis, by):
    other = dict(pos)
    other[axis] = lax.rem(pos[axis] + (by % RING), RING)
    return other


def sibling_of(pos):
    other = dict(pos)
    other["core"] = 1 - pos["core"]
    return other


class Copies:
    def __init__(self, send_sems, recv_sems):
        self.send_sems, self.recv_sems, self.started = send_sems, recv_sems, []

    def start(self, src, dst, device):
        slot = len(self.started)
        copy = pltpu.make_async_remote_copy(
            src_ref=src,
            dst_ref=dst,
            send_sem=self.send_sems.at[slot],
            recv_sem=self.recv_sems.at[slot],
            device_id=device,
            device_id_type=MESH,
        )
        copy.start()
        self.started.append(copy)
        return copy

    def finish(self):
        for copy in self.started:
            copy.wait_send()


OFFSETS = (0, 1, -1, 2)
FACING = (0, 2, 1, 3)
NEXT, BEFORE, FAR = 1, 2, 3
WHOLE, OTHERS = (0, RING), (1, RING - 1)


def view_index(axes, chosen, split_axis, half, columns):
    index = []
    for axis in axes:
        at = chosen[axis]
        if isinstance(at, tuple):
            start, size = at
            if axis == split_axis and half is not None:
                start, size = start + half * (size // 2), size // 2
            index.append(pl.ds(start, size))
        else:
            index.append(at)
    index.append(slice(None))
    if split_axis is None and half is not None:
        low = (columns // LANES + 1) // 2 * LANES
        index.append(pl.ds(0, low) if half == 0 else pl.ds(low, columns - low))
    else:
        index.append(slice(None))
    return tuple(index)


def over_blocks(axes, chosen, split_axis, half, body):
    spans = []
    for axis in axes:
        at = chosen[axis]
        start, size = at if isinstance(at, tuple) else (at, 1)
        if axis == split_axis and half is not None:
            start, size = start + half * (size // 2), size // 2
        spans.append((axis, start, size))
    steps = 1
    for _, _, size in spans:
        steps *= size

    def one(step, carry):
        places, rest = {}, step
        for axis, start, size in reversed(spans):
            if size == 1:
                places[axis] = start
            else:
                places[axis] = start + lax.rem(rest, size)
                rest = lax.div(rest, size)
        body(places)
        return carry

    if steps == 1:
        one(0, 0)
    else:
        lax.fori_loop(0, steps, one, 0)


class Ring:
    def __init__(self, copies, pos, ref, axes, axis, chosen, split_axis):
        self.copies, self.ref, self.axes, self.axis = copies, ref, axes, axis
        self.chosen, self.split_axis = chosen, split_axis
        self.columns = ref.shape[-1]
        self.plus, self.minus = device_at(moved(pos, axis, 1)), device_at(moved(pos, axis, -1))
        self.across = device_at(moved(pos, axis, 2))

    def block(self, place, half):
        chosen = dict(self.chosen)
        chosen[self.axis] = place
        return self.ref.at[view_index(self.axes, chosen, self.split_axis, half, self.columns)]


class Gather(Ring):
    def begin(self):
        start, block = self.copies.start, self.block
        self.first = [
            start(block(0, 0), block(BEFORE, 0), self.plus),
            start(block(0, 1), block(NEXT, 1), self.minus),
            start(block(0, 1), block(BEFORE, 1), self.plus),
            start(block(0, 0), block(NEXT, 0), self.minus),
        ]

    def relay(self):
        start, block = self.copies.start, self.block
        self.first[0].wait_recv()
        self.far = [start(block(BEFORE, 0), block(FAR, 0), self.plus)]
        self.first[1].wait_recv()
        self.far.append(start(block(NEXT, 1), block(FAR, 1), self.minus))

    def send_direct(self):
        start, block = self.copies.start, self.block
        self.direct = [
            start(block(0, None), block(FAR, None), self.across),
            start(block(0, None), block(BEFORE, None), self.plus),
            start(block(0, None), block(NEXT, None), self.minus),
        ]

    def wait_direct(self):
        for copy in self.direct:
            copy.wait_recv()

    def wait_near(self):
        self.first[2].wait_recv()
        self.first[3].wait_recv()

    def wait_far(self):
        self.far[0].wait_recv()
        self.far[1].wait_recv()


class Scatter(Ring):
    def land(self, landing):
        self.later = tuple(a for a in self.axes if isinstance(self.chosen.get(a), tuple))
        self.landing_axes, self.landing = landing
        self.relayed, self.from_before, self.from_next = self.landing
        return self

    def landed(self, ref, half):
        return ref.at[
            view_index(self.landing_axes, self.chosen, self.split_axis, half, self.columns)
        ]

    def send_far(self):
        start = self.copies.start
        self.far = [
            start(self.block(FAR, 0), self.landed(self.relayed, 0), self.plus),
            start(self.block(FAR, 1), self.landed(self.relayed, 1), self.minus),
        ]

    def send_near(self):
        start = self.copies.start
        self.near = [
            start(self.block(NEXT, 1), self.landed(self.from_before, 1), self.plus),
            start(self.block(BEFORE, 0), self.landed(self.from_next, 0), self.minus),
        ]

    def add_into(self, place, half, refs):
        tail = view_index((), {}, self.split_axis, half, self.columns)

        def slab(places):
            both = dict(self.chosen)
            both.update(places)
            both[self.axis] = place
            block = tuple(both[axis] for axis in self.axes) + tail
            land = tuple(both[axis] for axis in self.landing_axes) + tail
            total = self.ref[block].astype(F32)
            for ref in refs:
                total += ref[land].astype(F32)
            self.ref[block] = total.astype(BF16)

        over_blocks(self.later, self.chosen, self.split_axis, half, slab)

    def relay(self):
        start = self.copies.start
        self.far[0].wait_recv()
        self.add_into(NEXT, 0, [self.relayed])
        self.near.append(start(self.block(NEXT, 0), self.landed(self.from_before, 0), self.plus))
        self.far[1].wait_recv()
        self.add_into(BEFORE, 1, [self.relayed])
        self.near.append(start(self.block(BEFORE, 1), self.landed(self.from_next, 1), self.minus))

    def wait_near(self):
        for copy in self.near:
            copy.wait_recv()

    def finish(self):
        self.wait_near()
        self.add_into(0, None, [self.from_before, self.from_next])

    def send_direct(self):
        start = self.copies.start
        self.direct = [
            start(self.block(FAR, None), self.landed(self.relayed, None), self.across),
            start(self.block(NEXT, None), self.landed(self.from_before, None), self.plus),
            start(self.block(BEFORE, None), self.landed(self.from_next, None), self.minus),
        ]

    def finish_direct(self):
        total = self.ref[(0,) * len(self.axes)].astype(F32)
        for copy, ref in zip(self.direct, self.landing):
            copy.wait_recv()
            total += ref[...].astype(F32)
        return total


class Scatters:
    def __init__(self, copies, pos, axes, ref, order, landing):
        first, rest = order[0], order[1:]

        def ring(phase, chosen):
            later = [axis for axis in order[phase + 1 :] if isinstance(chosen[axis], tuple)]
            even = [axis for axis in later if chosen[axis][1] % 2 == 0]
            landing_axes = tuple(axis for axis in axes if axis in order[phase + 1 :])
            one = Scatter(
                copies, pos, ref, axes, order[phase], chosen, even[-1] if even else None
            )
            return one.land((landing_axes, landing[phase]))

        whole = {axis: WHOLE for axis in rest}
        self.portion = ring(0, {**whole, rest[0]: OTHERS})
        self.remainder = ring(0, {**whole, rest[0]: 0})
        self.second = ring(1, {first: 0, **{axis: WHOLE for axis in rest[1:]}})
        self.third = ring(2, {first: 0, rest[0]: 0}) if len(rest) > 1 else None
        self.last = self.third or self.second


def landing_shapes(axis_count, rows, columns):
    shapes = []
    for phase in range(axis_count):
        lead = (RING,) * (axis_count - 1 - phase)
        shapes += [pltpu.VMEM(lead + (rows, columns), BF16)] * 3
    return shapes


def by_phase(refs):
    return [refs[3 * k : 3 * k + 3] for k in range(len(refs) // 3)]


def nt_dot(left, right):
    return lax.dot_general(left, right, (((1,), (1,)), ((), ())), preferred_element_type=F32)


def nn_dot(left, right):
    return jnp.dot(left, right, preferred_element_type=F32)


def silu(value):
    return value / (1.0 + jnp.exp(-value))


def visible_from(parents):
    count = parents.shape[-1]
    above = lax.broadcasted_iota(jnp.int32, (count, count), 0)
    below = lax.broadcasted_iota(jnp.int32, (count, count), 1)
    reach = ((above == parents) | (above == below)).astype(F32)
    hops = 1
    while hops < count - 1:
        reach = (nn_dot(reach.astype(BF16), reach.astype(BF16)) > 0.5).astype(F32)
        hops *= 2
    return reach.astype(BF16)


def routing_lanes(experts, weights, expert_count):
    rows, top = experts.shape
    lane = lax.rem(lax.broadcasted_iota(jnp.int32, (rows, LANES), 1), expert_count)
    total = jnp.zeros((rows, LANES), F32)
    for k in range(top):
        total += jnp.where(lane == experts[:, k : k + 1], weights[:, k : k + 1], 0.0)
    return total


def in_three(values, expert_count):
    high = values.astype(BF16).astype(F32)
    middle = (values - high).astype(BF16).astype(F32)
    low = values - high - middle
    lane = lax.broadcasted_iota(jnp.int32, values.shape, 1)
    terms = jnp.where(
        lane < expert_count,
        high,
        jnp.where(lane < 2 * expert_count, middle, jnp.where(lane < 3 * expert_count, low, 0.0)),
    )
    return terms.astype(BF16)


def layer_kernel(
    cache_len_ref,
    parents_ref,
    experts_ref,
    weights_ref,
    hidden_ref,
    node_ref,
    gain_ref,
    queries_hbm,
    cache_hbm,
    value_up_hbm,
    out_proj_hbm,
    gate_hbm,
    up_hbm,
    down_hbm,
    shared_gate_hbm,
    shared_up_hbm,
    shared_down_hbm,
    out_ref,
    queries,
    cache,
    value_up,
    proj,
    latent_out,
    latents,
    head_out,
    residual,
    hidden_away,
    squares,
    squares_in,
    attended_rows,
    plane_refs,
    plane_landing,
    row_refs,
    inner_weights,
    shared_weights,
    down_weights,
    row_scale,
    sums,
    sums_out,
    sums_in,
    shared_sums,
    shared_in,
    hidden,
    part_refs,
    landing_refs,
    final,
    final_in,
    send_sems,
    recv_sems,
    local_sems,
):
    pos = my_position()
    core, group, inner = pos["core"], lax.axis_index("group"), lax.axis_index("ingroup")
    sibling = device_at(sibling_of(pos))
    rows, model_width = hidden_ref.shape
    half = model_width // CORES
    chip_rows = CORES * rows
    plane_rows = RING * RING * chip_rows
    inner_count, _, latent_width = latents.shape
    head_count, _, value_width = value_up.shape
    all_heads, cached = queries.shape[1], cache.shape[1]
    unit_count = gate_hbm.shape[2]
    shared_count = shared_gate_hbm.shape[0]
    expert_count = RING * CORES * RING
    depth = CORES * unit_count + shared_count
    mine = pl.ds(pl.multiple_of(core * half, LANES), half)
    other = pl.ds(pl.multiple_of((1 - core) * half, LANES), half)
    own_units = pl.ds(pl.multiple_of(core * unit_count, unit_count), unit_count)
    shared_units = pl.ds(CORES * unit_count, shared_count)
    gates, ups = pl.ds(0, unit_count), pl.ds(unit_count, unit_count)

    loads = []

    def load(src, dst):
        copy = pltpu.make_async_copy(src, dst, local_sems.at[len(loads)])
        copy.start()
        loads.append(copy)
        return copy

    first_loads = [load(queries_hbm, queries), load(cache_hbm.at[0], cache)]
    head_loads = [load(value_up_hbm, value_up), load(out_proj_hbm.at[:, mine], proj)]

    peers = [lax.rem(inner + step, inner_count) for step in range(1, inner_count)]
    z_neighbours = [device_at(moved(pos, "z", by)) for by in (1, -1, 2)]
    partners = [(group, peer) for peer in peers] + z_neighbours + [sibling]
    barrier = pltpu.get_barrier_semaphore()
    for partner in partners:
        pl.semaphore_signal(barrier, inc=1, device_id=partner, device_id_type=MESH)

    routing = routing_lanes(experts_ref[...], weights_ref[...], expert_count)
    hidden_away[:, :half] = hidden_ref[:, other].astype(F32)
    hidden_away[:, half:] = routing
    residual[core, :, :half] = hidden_ref[:, mine].astype(F32)
    residual[core, :, half:] = routing

    reach = visible_from(parents_ref[...])
    node_keys = node_ref[...]
    chunk_heads = all_heads // 2
    chunk_rows = chunk_heads * rows
    chunk_peers = inner_count // 2
    row = lax.broadcasted_iota(jnp.int32, (chunk_rows, rows), 0)
    lane = lax.broadcasted_iota(jnp.int32, (chunk_rows, rows), 1)
    node_of = (lax.div(row, chunk_heads) == lane).astype(F32).astype(BF16)
    seen = nt_dot(node_of, reach) > 0.5
    to_row = lax.broadcasted_iota(jnp.int32, (chunk_rows, chunk_rows), 0)
    from_row = lax.broadcasted_iota(jnp.int32, (chunk_rows, chunk_rows), 1)
    head_major = (
        (from_row == lax.rem(to_row, rows) * chunk_heads + lax.div(to_row, rows))
        .astype(F32)
        .astype(BF16)
    )
    for copy in first_loads:
        copy.wait()

    for chunk in range(2):
        query = queries[:, chunk * chunk_heads : (chunk + 1) * chunk_heads, :]
        query = query.reshape(chunk_rows, query.shape[-1])
        scores = nn_dot(query, cache[...]) * SCALE_QK
        live = lax.broadcasted_iota(jnp.int32, scores.shape, 1) < cache_len_ref[0]
        scores = jnp.where(live, scores, -jnp.inf)
        node_scores = jnp.where(seen, nt_dot(query, node_keys) * SCALE_QK, -jnp.inf)
        highest = jnp.maximum(
            jnp.max(scores, axis=1, keepdims=True), jnp.max(node_scores, axis=1, keepdims=True)
        )
        scores = jnp.exp(scores - highest)
        node_scores = jnp.exp(node_scores - highest)
        total = jnp.sum(scores, axis=1, keepdims=True) + jnp.sum(
            node_scores, axis=1, keepdims=True
        )
        share = 1.0 / total
        latent = nt_dot((scores * share).astype(BF16), cache[:latent_width, :])
        latent += nn_dot((node_scores * share).astype(BF16), node_keys[:, :latent_width])
        latent = nn_dot(head_major, latent.astype(BF16)).astype(BF16)
        latent_out[chunk * chunk_peers : (chunk + 1) * chunk_peers] = latent.reshape(
            chunk_peers, head_count * rows, latent_width
        )
    pl.semaphore_wait(barrier, len(partners))
    copies = Copies(send_sems, recv_sems)
    arrivals = []
    for place_x, place_y in sorted(
        ((i, j) for i in range(RING) for j in range(RING) if i or j), reverse=True
    ):
        peer = moved(moved(pos, "x", OFFSETS[place_x]), "y", OFFSETS[place_y])
        src = latent_out.at[peer["x"] * RING + peer["y"]]
        dst = latents.at[FACING[place_x] * RING + FACING[place_y]]
        arrivals.append(copies.start(src, dst, device_at(peer)))
    hidden_copy = copies.start(hidden_away, residual.at[core], sibling)
    late_loads = [
        load(gate_hbm.at[0, mine, :], inner_weights.at[core, :, gates]),
        load(up_hbm.at[0, mine, :], inner_weights.at[core, :, ups]),
        load(shared_gate_hbm.at[:, mine], shared_weights.at[0]),
        load(shared_up_hbm.at[:, mine], shared_weights.at[1]),
        load(down_hbm.at[0, :, mine], down_weights.at[own_units, :]),
        load(shared_down_hbm.at[:, mine], down_weights.at[shared_units, :]),
    ]

    def prepare(places):
        at = tuple(places[axis] for axis in AXES)
        for which in range(CORES):
            sums[(which,) + at] = jnp.zeros((chip_rows, 2 * unit_count), F32)
        hidden[at + (slice(None), slice(CORES * unit_count, depth))] = jnp.zeros(
            (chip_rows, shared_count), BF16
        )

    over_blocks(AXES, {axis: WHOLE for axis in AXES}, None, None, prepare)
    latents[0] = latent_out[inner]
    for copy in arrivals:
        copy.wait_recv()

    for copy in head_loads:
        copy.wait()
    stacked = latents[...].reshape(inner_count * head_count * rows, latent_width)
    for head in range(head_count):
        product = nn_dot(stacked, value_up[head])
        product = product.reshape(inner_count, head_count, rows, value_width)[:, head]
        head_out[:, core, :, head * value_width : (head + 1) * value_width] = product.astype(
            BF16
        ).astype(F32)
    heads_copy = copies.start(head_out.at[:, core], head_out.at[:, core], sibling)
    heads_copy.wait_recv()
    weight_copies = [
        copies.start(gate_hbm.at[0, other, :], inner_weights.at[core, :, gates], sibling),
        copies.start(up_hbm.at[0, other, :], inner_weights.at[core, :, ups], sibling),
        copies.start(down_hbm.at[0, :, other], down_weights.at[own_units, :], sibling),
    ]
    heads = head_out[...].reshape(plane_rows, head_count * value_width).astype(BF16)

    plane_parts = column_parts(half, len(PLANE_ORDERS))
    scatters = []
    for (start, columns), ref, landing, order in zip(
        plane_parts, plane_refs, plane_landing, PLANE_ORDERS
    ):
        partial = nn_dot(heads, proj[:, start : start + columns])
        ref[...] = partial.astype(BF16).reshape(ref.shape)
        scatter = Scatters(copies, pos, ("x", "y"), ref, order, by_phase(landing))
        scatter.portion.send_far()
        scatter.portion.send_near()
        scatters.append(scatter)
    for scatter in scatters:
        scatter.portion.relay()
        scatter.remainder.send_far()
        scatter.remainder.send_near()
    for scatter in scatters:
        scatter.portion.finish()
        scatter.second.send_direct()
    for scatter in scatters:
        scatter.remainder.relay()
    for scatter in scatters:
        scatter.remainder.finish()
    hidden_copy.wait_recv()
    square_sum = jnp.zeros((chip_rows, 1), F32)
    for (start, columns), scatter in zip(plane_parts, scatters):
        total = scatter.last.finish_direct()
        total += residual[:, :, start : start + columns].reshape(chip_rows, columns)
        attended = total.astype(BF16)
        attended_rows[:, start : start + columns] = attended
        wide = attended.astype(F32)
        square_sum += jnp.sum(wide * wide, axis=1, keepdims=True)
    squares[...] = jnp.broadcast_to(square_sum, squares.shape)
    squares_copy = copies.start(squares, squares_in, sibling)
    squares_copy.wait_recv()
    mean_square = (square_sum + squares_in[:, :1]) / model_width
    scale = lax.rsqrt(mean_square + NORM_EPS)
    normed = (attended_rows[...].astype(F32) * scale * gain_ref[:, mine]).astype(BF16)

    parts = column_parts(half, len(GATHER_ORDERS))
    for (start, columns), ref in zip(parts, row_refs):
        ref[0, 0, 0, :, :columns] = normed[:, start : start + columns]
    weighed = parts[1][1]
    row_refs[1][0, 0, 0, :, weighed:] = in_three(
        residual[:, :, half:].reshape(chip_rows, LANES), expert_count
    )

    def gather_ring(ref, order, phase, ranges):
        chosen = {axis: 0 for axis in AXES}
        chosen.update(zip(order, ranges))
        return Gather(copies, pos, ref, AXES, order[phase], chosen, order[0] if phase else None)

    rings = [
        (
            gather_ring(ref, order, 0, ()),
            gather_ring(ref, order, 1, (WHOLE,)),
            gather_ring(ref, order, 2, (WHOLE, 0)),
            gather_ring(ref, order, 2, (WHOLE, OTHERS)),
        )
        for ref, order in zip(row_refs, GATHER_ORDERS)
    ]

    def multiply(which_part, places):
        start, columns = parts[which_part]
        ref = row_refs[which_part]
        chosen = {axis: WHOLE for axis in AXES}
        chosen[GATHER_ORDERS[which_part][-1]] = places
        index = view_index(AXES, chosen, None, None, columns)
        spans = tuple(chosen[axis][1] for axis in AXES)
        count = places[1] * plane_rows

        def one(which, carry):
            block = ref[index[:-1] + (slice(0, columns),)].reshape(count, columns)
            product = nn_dot(block, inner_weights[which, start : start + columns, :])
            at = (which,) + index
            sums[at] = sums[at] + product.reshape(spans + (chip_rows, 2 * unit_count))
            return carry

        lax.fori_loop(0, CORES, one, 0)

    for ring in rings:
        ring[0].send_direct()

    for ring in rings:
        ring[0].wait_direct()
        ring[1].begin()
    for ring in rings:
        ring[1].relay()
    for ring in rings:
        ring[2].begin()
    for copy in late_loads:
        copy.wait()
    for ring in rings:
        ring[1].wait_near()
        ring[1].wait_far()
        ring[3].begin()
    for ring in rings:
        ring[2].relay()
    for copy in weight_copies:
        copy.wait_recv()
    for k in range(len(rings)):
        multiply(k, (0, 1))
    for ring in rings:
        ring[3].relay()
    for k, ring in enumerate(rings):
        ring[2].wait_near()
        ring[3].wait_near()
        multiply(k, (NEXT, 2))

    def narrow(ranges):
        chosen = dict(zip(AXES, ranges))

        def one(places):
            at = tuple(places[axis] for axis in AXES)
            for which in range(CORES):
                sums_out[(which,) + at] = sums[(which,) + at].astype(BF16)

        over_blocks(AXES, chosen, None, None, one)
        index = (slice(None),) + view_index(AXES, chosen, None, None, unit_count)
        return copies.start(sums_out.at[index], sums_in.at[index], sibling)

    near, far = (0, FAR), (FAR, 1)
    regions = [((z, 1), near, near) for z in range(FAR)]
    regions += [(far, WHOLE, WHOLE), (near, far, WHOLE), (near, near, far)]
    exchanges = [narrow(region) for region in regions[:FAR]]
    for k, ring in enumerate(rings):
        ring[2].wait_far()
        ring[3].wait_far()
        multiply(k, far)
    exchanges += [narrow(region) for region in regions[FAR:]]
    for which in range(2):
        total = jnp.zeros((plane_rows, shared_count), F32)
        for (start, columns), ref in zip(parts, row_refs):
            total += nt_dot(
                ref[0, :, :, :, :columns].reshape(plane_rows, columns),
                shared_weights[which, :, start : start + columns],
            )
        shared_sums[which] = total
    shared_copy = copies.start(shared_sums, shared_in, sibling)
    picks_from = lax.broadcasted_iota(jnp.int32, (LANES, CORES * LANES), 0)
    picks_to = lax.div(lax.broadcasted_iota(jnp.int32, (LANES, CORES * LANES), 1), LANES)
    chosen = (pos["z"] * CORES + picks_to) * RING + pos["x"]
    picks = ((lax.rem(picks_from, expert_count) == chosen).astype(F32)).astype(BF16)
    for z in range(RING):
        terms = row_refs[1][z, :, :, :, weighed:].reshape(plane_rows, LANES)
        row_scale[z] = nn_dot(terms, picks).reshape(RING, RING, chip_rows, CORES * LANES)
    for region, exchange in zip(regions, exchanges):
        exchange.wait_recv()

        def activate(places):
            at = tuple(places[axis] for axis in AXES)
            for which in range(CORES):
                both = sums[(which,) + at] + sums_in[(which,) + at].astype(F32)
                gate, up = both[:, :unit_count], both[:, unit_count:]
                lanes = slice(which * LANES, (which + 1) * LANES)
                scale = row_scale[at + (slice(None), lanes)]
                scale = jnp.concatenate([scale] * (unit_count // LANES), axis=1)
                value = (silu(gate) * up * scale).astype(BF16)
                units = slice(which * unit_count, (which + 1) * unit_count)
                hidden[at + (slice(None), units)] = value

        over_blocks(AXES, dict(zip(AXES, region)), None, None, activate)
    shared_copy.wait_recv()
    shared_gate_part, shared_up_part = (shared_sums[k] + shared_in[k] for k in (0, 1))
    shared_hidden = (silu(shared_gate_part) * shared_up_part).astype(BF16)
    hidden[0, :, :, :, CORES * unit_count :] = shared_hidden.reshape(
        RING, RING, chip_rows, shared_count
    )

    scatters = [
        Scatters(copies, pos, AXES, ref, order, by_phase(landing))
        for ref, order, landing in zip(part_refs, SCATTER_ORDERS, landing_refs)
    ]

    def project(which_part, places):
        start, columns = parts[which_part]
        chosen = {axis: WHOLE for axis in AXES}
        chosen[SCATTER_ORDERS[which_part][0]] = places
        index = view_index(AXES, chosen, None, None, columns)
        spans = tuple(chosen[axis][1] for axis in AXES)
        product = nn_dot(
            hidden[index].reshape(places[1] * plane_rows, depth),
            down_weights[:, start : start + columns],
        )
        part_refs[which_part][index] = product.astype(BF16).reshape(
            spans + (chip_rows, columns)
        )

    for k, scatter in enumerate(scatters):
        project(k, far)
        scatter.portion.send_far()
    for k, scatter in enumerate(scatters):
        project(k, (NEXT, 1))
        project(k, (BEFORE, 1))
        scatter.portion.send_near()
    for k in range(len(scatters)):
        project(k, (0, 1))
    for scatter in scatters:
        scatter.portion.relay()
    for scatter in scatters:
        scatter.remainder.send_far()
        scatter.remainder.send_near()
    for scatter in scatters:
        scatter.portion.finish()
        scatter.second.send_far()
        scatter.second.send_near()
    for scatter in scatters:
        scatter.remainder.relay()
    for scatter in scatters:
        scatter.second.relay()
    for scatter in scatters:
        scatter.remainder.finish()
        scatter.second.finish()
        scatter.third.send_direct()
    for (start, columns), scatter in zip(parts, scatters):
        total = scatter.last.finish_direct() + attended_rows[:, start : start + columns].astype(F32)
        final[:, :, start : start + columns] = total.reshape(CORES, rows, columns)
    final_copy = copies.start(final.at[1 - core], final_in, sibling)
    out_ref[:, mine] = final[core].astype(BF16)
    final_copy.wait_recv()
    out_ref[:, other] = final_in[...].astype(BF16)
    copies.finish()


def local(
    hidden_in,
    queries,
    node_latent,
    cache,
    cache_len,
    parents,
    value_up,
    out_proj,
    ffn_gain,
    route_experts,
    route_weights,
    expert_gate,
    expert_up,
    expert_down,
    shared_gate,
    shared_up,
    shared_down,
):
    rows, model_width = hidden_in.shape
    half = model_width // CORES
    chip_rows = CORES * rows
    inner_count = lax.axis_size("ingroup")
    head_count, latent_width, value_width = value_up.shape
    proj_rows = out_proj.shape[0]
    unit_count = expert_gate.shape[2]
    shared_count = shared_gate.shape[1]
    plane_rows = RING * RING * chip_rows
    depth = CORES * unit_count + shared_count
    plane_parts = column_parts(half, len(PLANE_ORDERS))
    parts = column_parts(half, len(GATHER_ORDERS))
    gathered = [columns + (LANES if k == 1 else 0) for k, (_, columns) in enumerate(parts)]
    grid3 = (RING, RING, RING)
    vmem = pl.BlockSpec(memory_space=pltpu.VMEM)
    smem = pl.BlockSpec(memory_space=pltpu.SMEM)
    hbm = pl.BlockSpec(memory_space=pl.ANY)
    copy_count = inner_count - 1 + 6 * (2 * 3 + 3 * 4 * 2) + 6 + 3 + 5
    load_count = 10
    return pl.pallas_call(
        layer_kernel,
        out_shape=jax.ShapeDtypeStruct((rows, model_width), BF16),
        in_specs=[smem] + [vmem] * 6 + [hbm] * 10,
        out_specs=vmem,
        scratch_shapes=[
            pltpu.VMEM(queries.shape, BF16),
            pltpu.VMEM((cache.shape[2], cache.shape[1]), BF16),
            pltpu.VMEM(value_up.shape, BF16),
            pltpu.VMEM((proj_rows, half), BF16),
            pltpu.VMEM((inner_count, head_count * rows, latent_width), BF16),
            pltpu.VMEM((inner_count, head_count * rows, latent_width), BF16),
            pltpu.VMEM((inner_count, CORES, rows, proj_rows), F32),
            pltpu.VMEM((CORES, rows, half + LANES), F32),
            pltpu.VMEM((rows, half + LANES), F32),
            pltpu.VMEM((chip_rows, LANES), F32),
            pltpu.VMEM((chip_rows, LANES), F32),
            pltpu.VMEM((chip_rows, half), BF16),
            [pltpu.VMEM((RING, RING, chip_rows, columns), BF16) for _, columns in plane_parts],
            [landing_shapes(2, chip_rows, columns) for _, columns in plane_parts],
            [pltpu.VMEM(grid3 + (chip_rows, columns), BF16) for columns in gathered],
            pltpu.VMEM((CORES, half, 2 * unit_count), BF16),
            pltpu.VMEM((2, shared_count, half), BF16),
            pltpu.VMEM((depth, half), BF16),
            pltpu.VMEM(grid3 + (chip_rows, CORES * LANES), F32),
            pltpu.VMEM((CORES,) + grid3 + (chip_rows, 2 * unit_count), F32),
            pltpu.VMEM((CORES,) + grid3 + (chip_rows, 2 * unit_count), BF16),
            pltpu.VMEM((CORES,) + grid3 + (chip_rows, 2 * unit_count), BF16),
            pltpu.VMEM((2, plane_rows, shared_count), F32),
            pltpu.VMEM((2, plane_rows, shared_count), F32),
            pltpu.VMEM(grid3 + (chip_rows, depth), BF16),
            [pltpu.VMEM(grid3 + (chip_rows, columns), BF16) for _, columns in parts],
            [landing_shapes(3, chip_rows, columns) for _, columns in parts],
            pltpu.VMEM((CORES, rows, half), F32),
            pltpu.VMEM((rows, half), F32),
            pltpu.SemaphoreType.DMA((copy_count,)),
            pltpu.SemaphoreType.DMA((copy_count,)),
            pltpu.SemaphoreType.DMA((load_count,)),
        ],
        compiler_params=pltpu.CompilerParams(
            collective_id=0, has_side_effects=True, vmem_limit_bytes=VMEM_LIMIT
        ),
        name="layer",
    )(
        cache_len,
        parents,
        route_experts,
        route_weights,
        hidden_in,
        node_latent,
        ffn_gain.reshape(1, -1),
        queries,
        jnp.swapaxes(cache, 1, 2),
        value_up,
        out_proj,
        expert_gate,
        expert_up,
        expert_down,
        jnp.swapaxes(shared_gate, 0, 1),
        jnp.swapaxes(shared_up, 0, 1),
        shared_down,
    )


def solution(mesh):
    both = ("group", "ingroup")
    in_specs = (
        P(both, None),
        P(both, None, None),
        P(both, None),
        P(both, None, None),
        P(both),
        P(both, None),
        P("ingroup", None, None),
        P("ingroup", None),
        P(),
        P(both, None),
        P(both, None),
        P(both, None, None),
        P(both, None, None),
        P(both, None, None),
        P(None, "ingroup"),
        P(None, "ingroup"),
        P("ingroup", None),
    )
    return jax.shard_map(
        local, mesh=mesh, in_specs=in_specs, out_specs=P(both, None), check_vma=False
    )
```

```python
import functools

import jax
import jax.numpy as jnp
from jax import lax
from jax.experimental import pallas as pl
from jax.experimental.pallas import tpu as pltpu
from jax.sharding import PartitionSpec as P

MESH = pl.DeviceIdType.MESH
F32 = jnp.float32
BF16 = jnp.bfloat16
SCALE_QK = 192.0 ** (-0.5)
NORM_EPS = 1e-06
RING = 4
CORES = 2
LANES = 128
SCALE_LANE = 96
VMEM_LIMIT = 62 * 2**20
AXES = ("z", "x", "y")
GATHER_ORDERS = (("x", "y", "z"), ("y", "z", "x"), ("z", "x", "y"))
TERMS_ORDER = ("z", "y", "x")
SCATTER_ORDERS = (("z", "x", "y"), ("x", "y", "z"), ("y", "z", "x"))
PLANE_ORDERS = (("x", "y"), ("y", "x"))


def column_parts(width, count):
    tiles = width // LANES
    sizes = [tiles // count + (1 if k < tiles % count else 0) for k in range(count)]
    parts, start = [], 0
    for size in sizes:
        parts.append((start * LANES, size * LANES))
        start += size
    return tuple(parts)


def my_position():
    group, inner = lax.axis_index("group"), lax.axis_index("ingroup")
    return {
        "z": lax.div(group, CORES),
        "core": lax.rem(group, CORES),
        "x": lax.div(inner, RING),
        "y": lax.rem(inner, RING),
    }


def device_at(pos):
    return (pos["z"] * CORES + pos["core"], pos["x"] * RING + pos["y"])


def moved(pos, axis, by):
    other = dict(pos)
    other[axis] = lax.rem(pos[axis] + (by % RING), RING)
    return other


def sibling_of(pos):
    other = dict(pos)
    other["core"] = 1 - pos["core"]
    return other


class Copies:
    def __init__(self, send_sems, recv_sems):
        self.send_sems, self.recv_sems, self.started = send_sems, recv_sems, []

    def start(self, src, dst, device):
        slot = len(self.started)
        copy = pltpu.make_async_remote_copy(
            src_ref=src,
            dst_ref=dst,
            send_sem=self.send_sems.at[slot],
            recv_sem=self.recv_sems.at[slot],
            device_id=device,
            device_id_type=MESH,
        )
        copy.start()
        self.started.append(copy)
        return copy

    def finish(self):
        for copy in self.started:
            copy.wait_send()


OFFSETS = (0, 1, -1, 2)
FACING = (0, 2, 1, 3)
NEXT, BEFORE, FAR = 1, 2, 3
WHOLE, OTHERS = (0, RING), (1, RING - 1)


def view_index(axes, chosen, split_axis, half, columns):
    index = []
    for axis in axes:
        at = chosen[axis]
        if isinstance(at, tuple):
            start, size = at
            if axis == split_axis and half is not None:
                start, size = start + half * (size // 2), size // 2
            index.append(pl.ds(start, size))
        else:
            index.append(at)
    index.append(slice(None))
    if split_axis is None and half is not None:
        low = (columns // LANES + 1) // 2 * LANES
        index.append(pl.ds(0, low) if half == 0 else pl.ds(low, columns - low))
    else:
        index.append(slice(None))
    return tuple(index)


def over_blocks(axes, chosen, split_axis, half, body):
    spans = []
    for axis in axes:
        at = chosen[axis]
        start, size = at if isinstance(at, tuple) else (at, 1)
        if axis == split_axis and half is not None:
            start, size = start + half * (size // 2), size // 2
        spans.append((axis, start, size))
    steps = 1
    for _, _, size in spans:
        steps *= size

    def one(step, carry):
        places, rest = {}, step
        for axis, start, size in reversed(spans):
            if size == 1:
                places[axis] = start
            else:
                places[axis] = start + lax.rem(rest, size)
                rest = lax.div(rest, size)
        body(places)
        return carry

    if steps == 1:
        one(0, 0)
    else:
        lax.fori_loop(0, steps, one, 0)


class Ring:
    def __init__(self, copies, pos, ref, axes, axis, chosen, split_axis):
        self.copies, self.ref, self.axes, self.axis = copies, ref, axes, axis
        self.chosen, self.split_axis = chosen, split_axis
        self.columns = ref.shape[-1]
        self.plus, self.minus = device_at(moved(pos, axis, 1)), device_at(moved(pos, axis, -1))
        self.across = device_at(moved(pos, axis, 2))

    def block(self, place, half):
        chosen = dict(self.chosen)
        chosen[self.axis] = place
        return self.ref.at[view_index(self.axes, chosen, self.split_axis, half, self.columns)]


class Gather(Ring):
    def begin(self):
        start, block = self.copies.start, self.block
        self.first = [
            start(block(0, 0), block(BEFORE, 0), self.plus),
            start(block(0, 1), block(NEXT, 1), self.minus),
            start(block(0, 1), block(BEFORE, 1), self.plus),
            start(block(0, 0), block(NEXT, 0), self.minus),
        ]

    def relay(self):
        start, block = self.copies.start, self.block
        self.first[0].wait_recv()
        self.far = [start(block(BEFORE, 0), block(FAR, 0), self.plus)]
        self.first[1].wait_recv()
        self.far.append(start(block(NEXT, 1), block(FAR, 1), self.minus))

    def send_direct(self):
        start, block = self.copies.start, self.block
        self.direct = [
            start(block(0, None), block(FAR, None), self.across),
            start(block(0, None), block(BEFORE, None), self.plus),
            start(block(0, None), block(NEXT, None), self.minus),
        ]

    def wait_direct(self):
        for copy in self.direct:
            copy.wait_recv()

    def wait_near(self):
        self.first[2].wait_recv()
        self.first[3].wait_recv()

    def wait_far(self):
        self.far[0].wait_recv()
        self.far[1].wait_recv()


class Scatter(Ring):
    def land(self, landing):
        self.later = tuple(a for a in self.axes if isinstance(self.chosen.get(a), tuple))
        self.landing_axes, self.landing = landing
        self.relayed, self.from_before, self.from_next = self.landing
        return self

    def landed(self, ref, half):
        return ref.at[
            view_index(self.landing_axes, self.chosen, self.split_axis, half, self.columns)
        ]

    def send_far(self):
        start = self.copies.start
        self.far = [
            start(self.block(FAR, 0), self.landed(self.relayed, 0), self.plus),
            start(self.block(FAR, 1), self.landed(self.relayed, 1), self.minus),
        ]

    def send_near(self):
        start = self.copies.start
        self.near = [
            start(self.block(NEXT, 1), self.landed(self.from_before, 1), self.plus),
            start(self.block(BEFORE, 0), self.landed(self.from_next, 0), self.minus),
        ]

    def add_into(self, place, half, refs):
        tail = view_index((), {}, self.split_axis, half, self.columns)

        def slab(places):
            both = dict(self.chosen)
            both.update(places)
            both[self.axis] = place
            block = tuple(both[axis] for axis in self.axes) + tail
            land = tuple(both[axis] for axis in self.landing_axes) + tail
            total = self.ref[block].astype(F32)
            for ref in refs:
                total += ref[land].astype(F32)
            self.ref[block] = total.astype(BF16)

        over_blocks(self.later, self.chosen, self.split_axis, half, slab)

    def relay(self):
        start = self.copies.start
        self.far[0].wait_recv()
        self.add_into(NEXT, 0, [self.relayed])
        self.near.append(start(self.block(NEXT, 0), self.landed(self.from_before, 0), self.plus))
        self.far[1].wait_recv()
        self.add_into(BEFORE, 1, [self.relayed])
        self.near.append(start(self.block(BEFORE, 1), self.landed(self.from_next, 1), self.minus))

    def wait_near(self):
        for copy in self.near:
            copy.wait_recv()

    def finish(self):
        self.wait_near()
        self.add_into(0, None, [self.from_before, self.from_next])

    def send_direct(self):
        start = self.copies.start
        self.direct = [
            start(self.block(FAR, None), self.landed(self.relayed, None), self.across),
            start(self.block(NEXT, None), self.landed(self.from_before, None), self.plus),
            start(self.block(BEFORE, None), self.landed(self.from_next, None), self.minus),
        ]

    def finish_direct(self):
        total = self.ref[(0,) * len(self.axes)].astype(F32)
        for copy, ref in zip(self.direct, self.landing):
            copy.wait_recv()
            total += ref[...].astype(F32)
        return total


class Scatters:
    def __init__(self, copies, pos, axes, ref, order, landing):
        first, rest = order[0], order[1:]

        def ring(phase, chosen):
            later = [axis for axis in order[phase + 1 :] if isinstance(chosen[axis], tuple)]
            even = [axis for axis in later if chosen[axis][1] % 2 == 0]
            landing_axes = tuple(axis for axis in axes if axis in order[phase + 1 :])
            one = Scatter(
                copies, pos, ref, axes, order[phase], chosen, even[-1] if even else None
            )
            return one.land((landing_axes, landing[phase]))

        whole = {axis: WHOLE for axis in rest}
        self.portion = ring(0, {**whole, rest[0]: OTHERS})
        self.remainder = ring(0, {**whole, rest[0]: 0})
        self.second = ring(1, {first: 0, **{axis: WHOLE for axis in rest[1:]}})
        self.third = ring(2, {first: 0, rest[0]: 0}) if len(rest) > 1 else None
        self.last = self.third or self.second


def landing_shapes(axis_count, rows, columns):
    shapes = []
    for phase in range(axis_count):
        lead = (RING,) * (axis_count - 1 - phase)
        shapes += [pltpu.VMEM(lead + (rows, columns), BF16)] * 3
    return shapes


def by_phase(refs):
    return [refs[3 * k : 3 * k + 3] for k in range(len(refs) // 3)]


def nt_dot(left, right):
    return lax.dot_general(left, right, (((1,), (1,)), ((), ())), preferred_element_type=F32)


def nn_dot(left, right):
    return jnp.dot(left, right, preferred_element_type=F32)


def silu(value):
    return value / (1.0 + jnp.exp(-value))


def visible_from(parents):
    count = parents.shape[-1]
    above = lax.broadcasted_iota(jnp.int32, (count, count), 0)
    below = lax.broadcasted_iota(jnp.int32, (count, count), 1)
    reach = ((above == parents) | (above == below)).astype(F32)
    hops = 1
    while hops < count - 1:
        reach = (nn_dot(reach.astype(BF16), reach.astype(BF16)) > 0.5).astype(F32)
        hops *= 2
    return reach.astype(BF16)


def routing_lanes(experts, weights, expert_count):
    rows, top = experts.shape
    lane = lax.rem(lax.broadcasted_iota(jnp.int32, (rows, LANES), 1), expert_count)
    total = jnp.zeros((rows, LANES), F32)
    for k in range(top):
        total += jnp.where(lane == experts[:, k : k + 1], weights[:, k : k + 1], 0.0)
    return total


def in_three(values, expert_count):
    high = values.astype(BF16).astype(F32)
    middle = (values - high).astype(BF16).astype(F32)
    low = values - high - middle
    lane = lax.broadcasted_iota(jnp.int32, values.shape, 1)
    terms = jnp.where(
        lane < expert_count,
        high,
        jnp.where(lane < 2 * expert_count, middle, jnp.where(lane < 3 * expert_count, low, 0.0)),
    )
    return terms.astype(BF16)


def layer_kernel(
    cache_len_ref,
    hidden_ref,
    node_ref,
    parents_hbm,
    experts_hbm,
    weights_hbm,
    gain_hbm,
    queries_hbm,
    cache_hbm,
    value_up_hbm,
    out_proj_hbm,
    gate_hbm,
    up_hbm,
    down_hbm,
    shared_gate_hbm,
    shared_up_hbm,
    shared_down_hbm,
    out_ref,
    parents_ref,
    experts_ref,
    weights_ref,
    gain_ref,
    queries,
    cache,
    value_up,
    proj,
    latent_out,
    latents,
    head_out,
    residual,
    hidden_away,
    squares,
    squares_in,
    attended_rows,
    plane_refs,
    plane_landing,
    row_refs,
    terms_ref,
    inner_weights,
    shared_weights,
    down_weights,
    row_scale,
    sums,
    sums_out,
    sums_in,
    shared_sums,
    shared_in,
    hidden,
    part_refs,
    landing_refs,
    final,
    final_in,
    send_sems,
    recv_sems,
    local_sems,
):
    pos = my_position()
    core, group, inner = pos["core"], lax.axis_index("group"), lax.axis_index("ingroup")
    sibling = device_at(sibling_of(pos))
    rows, model_width = hidden_ref.shape
    half = model_width // CORES
    chip_rows = CORES * rows
    plane_rows = RING * RING * chip_rows
    inner_count, _, latent_width = latents.shape
    head_count, _, value_width = value_up.shape
    all_heads, cached = queries.shape[1], cache.shape[1]
    unit_count = gate_hbm.shape[2]
    shared_count = shared_gate_hbm.shape[0]
    expert_count = RING * CORES * RING
    depth = CORES * unit_count + shared_count
    mine = pl.ds(pl.multiple_of(core * half, LANES), half)
    other = pl.ds(pl.multiple_of((1 - core) * half, LANES), half)
    own_units = pl.ds(pl.multiple_of(core * unit_count, unit_count), unit_count)
    shared_units = pl.ds(CORES * unit_count, shared_count)
    gates, ups = pl.ds(0, unit_count), pl.ds(unit_count, unit_count)

    loads = []

    def load(src, dst):
        copy = pltpu.make_async_copy(src, dst, local_sems.at[len(loads)])
        copy.start()
        loads.append(copy)
        return copy

    small_loads = [
        load(parents_hbm, parents_ref),
        load(experts_hbm, experts_ref),
        load(weights_hbm, weights_ref),
        load(gain_hbm.at[:, mine], gain_ref),
    ]
    first_loads = [load(queries_hbm, queries), load(cache_hbm.at[0], cache)]
    head_loads = [load(value_up_hbm, value_up), load(out_proj_hbm.at[:, mine], proj)]

    peers = [lax.rem(inner + step, inner_count) for step in range(1, inner_count)]
    z_neighbours = [device_at(moved(pos, "z", by)) for by in (1, -1, 2)]
    partners = [(group, peer) for peer in peers] + z_neighbours + [sibling]
    barrier = pltpu.get_barrier_semaphore()
    for partner in partners:
        pl.semaphore_signal(barrier, inc=1, device_id=partner, device_id_type=MESH)

    for copy in small_loads:
        copy.wait()
    routing = routing_lanes(experts_ref[...], weights_ref[...], expert_count)
    hidden_away[:, :half] = hidden_ref[:, other].astype(F32)
    hidden_away[:, half:] = routing
    residual[core, :, :half] = hidden_ref[:, mine].astype(F32)
    residual[core, :, half:] = routing

    reach = visible_from(parents_ref[...])
    node_keys = node_ref[...]
    chunk_heads = all_heads // 2
    chunk_rows = chunk_heads * rows
    chunk_peers = inner_count // 2
    row = lax.broadcasted_iota(jnp.int32, (chunk_rows, rows), 0)
    lane = lax.broadcasted_iota(jnp.int32, (chunk_rows, rows), 1)
    node_of = (lax.div(row, chunk_heads) == lane).astype(F32).astype(BF16)
    seen = nt_dot(node_of, reach) > 0.5
    to_row = lax.broadcasted_iota(jnp.int32, (chunk_rows, chunk_rows), 0)
    from_row = lax.broadcasted_iota(jnp.int32, (chunk_rows, chunk_rows), 1)
    head_major = (
        (from_row == lax.rem(to_row, rows) * chunk_heads + lax.div(to_row, rows))
        .astype(F32)
        .astype(BF16)
    )
    for copy in first_loads:
        copy.wait()

    for chunk in range(2):
        query = queries[:, chunk * chunk_heads : (chunk + 1) * chunk_heads, :]
        query = query.reshape(chunk_rows, query.shape[-1])
        scores = nn_dot(query, cache[...]) * SCALE_QK
        live = lax.broadcasted_iota(jnp.int32, scores.shape, 1) < cache_len_ref[0]
        scores = jnp.where(live, scores, -jnp.inf)
        node_scores = jnp.where(seen, nt_dot(query, node_keys) * SCALE_QK, -jnp.inf)
        highest = jnp.maximum(
            jnp.max(scores, axis=1, keepdims=True), jnp.max(node_scores, axis=1, keepdims=True)
        )
        scores = jnp.exp(scores - highest)
        node_scores = jnp.exp(node_scores - highest)
        total = jnp.sum(scores, axis=1, keepdims=True) + jnp.sum(
            node_scores, axis=1, keepdims=True
        )
        share = 1.0 / total
        latent = nt_dot((scores * share).astype(BF16), cache[:latent_width, :])
        latent += nn_dot((node_scores * share).astype(BF16), node_keys[:, :latent_width])
        latent = nn_dot(head_major, latent.astype(BF16)).astype(BF16)
        latent_out[chunk * chunk_peers : (chunk + 1) * chunk_peers] = latent.reshape(
            chunk_peers, head_count * rows, latent_width
        )
    pl.semaphore_wait(barrier, len(partners))
    copies = Copies(send_sems, recv_sems)
    arrivals = []
    for place_x, place_y in sorted(
        ((i, j) for i in range(RING) for j in range(RING) if i or j), reverse=True
    ):
        peer = moved(moved(pos, "x", OFFSETS[place_x]), "y", OFFSETS[place_y])
        src = latent_out.at[peer["x"] * RING + peer["y"]]
        dst = latents.at[FACING[place_x] * RING + FACING[place_y]]
        arrivals.append(copies.start(src, dst, device_at(peer)))
    hidden_copy = copies.start(hidden_away, residual.at[core], sibling)
    late_loads = [
        load(gate_hbm.at[0, mine, :], inner_weights.at[core, :, gates]),
        load(up_hbm.at[0, mine, :], inner_weights.at[core, :, ups]),
        load(shared_gate_hbm.at[:, mine], shared_weights.at[0]),
        load(shared_up_hbm.at[:, mine], shared_weights.at[1]),
        load(down_hbm.at[0, :, mine], down_weights.at[own_units, :]),
        load(shared_down_hbm.at[:, mine], down_weights.at[shared_units, :]),
    ]

    def prepare(places):
        at = tuple(places[axis] for axis in AXES)
        for which in range(CORES):
            sums[(which,) + at] = jnp.zeros((chip_rows, 2 * unit_count), F32)
        hidden[at + (slice(None), slice(CORES * unit_count, depth))] = jnp.zeros(
            (chip_rows, shared_count), BF16
        )

    over_blocks(AXES, {axis: WHOLE for axis in AXES}, None, None, prepare)
    latents[0] = latent_out[inner]
    for copy in arrivals:
        copy.wait_recv()

    for copy in head_loads:
        copy.wait()
    stacked = latents[...].reshape(inner_count * head_count * rows, latent_width)
    for head in range(head_count):
        product = nn_dot(stacked, value_up[head])
        product = product.reshape(inner_count, head_count, rows, value_width)[:, head]
        head_out[:, core, :, head * value_width : (head + 1) * value_width] = product.astype(
            BF16
        ).astype(F32)
    heads_copy = copies.start(head_out.at[:, core], head_out.at[:, core], sibling)
    heads_copy.wait_recv()
    weight_copies = [
        copies.start(gate_hbm.at[0, other, :], inner_weights.at[core, :, gates], sibling),
        copies.start(up_hbm.at[0, other, :], inner_weights.at[core, :, ups], sibling),
        copies.start(down_hbm.at[0, :, other], down_weights.at[own_units, :], sibling),
    ]
    heads = head_out[...].reshape(plane_rows, head_count * value_width).astype(BF16)

    plane_parts = column_parts(half, len(PLANE_ORDERS))
    scatters = []
    for (start, columns), ref, landing, order in zip(
        plane_parts, plane_refs, plane_landing, PLANE_ORDERS
    ):
        partial = nn_dot(heads, proj[:, start : start + columns])
        ref[...] = partial.astype(BF16).reshape(ref.shape)
        scatter = Scatters(copies, pos, ("x", "y"), ref, order, by_phase(landing))
        scatter.portion.send_far()
        scatter.portion.send_near()
        scatters.append(scatter)
    for scatter in scatters:
        scatter.portion.relay()
        scatter.remainder.send_far()
        scatter.remainder.send_near()
    for scatter in scatters:
        scatter.portion.finish()
        scatter.second.send_direct()
    for scatter in scatters:
        scatter.remainder.relay()
    for scatter in scatters:
        scatter.remainder.finish()
    hidden_copy.wait_recv()
    square_sum = jnp.zeros((chip_rows, 1), F32)
    for (start, columns), scatter in zip(plane_parts, scatters):
        total = scatter.last.finish_direct()
        total += residual[:, :, start : start + columns].reshape(chip_rows, columns)
        attended = total.astype(BF16)
        attended_rows[:, start : start + columns] = attended
        wide = attended.astype(F32)
        square_sum += jnp.sum(wide * wide, axis=1, keepdims=True)
    squares[...] = jnp.broadcast_to(square_sum, squares.shape)
    squares_copy = copies.start(squares, squares_in, sibling)
    parts = column_parts(half, len(GATHER_ORDERS))
    for (start, columns), ref in zip(parts, row_refs):
        span = slice(start, start + columns)
        scaled = attended_rows[:, span].astype(F32) * gain_ref[:, span]
        ref[0, 0, 0] = scaled.astype(BF16)

    def gather_ring(ref, order, phase, ranges):
        chosen = {axis: 0 for axis in AXES}
        chosen.update(zip(order, ranges))
        return Gather(copies, pos, ref, AXES, order[phase], chosen, order[0] if phase else None)

    rings = [
        (
            gather_ring(ref, order, 0, ()),
            gather_ring(ref, order, 1, (WHOLE,)),
            gather_ring(ref, order, 2, (WHOLE, 0)),
            gather_ring(ref, order, 2, (WHOLE, OTHERS)),
        )
        for ref, order in zip(row_refs, GATHER_ORDERS)
    ]
    terms_rings = [
        gather_ring(terms_ref, TERMS_ORDER, phase, (WHOLE,) * phase) for phase in range(3)
    ]

    def multiply(which_part, places):
        start, columns = parts[which_part]
        ref = row_refs[which_part]
        chosen = {axis: WHOLE for axis in AXES}
        chosen[GATHER_ORDERS[which_part][-1]] = places
        index = view_index(AXES, chosen, None, None, columns)
        spans = tuple(chosen[axis][1] for axis in AXES)
        count = places[1] * plane_rows

        def one(which, carry):
            block = ref[index[:-1] + (slice(0, columns),)].reshape(count, columns)
            product = nn_dot(block, inner_weights[which, start : start + columns, :])
            at = (which,) + index
            sums[at] = sums[at] + product.reshape(spans + (chip_rows, 2 * unit_count))
            return carry

        lax.fori_loop(0, CORES, one, 0)

    for ring in rings:
        ring[0].send_direct()
    squares_copy.wait_recv()
    mean_square = (square_sum + squares_in[:, :1]) / model_width
    scale = lax.rsqrt(mean_square + NORM_EPS)
    routing_terms = in_three(residual[:, :, half:].reshape(chip_rows, LANES), expert_count)
    lane = lax.broadcasted_iota(jnp.int32, (chip_rows, LANES), 1)
    scale_high = scale.astype(BF16).astype(F32)
    scale_middle = (scale - scale_high).astype(BF16).astype(F32)
    scale_terms = jnp.where(
        lane == SCALE_LANE,
        scale_high,
        jnp.where(lane == SCALE_LANE + 1, scale_middle, scale - scale_high - scale_middle),
    )
    is_scale = (lane >= SCALE_LANE) & (lane < SCALE_LANE + 3)
    terms_ref[0, 0, 0] = jnp.where(is_scale, scale_terms, routing_terms.astype(F32)).astype(BF16)
    terms_rings[0].send_direct()

    for ring in rings:
        ring[0].wait_direct()
        ring[1].begin()
    for ring in rings:
        ring[1].relay()
    for ring in rings:
        ring[2].begin()
    terms_rings[0].wait_direct()
    terms_rings[1].send_direct()
    for copy in late_loads:
        copy.wait()
    for ring in rings:
        ring[1].wait_near()
        ring[1].wait_far()
        ring[3].begin()
    for ring in rings:
        ring[2].relay()
    terms_rings[1].wait_direct()
    terms_rings[2].send_direct()
    for copy in weight_copies:
        copy.wait_recv()
    for k in range(len(rings)):
        multiply(k, (0, 1))
    for ring in rings:
        ring[3].relay()
    for k, ring in reversed(list(enumerate(rings))):
        ring[2].wait_near()
        ring[3].wait_near()
        multiply(k, (NEXT, 2))

    def narrow(ranges):
        chosen = dict(zip(AXES, ranges))

        def one(places):
            at = tuple(places[axis] for axis in AXES)
            for which in range(CORES):
                sums_out[(which,) + at] = sums[(which,) + at].astype(BF16)

        over_blocks(AXES, chosen, None, None, one)
        index = (slice(None),) + view_index(AXES, chosen, None, None, unit_count)
        return copies.start(sums_out.at[index], sums_in.at[index], sibling)

    near, far = (0, FAR), (FAR, 1)
    regions = [((z, 1), near, near) for z in range(FAR)]
    regions += [(far, WHOLE, WHOLE), (near, far, WHOLE), (near, near, far)]
    exchanges = [narrow(region) for region in regions[:FAR]]
    for k, ring in reversed(list(enumerate(rings))):
        ring[2].wait_far()
        ring[3].wait_far()
        multiply(k, far)
    exchanges += [narrow(region) for region in regions[FAR:]]
    for which in range(2):
        total = jnp.zeros((plane_rows, shared_count), F32)
        for (start, columns), ref in zip(parts, row_refs):
            total += nt_dot(
                ref[0, :, :, :, :columns].reshape(plane_rows, columns),
                shared_weights[which, :, start : start + columns],
            )
        shared_sums[which] = total
    shared_copy = copies.start(shared_sums, shared_in, sibling)
    terms_rings[2].wait_direct()
    picks_shape = (LANES, (CORES + 1) * LANES)
    picks_from = lax.broadcasted_iota(jnp.int32, picks_shape, 0)
    picks_to = lax.div(lax.broadcasted_iota(jnp.int32, picks_shape, 1), LANES)
    chosen_expert = (pos["z"] * CORES + picks_to) * RING + pos["x"]
    is_weight = (picks_from < SCALE_LANE) & (picks_to < CORES)
    picked = (is_weight & (lax.rem(picks_from, expert_count) == chosen_expert)) | (
        (picks_from >= SCALE_LANE) & (picks_to == CORES)
    )
    picks = picked.astype(F32).astype(BF16)
    for z in range(RING):
        terms = terms_ref[z].reshape(plane_rows, LANES)
        row_scale[z] = nn_dot(terms, picks).reshape(RING, RING, chip_rows, (CORES + 1) * LANES)
    for region, exchange in zip(regions, exchanges):
        exchange.wait_recv()

        def activate(places):
            at = tuple(places[axis] for axis in AXES)
            for which in range(CORES):
                both = sums[(which,) + at] + sums_in[(which,) + at].astype(F32)
                norm = row_scale[at + (slice(None), slice(CORES * LANES, (CORES + 1) * LANES))]
                both = both * jnp.concatenate([norm] * (2 * unit_count // LANES), axis=1)
                gate, up = both[:, :unit_count], both[:, unit_count:]
                lanes = slice(which * LANES, (which + 1) * LANES)
                scale = row_scale[at + (slice(None), lanes)]
                scale = jnp.concatenate([scale] * (unit_count // LANES), axis=1)
                value = (silu(gate) * up * scale).astype(BF16)
                units = slice(which * unit_count, (which + 1) * unit_count)
                hidden[at + (slice(None), units)] = value

        over_blocks(AXES, dict(zip(AXES, region)), None, None, activate)
    shared_copy.wait_recv()
    norm_lanes = slice(CORES * LANES, CORES * LANES + shared_count)
    norm = row_scale[0, :, :, :, norm_lanes].reshape(plane_rows, shared_count)
    shared_gate_part, shared_up_part = (
        (shared_sums[k] + shared_in[k]) * norm for k in (0, 1)
    )
    shared_hidden = (silu(shared_gate_part) * shared_up_part).astype(BF16)
    hidden[0, :, :, :, CORES * unit_count :] = shared_hidden.reshape(
        RING, RING, chip_rows, shared_count
    )

    scatters = [
        Scatters(copies, pos, AXES, ref, order, by_phase(landing))
        for ref, order, landing in zip(part_refs, SCATTER_ORDERS, landing_refs)
    ]

    def project(which_part, places):
        start, columns = parts[which_part]
        chosen = {axis: WHOLE for axis in AXES}
        chosen[SCATTER_ORDERS[which_part][0]] = places
        index = view_index(AXES, chosen, None, None, columns)
        spans = tuple(chosen[axis][1] for axis in AXES)
        product = nn_dot(
            hidden[index].reshape(places[1] * plane_rows, depth),
            down_weights[:, start : start + columns],
        )
        part_refs[which_part][index] = product.astype(BF16).reshape(
            spans + (chip_rows, columns)
        )

    for k, scatter in enumerate(scatters):
        project(k, far)
        scatter.portion.send_far()
    for k, scatter in enumerate(scatters):
        project(k, (NEXT, 1))
        project(k, (BEFORE, 1))
        scatter.portion.send_near()
    for k in range(len(scatters)):
        project(k, (0, 1))
    for scatter in scatters:
        scatter.portion.relay()
    for scatter in scatters:
        scatter.remainder.send_far()
        scatter.remainder.send_near()
    for scatter in scatters:
        scatter.portion.finish()
        scatter.second.send_far()
        scatter.second.send_near()
    for scatter in scatters:
        scatter.remainder.relay()
    for scatter in scatters:
        scatter.second.relay()
    for scatter in scatters:
        scatter.remainder.finish()
        scatter.second.finish()
        scatter.third.send_direct()
    for (start, columns), scatter in zip(parts, scatters):
        total = scatter.last.finish_direct() + attended_rows[:, start : start + columns].astype(F32)
        final[:, :, start : start + columns] = total.reshape(CORES, rows, columns)
    final_copy = copies.start(final.at[1 - core], final_in, sibling)
    out_ref[:, mine] = final[core].astype(BF16)
    final_copy.wait_recv()
    out_ref[:, other] = final_in[...].astype(BF16)
    copies.finish()


def local(
    hidden_in,
    queries,
    node_latent,
    cache,
    cache_len,
    parents,
    value_up,
    out_proj,
    ffn_gain,
    route_experts,
    route_weights,
    expert_gate,
    expert_up,
    expert_down,
    shared_gate,
    shared_up,
    shared_down,
):
    rows, model_width = hidden_in.shape
    half = model_width // CORES
    chip_rows = CORES * rows
    inner_count = lax.axis_size("ingroup")
    head_count, latent_width, value_width = value_up.shape
    proj_rows = out_proj.shape[0]
    unit_count = expert_gate.shape[2]
    shared_count = shared_gate.shape[1]
    plane_rows = RING * RING * chip_rows
    depth = CORES * unit_count + shared_count
    plane_parts = column_parts(half, len(PLANE_ORDERS))
    parts = column_parts(half, len(GATHER_ORDERS))
    grid3 = (RING, RING, RING)
    vmem = pl.BlockSpec(memory_space=pltpu.VMEM)
    smem = pl.BlockSpec(memory_space=pltpu.SMEM)
    hbm = pl.BlockSpec(memory_space=pl.ANY)
    copy_count = inner_count - 1 + 9 + 6 * (2 * 3 + 3 * 4 * 2) + 6 + 3 + 5
    load_count = 14
    return pl.pallas_call(
        layer_kernel,
        out_shape=jax.ShapeDtypeStruct((rows, model_width), BF16),
        in_specs=[smem] + [vmem] * 2 + [hbm] * 14,
        out_specs=vmem,
        scratch_shapes=[
            pltpu.VMEM(parents.shape, jnp.int32),
            pltpu.VMEM(route_experts.shape, jnp.int32),
            pltpu.VMEM(route_weights.shape, F32),
            pltpu.VMEM((1, half), F32),
            pltpu.VMEM(queries.shape, BF16),
            pltpu.VMEM((cache.shape[2], cache.shape[1]), BF16),
            pltpu.VMEM(value_up.shape, BF16),
            pltpu.VMEM((proj_rows, half), BF16),
            pltpu.VMEM((inner_count, head_count * rows, latent_width), BF16),
            pltpu.VMEM((inner_count, head_count * rows, latent_width), BF16),
            pltpu.VMEM((inner_count, CORES, rows, proj_rows), F32),
            pltpu.VMEM((CORES, rows, half + LANES), F32),
            pltpu.VMEM((rows, half + LANES), F32),
            pltpu.VMEM((chip_rows, LANES), F32),
            pltpu.VMEM((chip_rows, LANES), F32),
            pltpu.VMEM((chip_rows, half), BF16),
            [pltpu.VMEM((RING, RING, chip_rows, columns), BF16) for _, columns in plane_parts],
            [landing_shapes(2, chip_rows, columns) for _, columns in plane_parts],
            [pltpu.VMEM(grid3 + (chip_rows, columns), BF16) for _, columns in parts],
            pltpu.VMEM(grid3 + (chip_rows, LANES), BF16),
            pltpu.VMEM((CORES, half, 2 * unit_count), BF16),
            pltpu.VMEM((2, shared_count, half), BF16),
            pltpu.VMEM((depth, half), BF16),
            pltpu.VMEM(grid3 + (chip_rows, (CORES + 1) * LANES), F32),
            pltpu.VMEM((CORES,) + grid3 + (chip_rows, 2 * unit_count), F32),
            pltpu.VMEM((CORES,) + grid3 + (chip_rows, 2 * unit_count), BF16),
            pltpu.VMEM((CORES,) + grid3 + (chip_rows, 2 * unit_count), BF16),
            pltpu.VMEM((2, plane_rows, shared_count), F32),
            pltpu.VMEM((2, plane_rows, shared_count), F32),
            pltpu.VMEM(grid3 + (chip_rows, depth), BF16),
            [pltpu.VMEM(grid3 + (chip_rows, columns), BF16) for _, columns in parts],
            [landing_shapes(3, chip_rows, columns) for _, columns in parts],
            pltpu.VMEM((CORES, rows, half), F32),
            pltpu.VMEM((rows, half), F32),
            pltpu.SemaphoreType.DMA((copy_count,)),
            pltpu.SemaphoreType.DMA((copy_count,)),
            pltpu.SemaphoreType.DMA((load_count,)),
        ],
        compiler_params=pltpu.CompilerParams(
            collective_id=0, has_side_effects=True, vmem_limit_bytes=VMEM_LIMIT
        ),
        name="layer",
    )(
        cache_len,
        hidden_in,
        node_latent,
        parents,
        route_experts,
        route_weights,
        ffn_gain.reshape(1, -1),
        queries,
        jnp.swapaxes(cache, 1, 2),
        value_up,
        out_proj,
        expert_gate,
        expert_up,
        expert_down,
        jnp.swapaxes(shared_gate, 0, 1),
        jnp.swapaxes(shared_up, 0, 1),
        shared_down,
    )


def solution(mesh):
    both = ("group", "ingroup")
    in_specs = (
        P(both, None),
        P(both, None, None),
        P(both, None),
        P(both, None, None),
        P(both),
        P(both, None),
        P("ingroup", None, None),
        P("ingroup", None),
        P(),
        P(both, None),
        P(both, None),
        P(both, None, None),
        P(both, None, None),
        P(both, None, None),
        P(None, "ingroup"),
        P(None, "ingroup"),
        P("ingroup", None),
    )
    return jax.shard_map(
        local, mesh=mesh, in_specs=in_specs, out_specs=P(both, None), check_vma=False
    )
```

```python
import functools

import jax
import jax.numpy as jnp
from jax import lax
from jax.experimental import pallas as pl
from jax.experimental.pallas import tpu as pltpu
from jax.sharding import PartitionSpec as P

MESH = pl.DeviceIdType.MESH
F32 = jnp.float32
BF16 = jnp.bfloat16
SCALE_QK = 192.0 ** (-0.5)
NORM_EPS = 1e-06
RING = 4
CORES = 2
LANES = 128
SCALE_LANE = 96
VMEM_LIMIT = 62 * 2**20
AXES = ("z", "x", "y")
GATHER_ORDERS = (("x", "y", "z"), ("y", "z", "x"), ("z", "x", "y"))
TERMS_ORDER = ("z", "y", "x")
SCATTER_ORDERS = (("z", "x", "y"), ("x", "y", "z"), ("y", "z", "x"))
PLANE_ORDERS = (("x", "y"), ("y", "x"))


def column_parts(width, count):
    tiles = width // LANES
    sizes = [tiles // count + (1 if k < tiles % count else 0) for k in range(count)]
    parts, start = [], 0
    for size in sizes:
        parts.append((start * LANES, size * LANES))
        start += size
    return tuple(parts)


def my_position():
    group, inner = lax.axis_index("group"), lax.axis_index("ingroup")
    return {
        "z": lax.div(group, CORES),
        "core": lax.rem(group, CORES),
        "x": lax.div(inner, RING),
        "y": lax.rem(inner, RING),
    }


def device_at(pos):
    return (pos["z"] * CORES + pos["core"], pos["x"] * RING + pos["y"])


def moved(pos, axis, by):
    other = dict(pos)
    other[axis] = lax.rem(pos[axis] + (by % RING), RING)
    return other


def sibling_of(pos):
    other = dict(pos)
    other["core"] = 1 - pos["core"]
    return other


class Copies:
    def __init__(self, send_sems, recv_sems):
        self.send_sems, self.recv_sems, self.started = send_sems, recv_sems, []

    def start(self, src, dst, device):
        slot = len(self.started)
        copy = pltpu.make_async_remote_copy(
            src_ref=src,
            dst_ref=dst,
            send_sem=self.send_sems.at[slot],
            recv_sem=self.recv_sems.at[slot],
            device_id=device,
            device_id_type=MESH,
        )
        copy.start()
        self.started.append(copy)
        return copy

    def finish(self):
        for copy in self.started:
            copy.wait_send()


OFFSETS = (0, 1, -1, 2)
FACING = (0, 2, 1, 3)
NEXT, BEFORE, FAR = 1, 2, 3
WHOLE, OTHERS = (0, RING), (1, RING - 1)


def view_index(axes, chosen, split_axis, half, columns):
    index = []
    for axis in axes:
        at = chosen[axis]
        if isinstance(at, tuple):
            start, size = at
            if axis == split_axis and half is not None:
                start, size = start + half * (size // 2), size // 2
            index.append(pl.ds(start, size))
        else:
            index.append(at)
    index.append(slice(None))
    if split_axis is None and half is not None:
        low = (columns // LANES + 1) // 2 * LANES
        index.append(pl.ds(0, low) if half == 0 else pl.ds(low, columns - low))
    else:
        index.append(slice(None))
    return tuple(index)


def over_blocks(axes, chosen, split_axis, half, body):
    spans = []
    for axis in axes:
        at = chosen[axis]
        start, size = at if isinstance(at, tuple) else (at, 1)
        if axis == split_axis and half is not None:
            start, size = start + half * (size // 2), size // 2
        spans.append((axis, start, size))
    steps = 1
    for _, _, size in spans:
        steps *= size

    def one(step, carry):
        places, rest = {}, step
        for axis, start, size in reversed(spans):
            if size == 1:
                places[axis] = start
            else:
                places[axis] = start + lax.rem(rest, size)
                rest = lax.div(rest, size)
        body(places)
        return carry

    if steps == 1:
        one(0, 0)
    else:
        lax.fori_loop(0, steps, one, 0)


class Ring:
    def __init__(self, copies, pos, ref, axes, axis, chosen, split_axis):
        self.copies, self.ref, self.axes, self.axis = copies, ref, axes, axis
        self.chosen, self.split_axis = chosen, split_axis
        self.columns = ref.shape[-1]
        self.plus, self.minus = device_at(moved(pos, axis, 1)), device_at(moved(pos, axis, -1))
        self.across = device_at(moved(pos, axis, 2))

    def block(self, place, half):
        chosen = dict(self.chosen)
        chosen[self.axis] = place
        return self.ref.at[view_index(self.axes, chosen, self.split_axis, half, self.columns)]


class Gather(Ring):
    def begin(self):
        start, block = self.copies.start, self.block
        self.first = [
            start(block(0, 0), block(BEFORE, 0), self.plus),
            start(block(0, 1), block(NEXT, 1), self.minus),
            start(block(0, 1), block(BEFORE, 1), self.plus),
            start(block(0, 0), block(NEXT, 0), self.minus),
        ]

    def relay(self):
        start, block = self.copies.start, self.block
        self.first[0].wait_recv()
        self.far = [start(block(BEFORE, 0), block(FAR, 0), self.plus)]
        self.first[1].wait_recv()
        self.far.append(start(block(NEXT, 1), block(FAR, 1), self.minus))

    def send_direct(self):
        start, block = self.copies.start, self.block
        self.direct = [
            start(block(0, None), block(FAR, None), self.across),
            start(block(0, None), block(BEFORE, None), self.plus),
            start(block(0, None), block(NEXT, None), self.minus),
        ]

    def wait_direct(self):
        for copy in self.direct:
            copy.wait_recv()

    def wait_near(self):
        self.first[2].wait_recv()
        self.first[3].wait_recv()

    def wait_far(self):
        self.far[0].wait_recv()
        self.far[1].wait_recv()


class Scatter(Ring):
    def land(self, landing):
        self.later = tuple(a for a in self.axes if isinstance(self.chosen.get(a), tuple))
        self.landing_axes, self.landing = landing
        self.relayed, self.from_before, self.from_next = self.landing
        return self

    def landed(self, ref, half):
        return ref.at[
            view_index(self.landing_axes, self.chosen, self.split_axis, half, self.columns)
        ]

    def send_far(self):
        start = self.copies.start
        self.far = [
            start(self.block(FAR, 0), self.landed(self.relayed, 0), self.plus),
            start(self.block(FAR, 1), self.landed(self.relayed, 1), self.minus),
        ]

    def send_near(self):
        start = self.copies.start
        self.near = [
            start(self.block(NEXT, 1), self.landed(self.from_before, 1), self.plus),
            start(self.block(BEFORE, 0), self.landed(self.from_next, 0), self.minus),
        ]

    def add_into(self, place, half, refs):
        tail = view_index((), {}, self.split_axis, half, self.columns)

        def slab(places):
            both = dict(self.chosen)
            both.update(places)
            both[self.axis] = place
            block = tuple(both[axis] for axis in self.axes) + tail
            land = tuple(both[axis] for axis in self.landing_axes) + tail
            total = self.ref[block].astype(F32)
            for ref in refs:
                total += ref[land].astype(F32)
            self.ref[block] = total.astype(BF16)

        over_blocks(self.later, self.chosen, self.split_axis, half, slab)

    def relay(self):
        start = self.copies.start
        self.far[0].wait_recv()
        self.add_into(NEXT, 0, [self.relayed])
        self.near.append(start(self.block(NEXT, 0), self.landed(self.from_before, 0), self.plus))
        self.far[1].wait_recv()
        self.add_into(BEFORE, 1, [self.relayed])
        self.near.append(start(self.block(BEFORE, 1), self.landed(self.from_next, 1), self.minus))

    def wait_near(self):
        for copy in self.near:
            copy.wait_recv()

    def finish(self):
        self.wait_near()
        self.add_into(0, None, [self.from_before, self.from_next])

    def send_direct(self):
        start = self.copies.start
        self.direct = [
            start(self.block(FAR, None), self.landed(self.relayed, None), self.across),
            start(self.block(NEXT, None), self.landed(self.from_before, None), self.plus),
            start(self.block(BEFORE, None), self.landed(self.from_next, None), self.minus),
        ]

    def finish_direct(self):
        total = self.ref[(0,) * len(self.axes)].astype(F32)
        for copy, ref in zip(self.direct, self.landing):
            copy.wait_recv()
            total += ref[...].astype(F32)
        return total


class Scatters:
    def __init__(self, copies, pos, axes, ref, order, landing):
        first, rest = order[0], order[1:]

        def ring(phase, chosen):
            later = [axis for axis in order[phase + 1 :] if isinstance(chosen[axis], tuple)]
            even = [axis for axis in later if chosen[axis][1] % 2 == 0]
            landing_axes = tuple(axis for axis in axes if axis in order[phase + 1 :])
            one = Scatter(
                copies, pos, ref, axes, order[phase], chosen, even[-1] if even else None
            )
            return one.land((landing_axes, landing[phase]))

        whole = {axis: WHOLE for axis in rest}
        self.portion = ring(0, {**whole, rest[0]: OTHERS})
        self.remainder = ring(0, {**whole, rest[0]: 0})
        self.second = ring(1, {first: 0, **{axis: WHOLE for axis in rest[1:]}})
        self.third = ring(2, {first: 0, rest[0]: 0}) if len(rest) > 1 else None
        self.last = self.third or self.second


def landing_shapes(axis_count, rows, columns):
    shapes = []
    for phase in range(axis_count):
        lead = (RING,) * (axis_count - 1 - phase)
        shapes += [pltpu.VMEM(lead + (rows, columns), BF16)] * 3
    return shapes


def by_phase(refs):
    return [refs[3 * k : 3 * k + 3] for k in range(len(refs) // 3)]


def nt_dot(left, right):
    return lax.dot_general(left, right, (((1,), (1,)), ((), ())), preferred_element_type=F32)


def nn_dot(left, right):
    return jnp.dot(left, right, preferred_element_type=F32)


def silu(value):
    return value / (1.0 + jnp.exp(-value))


def visible_from(parents):
    count = parents.shape[-1]
    above = lax.broadcasted_iota(jnp.int32, (count, count), 0)
    below = lax.broadcasted_iota(jnp.int32, (count, count), 1)
    reach = ((above == parents) | (above == below)).astype(F32)
    hops = 1
    while hops < count - 1:
        reach = (nn_dot(reach.astype(BF16), reach.astype(BF16)) > 0.5).astype(F32)
        hops *= 2
    return reach.astype(BF16)


def routing_lanes(experts, weights, expert_count):
    rows, top = experts.shape
    lane = lax.rem(lax.broadcasted_iota(jnp.int32, (rows, LANES), 1), expert_count)
    total = jnp.zeros((rows, LANES), F32)
    for k in range(top):
        total += jnp.where(lane == experts[:, k : k + 1], weights[:, k : k + 1], 0.0)
    return total


def in_three(values, expert_count):
    high = values.astype(BF16).astype(F32)
    middle = (values - high).astype(BF16).astype(F32)
    low = values - high - middle
    lane = lax.broadcasted_iota(jnp.int32, values.shape, 1)
    terms = jnp.where(
        lane < expert_count,
        high,
        jnp.where(lane < 2 * expert_count, middle, jnp.where(lane < 3 * expert_count, low, 0.0)),
    )
    return terms.astype(BF16)


def layer_kernel(
    cache_len_ref,
    hidden_ref,
    node_ref,
    parents_hbm,
    experts_hbm,
    weights_hbm,
    gain_hbm,
    queries_hbm,
    cache_hbm,
    value_up_hbm,
    out_proj_hbm,
    gate_hbm,
    up_hbm,
    down_hbm,
    shared_gate_hbm,
    shared_up_hbm,
    shared_down_hbm,
    out_ref,
    parents_ref,
    experts_ref,
    weights_ref,
    gain_ref,
    queries,
    cache,
    value_up,
    proj,
    latent_out,
    latents,
    head_out,
    residual,
    hidden_away,
    squares,
    squares_in,
    attended_rows,
    plane_refs,
    plane_landing,
    row_refs,
    terms_ref,
    inner_weights,
    shared_weights,
    down_weights,
    row_scale,
    sums,
    sums_out,
    sums_in,
    shared_sums,
    shared_in,
    hidden,
    part_refs,
    landing_refs,
    final,
    final_in,
    send_sems,
    recv_sems,
    local_sems,
):
    pos = my_position()
    core, group, inner = pos["core"], lax.axis_index("group"), lax.axis_index("ingroup")
    sibling = device_at(sibling_of(pos))
    rows, model_width = hidden_ref.shape
    half = model_width // CORES
    chip_rows = CORES * rows
    plane_rows = RING * RING * chip_rows
    inner_count, _, latent_width = latents.shape
    head_count, _, value_width = value_up.shape
    all_heads, cached = queries.shape[1], cache.shape[1]
    unit_count = gate_hbm.shape[2]
    shared_count = shared_gate_hbm.shape[0]
    expert_count = RING * CORES * RING
    depth = CORES * unit_count + shared_count
    mine = pl.ds(pl.multiple_of(core * half, LANES), half)
    other = pl.ds(pl.multiple_of((1 - core) * half, LANES), half)
    own_units = pl.ds(pl.multiple_of(core * unit_count, unit_count), unit_count)
    shared_units = pl.ds(CORES * unit_count, shared_count)
    gates, ups = pl.ds(0, unit_count), pl.ds(unit_count, unit_count)

    loads = []

    def load(src, dst):
        copy = pltpu.make_async_copy(src, dst, local_sems.at[len(loads)])
        copy.start()
        loads.append(copy)
        return copy

    small_loads = [
        load(parents_hbm, parents_ref),
        load(experts_hbm, experts_ref),
        load(weights_hbm, weights_ref),
        load(gain_hbm.at[:, mine], gain_ref),
    ]
    first_loads = [load(queries_hbm, queries), load(cache_hbm.at[0], cache)]
    head_loads = [load(value_up_hbm, value_up), load(out_proj_hbm.at[:, mine], proj)]

    peers = [lax.rem(inner + step, inner_count) for step in range(1, inner_count)]
    z_neighbours = [device_at(moved(pos, "z", by)) for by in (1, -1, 2)]
    partners = [(group, peer) for peer in peers] + z_neighbours + [sibling]
    barrier = pltpu.get_barrier_semaphore()
    for partner in partners:
        pl.semaphore_signal(barrier, inc=1, device_id=partner, device_id_type=MESH)

    for copy in small_loads:
        copy.wait()
    routing = routing_lanes(experts_ref[...], weights_ref[...], expert_count)
    hidden_away[:, :half] = hidden_ref[:, other].astype(F32)
    hidden_away[:, half:] = routing
    residual[core, :, :half] = hidden_ref[:, mine].astype(F32)
    residual[core, :, half:] = routing

    reach = visible_from(parents_ref[...])
    node_keys = node_ref[...]
    chunk_heads = all_heads // 2
    chunk_rows = chunk_heads * rows
    chunk_peers = inner_count // 2
    row = lax.broadcasted_iota(jnp.int32, (chunk_rows, rows), 0)
    lane = lax.broadcasted_iota(jnp.int32, (chunk_rows, rows), 1)
    node_of = (lax.div(row, chunk_heads) == lane).astype(F32).astype(BF16)
    seen = nt_dot(node_of, reach) > 0.5
    to_row = lax.broadcasted_iota(jnp.int32, (chunk_rows, chunk_rows), 0)
    from_row = lax.broadcasted_iota(jnp.int32, (chunk_rows, chunk_rows), 1)
    head_major = (
        (from_row == lax.rem(to_row, rows) * chunk_heads + lax.div(to_row, rows))
        .astype(F32)
        .astype(BF16)
    )
    for copy in first_loads:
        copy.wait()

    for chunk in range(2):
        query = queries[:, chunk * chunk_heads : (chunk + 1) * chunk_heads, :]
        query = query.reshape(chunk_rows, query.shape[-1])
        scores = nn_dot(query, cache[...]) * SCALE_QK
        live = lax.broadcasted_iota(jnp.int32, scores.shape, 1) < cache_len_ref[0]
        scores = jnp.where(live, scores, -jnp.inf)
        node_scores = jnp.where(seen, nt_dot(query, node_keys) * SCALE_QK, -jnp.inf)
        highest = jnp.maximum(
            jnp.max(scores, axis=1, keepdims=True), jnp.max(node_scores, axis=1, keepdims=True)
        )
        scores = jnp.exp(scores - highest)
        node_scores = jnp.exp(node_scores - highest)
        total = jnp.sum(scores, axis=1, keepdims=True) + jnp.sum(
            node_scores, axis=1, keepdims=True
        )
        share = 1.0 / total
        latent = nt_dot((scores * share).astype(BF16), cache[:latent_width, :])
        latent += nn_dot((node_scores * share).astype(BF16), node_keys[:, :latent_width])
        latent = nn_dot(head_major, latent.astype(BF16)).astype(BF16)
        latent_out[chunk * chunk_peers : (chunk + 1) * chunk_peers] = latent.reshape(
            chunk_peers, head_count * rows, latent_width
        )
    pl.semaphore_wait(barrier, len(partners))
    copies = Copies(send_sems, recv_sems)
    arrivals = []
    for place_x, place_y in sorted(
        ((i, j) for i in range(RING) for j in range(RING) if i or j), reverse=True
    ):
        peer = moved(moved(pos, "x", OFFSETS[place_x]), "y", OFFSETS[place_y])
        src = latent_out.at[peer["x"] * RING + peer["y"]]
        dst = latents.at[FACING[place_x] * RING + FACING[place_y]]
        arrivals.append(copies.start(src, dst, device_at(peer)))
    hidden_copy = copies.start(hidden_away, residual.at[core], sibling)
    late_loads = [
        load(gate_hbm.at[0, mine, :], inner_weights.at[core, :, gates]),
        load(up_hbm.at[0, mine, :], inner_weights.at[core, :, ups]),
        load(shared_gate_hbm.at[:, mine], shared_weights.at[0]),
        load(shared_up_hbm.at[:, mine], shared_weights.at[1]),
        load(down_hbm.at[0, :, mine], down_weights.at[own_units, :]),
        load(shared_down_hbm.at[:, mine], down_weights.at[shared_units, :]),
    ]

    def prepare(places):
        at = tuple(places[axis] for axis in AXES)
        for which in range(CORES):
            sums[(which,) + at] = jnp.zeros((chip_rows, 2 * unit_count), F32)
        hidden[at + (slice(None), slice(CORES * unit_count, depth))] = jnp.zeros(
            (chip_rows, shared_count), BF16
        )

    over_blocks(AXES, {axis: WHOLE for axis in AXES}, None, None, prepare)
    latents[0] = latent_out[inner]
    for copy in arrivals:
        copy.wait_recv()

    for copy in head_loads:
        copy.wait()
    stacked = latents[...].reshape(inner_count * head_count * rows, latent_width)
    for head in range(head_count):
        product = nn_dot(stacked, value_up[head])
        product = product.reshape(inner_count, head_count, rows, value_width)[:, head]
        head_out[:, core, :, head * value_width : (head + 1) * value_width] = product.astype(
            BF16
        ).astype(F32)
    heads_copy = copies.start(head_out.at[:, core], head_out.at[:, core], sibling)
    heads_copy.wait_recv()
    weight_copies = [
        copies.start(gate_hbm.at[0, other, :], inner_weights.at[core, :, gates], sibling),
        copies.start(up_hbm.at[0, other, :], inner_weights.at[core, :, ups], sibling),
        copies.start(down_hbm.at[0, :, other], down_weights.at[own_units, :], sibling),
    ]
    heads = head_out[...].reshape(plane_rows, head_count * value_width).astype(BF16)

    plane_parts = column_parts(half, len(PLANE_ORDERS))
    scatters = []
    for (start, columns), ref, landing, order in zip(
        plane_parts, plane_refs, plane_landing, PLANE_ORDERS
    ):
        partial = nn_dot(heads, proj[:, start : start + columns])
        ref[...] = partial.astype(BF16).reshape(ref.shape)
        scatter = Scatters(copies, pos, ("x", "y"), ref, order, by_phase(landing))
        scatter.portion.send_far()
        scatter.portion.send_near()
        scatters.append(scatter)
    for scatter in scatters:
        scatter.portion.relay()
        scatter.remainder.send_far()
        scatter.remainder.send_near()
    for scatter in scatters:
        scatter.portion.finish()
        scatter.second.send_direct()
    for scatter in scatters:
        scatter.remainder.relay()
    for scatter in scatters:
        scatter.remainder.finish()
    hidden_copy.wait_recv()
    square_sum = jnp.zeros((chip_rows, 1), F32)
    for (start, columns), scatter in zip(plane_parts, scatters):
        total = scatter.last.finish_direct()
        total += residual[:, :, start : start + columns].reshape(chip_rows, columns)
        attended = total.astype(BF16)
        attended_rows[:, start : start + columns] = attended
        wide = attended.astype(F32)
        square_sum += jnp.sum(wide * wide, axis=1, keepdims=True)
    squares[...] = jnp.broadcast_to(square_sum, squares.shape)
    squares_copy = copies.start(squares, squares_in, sibling)
    parts = column_parts(half, len(GATHER_ORDERS))
    for (start, columns), ref in zip(parts, row_refs):
        span = slice(start, start + columns)
        scaled = attended_rows[:, span].astype(F32) * gain_ref[:, span]
        ref[0, 0, 0] = scaled.astype(BF16)

    def gather_ring(ref, order, phase, ranges):
        chosen = {axis: 0 for axis in AXES}
        chosen.update(zip(order, ranges))
        return Gather(copies, pos, ref, AXES, order[phase], chosen, order[0] if phase else None)

    rings = [
        (
            gather_ring(ref, order, 0, ()),
            gather_ring(ref, order, 1, (WHOLE,)),
            gather_ring(ref, order, 2, (WHOLE, 0)),
            gather_ring(ref, order, 2, (WHOLE, OTHERS)),
        )
        for ref, order in zip(row_refs, GATHER_ORDERS)
    ]
    terms_rings = [
        gather_ring(terms_ref, TERMS_ORDER, phase, (WHOLE,) * phase) for phase in range(3)
    ]

    def multiply(which_part, places):
        start, columns = parts[which_part]
        ref = row_refs[which_part]
        chosen = {axis: WHOLE for axis in AXES}
        chosen[GATHER_ORDERS[which_part][-1]] = places
        index = view_index(AXES, chosen, None, None, columns)
        spans = tuple(chosen[axis][1] for axis in AXES)
        count = places[1] * plane_rows

        def one(which, carry):
            block = ref[index[:-1] + (slice(0, columns),)].reshape(count, columns)
            product = nn_dot(block, inner_weights[which, start : start + columns, :])
            at = (which,) + index
            sums[at] = sums[at] + product.reshape(spans + (chip_rows, 2 * unit_count))
            return carry

        lax.fori_loop(0, CORES, one, 0)

    for ring in rings:
        ring[0].send_direct()
    squares_copy.wait_recv()
    mean_square = (square_sum + squares_in[:, :1]) / model_width
    scale = lax.rsqrt(mean_square + NORM_EPS)
    routing_terms = in_three(residual[:, :, half:].reshape(chip_rows, LANES), expert_count)
    lane = lax.broadcasted_iota(jnp.int32, (chip_rows, LANES), 1)
    scale_high = scale.astype(BF16).astype(F32)
    scale_middle = (scale - scale_high).astype(BF16).astype(F32)
    scale_terms = jnp.where(
        lane == SCALE_LANE,
        scale_high,
        jnp.where(lane == SCALE_LANE + 1, scale_middle, scale - scale_high - scale_middle),
    )
    is_scale = (lane >= SCALE_LANE) & (lane < SCALE_LANE + 3)
    terms_ref[0, 0, 0] = jnp.where(is_scale, scale_terms, routing_terms.astype(F32)).astype(BF16)
    terms_rings[0].send_direct()

    for ring in rings:
        ring[0].wait_direct()
        ring[1].begin()
    for ring in rings:
        ring[1].relay()
    for ring in rings:
        ring[2].begin()
    terms_rings[0].wait_direct()
    terms_rings[1].send_direct()
    for copy in late_loads:
        copy.wait()
    for ring in rings:
        ring[1].wait_near()
        ring[1].wait_far()
        ring[3].begin()
    for ring in rings:
        ring[2].relay()
    terms_rings[1].wait_direct()
    terms_rings[2].send_direct()
    for copy in weight_copies:
        copy.wait_recv()
    for k in range(len(rings)):
        multiply(k, (0, 1))
    for ring in rings:
        ring[3].relay()
    for k, ring in reversed(list(enumerate(rings))):
        ring[2].wait_near()
        ring[3].wait_near()
        multiply(k, (NEXT, 2))

    def narrow(ranges):
        chosen = dict(zip(AXES, ranges))

        def one(places):
            at = tuple(places[axis] for axis in AXES)
            for which in range(CORES):
                sums_out[(which,) + at] = sums[(which,) + at].astype(BF16)

        over_blocks(AXES, chosen, None, None, one)
        index = (slice(None),) + view_index(AXES, chosen, None, None, unit_count)
        return copies.start(sums_out.at[index], sums_in.at[index], sibling)

    near, far = (0, FAR), (FAR, 1)
    regions = [((z, 1), near, near) for z in range(FAR)]
    regions += [(far, WHOLE, WHOLE), (near, far, WHOLE), (near, near, far)]
    exchanges = [narrow(region) for region in regions[:FAR]]
    for k, ring in reversed(list(enumerate(rings))):
        ring[2].wait_far()
        ring[3].wait_far()
        multiply(k, far)
    exchanges += [narrow(region) for region in regions[FAR:]]
    for which in range(2):
        total = jnp.zeros((plane_rows, shared_count), F32)
        for (start, columns), ref in zip(parts, row_refs):
            total += nt_dot(
                ref[0, :, :, :, :columns].reshape(plane_rows, columns),
                shared_weights[which, :, start : start + columns],
            )
        shared_sums[which] = total
    shared_copy = copies.start(shared_sums, shared_in, sibling)
    terms_rings[2].wait_direct()
    picks_shape = (LANES, (CORES + 1) * LANES)
    picks_from = lax.broadcasted_iota(jnp.int32, picks_shape, 0)
    picks_to = lax.div(lax.broadcasted_iota(jnp.int32, picks_shape, 1), LANES)
    chosen_expert = (pos["z"] * CORES + picks_to) * RING + pos["x"]
    is_weight = (picks_from < SCALE_LANE) & (picks_to < CORES)
    picked = (is_weight & (lax.rem(picks_from, expert_count) == chosen_expert)) | (
        (picks_from >= SCALE_LANE) & (picks_to == CORES)
    )
    picks = picked.astype(F32).astype(BF16)
    for z in range(RING):
        terms = terms_ref[z].reshape(plane_rows, LANES)
        row_scale[z] = nn_dot(terms, picks).reshape(RING, RING, chip_rows, (CORES + 1) * LANES)
    for region, exchange in zip(regions, exchanges):
        exchange.wait_recv()

        def activate(places):
            at = tuple(places[axis] for axis in AXES)
            for which in range(CORES):
                both = sums[(which,) + at] + sums_in[(which,) + at].astype(F32)
                norm = row_scale[at + (slice(None), slice(CORES * LANES, (CORES + 1) * LANES))]
                both = both * jnp.concatenate([norm] * (2 * unit_count // LANES), axis=1)
                gate, up = both[:, :unit_count], both[:, unit_count:]
                lanes = slice(which * LANES, (which + 1) * LANES)
                scale = row_scale[at + (slice(None), lanes)]
                scale = jnp.concatenate([scale] * (unit_count // LANES), axis=1)
                value = (silu(gate) * up * scale).astype(BF16)
                units = slice(which * unit_count, (which + 1) * unit_count)
                hidden[at + (slice(None), units)] = value

        over_blocks(AXES, dict(zip(AXES, region)), None, None, activate)
    shared_copy.wait_recv()
    norm_lanes = slice(CORES * LANES, CORES * LANES + shared_count)
    norm = row_scale[0, :, :, :, norm_lanes].reshape(plane_rows, shared_count)
    shared_gate_part, shared_up_part = (
        (shared_sums[k] + shared_in[k]) * norm for k in (0, 1)
    )
    shared_hidden = (silu(shared_gate_part) * shared_up_part).astype(BF16)
    hidden[0, :, :, :, CORES * unit_count :] = shared_hidden.reshape(
        RING, RING, chip_rows, shared_count
    )

    scatters = [
        Scatters(copies, pos, AXES, ref, order, by_phase(landing))
        for ref, order, landing in zip(part_refs, SCATTER_ORDERS, landing_refs)
    ]

    def project(which_part, places):
        start, columns = parts[which_part]
        chosen = {axis: WHOLE for axis in AXES}
        chosen[SCATTER_ORDERS[which_part][0]] = places
        index = view_index(AXES, chosen, None, None, columns)
        spans = tuple(chosen[axis][1] for axis in AXES)
        product = nn_dot(
            hidden[index].reshape(places[1] * plane_rows, depth),
            down_weights[:, start : start + columns],
        )
        part_refs[which_part][index] = product.astype(BF16).reshape(
            spans + (chip_rows, columns)
        )

    for k, scatter in enumerate(scatters):
        project(k, far)
        scatter.portion.send_far()
    for k, scatter in enumerate(scatters):
        project(k, (NEXT, 1))
        project(k, (BEFORE, 1))
        scatter.portion.send_near()
    for k in range(len(scatters)):
        project(k, (0, 1))
    late_last = scatters[::-1]
    for scatter in late_last:
        scatter.portion.relay()
    for scatter in late_last:
        scatter.remainder.send_far()
        scatter.remainder.send_near()
    for scatter in late_last:
        scatter.portion.finish()
        scatter.second.send_far()
        scatter.second.send_near()
    for scatter in late_last:
        scatter.remainder.relay()
    for scatter in late_last:
        scatter.second.relay()
    for scatter in late_last:
        scatter.remainder.finish()
        scatter.second.finish()
        scatter.third.send_direct()
    final_copies = []
    for (start, columns), scatter in list(zip(parts, scatters))[::-1]:
        total = scatter.last.finish_direct() + attended_rows[:, start : start + columns].astype(F32)
        span = pl.ds(start, columns)
        final[:, :, span] = total.reshape(CORES, rows, columns)
        final_copies.append(
            copies.start(final.at[1 - core, :, span], final_in.at[:, span], sibling)
        )
    out_ref[:, mine] = final[core].astype(BF16)
    for copy in final_copies:
        copy.wait_recv()
    out_ref[:, other] = final_in[...].astype(BF16)
    copies.finish()


def local(
    hidden_in,
    queries,
    node_latent,
    cache,
    cache_len,
    parents,
    value_up,
    out_proj,
    ffn_gain,
    route_experts,
    route_weights,
    expert_gate,
    expert_up,
    expert_down,
    shared_gate,
    shared_up,
    shared_down,
):
    rows, model_width = hidden_in.shape
    half = model_width // CORES
    chip_rows = CORES * rows
    inner_count = lax.axis_size("ingroup")
    head_count, latent_width, value_width = value_up.shape
    proj_rows = out_proj.shape[0]
    unit_count = expert_gate.shape[2]
    shared_count = shared_gate.shape[1]
    plane_rows = RING * RING * chip_rows
    depth = CORES * unit_count + shared_count
    plane_parts = column_parts(half, len(PLANE_ORDERS))
    parts = column_parts(half, len(GATHER_ORDERS))
    grid3 = (RING, RING, RING)
    vmem = pl.BlockSpec(memory_space=pltpu.VMEM)
    smem = pl.BlockSpec(memory_space=pltpu.SMEM)
    hbm = pl.BlockSpec(memory_space=pl.ANY)
    copy_count = inner_count - 1 + 11 + 6 * (2 * 3 + 3 * 4 * 2) + 6 + 3 + 5
    load_count = 14
    return pl.pallas_call(
        layer_kernel,
        out_shape=jax.ShapeDtypeStruct((rows, model_width), BF16),
        in_specs=[smem] + [vmem] * 2 + [hbm] * 14,
        out_specs=vmem,
        scratch_shapes=[
            pltpu.VMEM(parents.shape, jnp.int32),
            pltpu.VMEM(route_experts.shape, jnp.int32),
            pltpu.VMEM(route_weights.shape, F32),
            pltpu.VMEM((1, half), F32),
            pltpu.VMEM(queries.shape, BF16),
            pltpu.VMEM((cache.shape[2], cache.shape[1]), BF16),
            pltpu.VMEM(value_up.shape, BF16),
            pltpu.VMEM((proj_rows, half), BF16),
            pltpu.VMEM((inner_count, head_count * rows, latent_width), BF16),
            pltpu.VMEM((inner_count, head_count * rows, latent_width), BF16),
            pltpu.VMEM((inner_count, CORES, rows, proj_rows), F32),
            pltpu.VMEM((CORES, rows, half + LANES), F32),
            pltpu.VMEM((rows, half + LANES), F32),
            pltpu.VMEM((chip_rows, LANES), F32),
            pltpu.VMEM((chip_rows, LANES), F32),
            pltpu.VMEM((chip_rows, half), BF16),
            [pltpu.VMEM((RING, RING, chip_rows, columns), BF16) for _, columns in plane_parts],
            [landing_shapes(2, chip_rows, columns) for _, columns in plane_parts],
            [pltpu.VMEM(grid3 + (chip_rows, columns), BF16) for _, columns in parts],
            pltpu.VMEM(grid3 + (chip_rows, LANES), BF16),
            pltpu.VMEM((CORES, half, 2 * unit_count), BF16),
            pltpu.VMEM((2, shared_count, half), BF16),
            pltpu.VMEM((depth, half), BF16),
            pltpu.VMEM(grid3 + (chip_rows, (CORES + 1) * LANES), F32),
            pltpu.VMEM((CORES,) + grid3 + (chip_rows, 2 * unit_count), F32),
            pltpu.VMEM((CORES,) + grid3 + (chip_rows, 2 * unit_count), BF16),
            pltpu.VMEM((CORES,) + grid3 + (chip_rows, 2 * unit_count), BF16),
            pltpu.VMEM((2, plane_rows, shared_count), F32),
            pltpu.VMEM((2, plane_rows, shared_count), F32),
            pltpu.VMEM(grid3 + (chip_rows, depth), BF16),
            [pltpu.VMEM(grid3 + (chip_rows, columns), BF16) for _, columns in parts],
            [landing_shapes(3, chip_rows, columns) for _, columns in parts],
            pltpu.VMEM((CORES, rows, half), F32),
            pltpu.VMEM((rows, half), F32),
            pltpu.SemaphoreType.DMA((copy_count,)),
            pltpu.SemaphoreType.DMA((copy_count,)),
            pltpu.SemaphoreType.DMA((load_count,)),
        ],
        compiler_params=pltpu.CompilerParams(
            collective_id=0, has_side_effects=True, vmem_limit_bytes=VMEM_LIMIT
        ),
        name="layer",
    )(
        cache_len,
        hidden_in,
        node_latent,
        parents,
        route_experts,
        route_weights,
        ffn_gain.reshape(1, -1),
        queries,
        jnp.swapaxes(cache, 1, 2),
        value_up,
        out_proj,
        expert_gate,
        expert_up,
        expert_down,
        jnp.swapaxes(shared_gate, 0, 1),
        jnp.swapaxes(shared_up, 0, 1),
        shared_down,
    )


def solution(mesh):
    both = ("group", "ingroup")
    in_specs = (
        P(both, None),
        P(both, None, None),
        P(both, None),
        P(both, None, None),
        P(both),
        P(both, None),
        P("ingroup", None, None),
        P("ingroup", None),
        P(),
        P(both, None),
        P(both, None),
        P(both, None, None),
        P(both, None, None),
        P(both, None, None),
        P(None, "ingroup"),
        P(None, "ingroup"),
        P("ingroup", None),
    )
    return jax.shard_map(
        local, mesh=mesh, in_specs=in_specs, out_specs=P(both, None), check_vma=False
    )
```
